128 devices in a mesh: rep: 2 (over core), exp: 32 (over z, x_lo, y), mdl: 2 (over x_hi).
Axes of the slice: x: 4 (x_hi: 2, x_lo: 2; x = x_hi * 2 + x_lo), y: 4, z: 4, core: 2. Of those that a mesh axis runs over, the one named last changes fastest.
Arguments:
- tokens_in: bfloat16 [12608, 768], P(('rep', 'exp')), may hold values from -6 to 6
- expert_ids: int32 [2, 12608, 2], P(None, ('rep', 'exp')), may hold values from 0 to 31, all different within a row; in each aligned block of 197 rows (0 to 196, 197 to 393, ..., all dimensions but the last counted through in order) at most 16 rows name the same one
- w_qkv: bfloat16 [2, 768, 3, 768], P(None, ('rep', 'exp'), None, 'mdl'), may hold values from -0.21875 to 0.21875
- w_out: bfloat16 [2, 768, 768], P(None, 'mdl', ('rep', 'exp')), may hold values from -1.75 to 1.75
- router: bfloat16 [2, 768, 32], P(None, ('rep', 'exp')), may hold values from -0.15625 to 0.15625
- gains: bfloat16 [2, 2, 768], P(None, None, ('rep', 'exp')), may hold values from 0.5 to 1.5
- shifts: bfloat16 [2, 3, 768], P(None, None, ('rep', 'exp')), may hold values from -1.1953125 to 1.1953125
- w_in: bfloat16 [2, 32, 768, 3072], P(None, 'exp', 'rep', 'mdl'), may hold values from -0.21875 to 0.21875
- b_in: bfloat16 [2, 32, 3072], P(None, 'exp', 'mdl'), may hold values from -1.796875 to 1.796875
- w_exp_out: bfloat16 [2, 32, 3072, 768], P(None, 'exp', 'mdl', 'rep'), may hold values from -0.109375 to 0.109375
- b_out: bfloat16 [2, 32, 768], P(None, 'exp', 'rep'), may hold values from -1.796875 to 1.796875
- cotangent: bfloat16 [12608, 768], P(('rep', 'exp')), may hold values from -6 to 6
Outputs:
- mixed: bfloat16 [12608, 768], P(('rep', 'exp'))
- grad_tokens: float32 [12608, 768], P(('rep', 'exp'))
- grad_w_qkv: float32 [2, 768, 3, 768], P(None, ('rep', 'exp'), None, 'mdl')
- grad_w_out: float32 [2, 768, 768], P(None, 'mdl', ('rep', 'exp'))
- grad_router: float32 [2, 768, 32], P(None, ('rep', 'exp'))
- grad_gains: float32 [2, 2, 768], P(None, None, ('rep', 'exp'))
- grad_shifts: float32 [2, 3, 768], P(None, None, ('rep', 'exp'))
- grad_w_in: float32 [2, 32, 768, 3072], P(None, 'exp', 'rep', 'mdl')
- grad_b_in: float32 [2, 32, 3072], P(None, 'exp', 'mdl')
- grad_w_exp_out: float32 [2, 32, 3072, 768], P(None, 'exp', 'mdl', 'rep')
- grad_b_out: float32 [2, 32, 768], P(None, 'exp', 'rep')
The draws below stay inside these ranges and needn't reach their ends.
Inputs may be any that keep to these rules, and one draw needn't show every extreme that they name: `expert_ids`: in each block, among the 197 tokens of one aligned block of tokens, no expert is chosen more than 16 times, a bound that some block reaches; a token's two experts differ.
All inputs are finite; a program needn't handle non-finite values.
Results may differ from the reference program's by a relative error of at most 0.025.
Values may be sent and summed in bfloat16 or wider, within the bound.
A program may use at most 192 MiB of HBM per device.

```python
import math
import jax
import jax.numpy as jnp
import numpy as np
from jax import lax

D = 768
HEADS = 12
HD = 64
FF = 3072
SEQ = 197
LAYERS = 2
EXPERTS = 32
TOK_DEV = 197
TOKENS = 12608
CAP = 16


def level_of(rng, dims, cuts, low, high):
    level, own = 1.0, jax.random.fold_in(rng, 6)
    for position, shards_of in cuts:
        draws = jnp.exp(jax.random.uniform(jax.random.fold_in(own, position), (shards_of,), jnp.float32, low / len(cuts), high / len(cuts)))
        level = level * jnp.repeat(draws, dims[position] // shards_of).reshape([-1 if axis == position else 1 for axis in range(len(dims))])
    return level


def deal_out(rng, own, number, rows, amount, top, most, lean):
    sequence = jax.random.permutation(rng, amount)
    heavy_load, common = shares(amount, rows * top, most, lean, True), shares(amount, rows * top, most, lean, False)
    places = jnp.arange(amount)

    def named(tallies, turn):
        used = int((tallies > 0).sum())
        fixed = max(1, used // 4)
        passed = fixed + (places - fixed + turn * (used - fixed)) % max(1, amount - fixed)
        return jnp.zeros((amount,), jnp.int32).at[sequence[jnp.where(places < fixed, places, passed)]].set(jnp.asarray(tallies, jnp.int32))

    tallies = jnp.where(number % 4 == 0, named(heavy_load, number // 4), named(common, number - number // 4 - 1))
    mixed = jax.random.permutation(jax.random.fold_in(own, 3), amount)
    source_of, sink = mixed[0:amount // 2 * 2:2], mixed[1:amount // 2 * 2:2]
    slack = jnp.minimum(tallies[source_of] - 1, most - tallies[sink]) // 2
    slack = jnp.where((source_of == sequence[0]) | (sink == sequence[0]) | (tallies[sink] == 0), 0, jnp.maximum(slack, 0))
    passed = jax.random.randint(jax.random.fold_in(own, 4), (amount // 2,), 0, 1 << 20) % (slack + 1)
    tallies = tallies.at[source_of].add(-passed).at[sink].add(passed)
    labels = jnp.searchsorted(jnp.cumsum(tallies), jnp.arange(rows * top), side="right").astype(jnp.int32)
    listing = labels.reshape(top, rows).T
    listing = listing[jax.random.permutation(jax.random.fold_in(own, 1), rows)]
    turn = jax.random.randint(jax.random.fold_in(own, 2), (rows, 1), 0, top)
    return jnp.take_along_axis(listing, (jnp.arange(top)[None, :] + turn) % top, axis=1)


def shares(count, total, limit, skew, full):
    portions = [(1 << 20) // math.isqrt(grade ** skew) + 1 for grade in range(1, count + 1)]
    largest = limit if full else min(limit, max(-(-total // count), total * portions[0] // sum(portions)))
    least = 1 if total - largest >= count - 1 else 0
    counts, surplus = [largest] + [least] * (count - 1), total - largest - least * (count - 1)
    while surplus > 0:
        free = [i for i in range(1, count) if counts[i] < largest] or [i for i in range(1, count) if counts[i] < limit]
        whole, left = sum([portions[i] for i in free]), surplus
        for i in free:
            extra = min(limit - counts[i], max(1, left * portions[i] // whole), surplus)
            counts[i] = counts[i] + extra
            surplus = surplus - extra
    return np.array(counts)


def normal_values(rng, shape, spread, bound, split=(), held_as=jnp.bfloat16):
    loudness = level_of(rng, shape, split, -0.22, 0.18) if split else 1.0
    drawn = jax.random.normal(rng, shape, jnp.float32) * spread * loudness
    return jnp.minimum(jnp.maximum(drawn, -bound), bound).astype(held_as)


def setup_inputs(seed: int = 0) -> dict:
    seeds = jax.random.split(jax.random.key(seed), 13)
    tokens_in = normal_values(seeds[0], (TOKENS, D), 1.0, 6.0, ((0, 64),))
    expert_ids_keys = jax.random.split(jax.random.fold_in(seeds[1], 1), LAYERS * TOKENS // TOK_DEV)
    expert_ids_turns = jax.random.permutation(jax.random.fold_in(seeds[1], 3), LAYERS * TOKENS // TOK_DEV)
    expert_ids = jax.vmap(lambda own, number: deal_out(jax.random.fold_in(seeds[1], 2), own, number, TOK_DEV, EXPERTS, 2, CAP, 1))(expert_ids_keys, expert_ids_turns).reshape((LAYERS, TOKENS, 2))
    w_qkv = normal_values(seeds[2], (LAYERS, D, 3, HEADS * HD), D ** -0.5, 0.21875, ((1, 64), (3, 2)))
    w_out = normal_values(seeds[3], (LAYERS, HEADS * HD, D), (HEADS * HD // 64) ** -0.5, 1.75, ((1, 2), (2, 64)))
    router = normal_values(seeds[4], (LAYERS, D, EXPERTS), (2 * D) ** -0.5, 0.15625, ((1, 64),))
    gains = jnp.clip(1.0 + 0.1 * jax.random.normal(seeds[5], (LAYERS, 2, D), jnp.float32), 0.5, 1.5).astype(jnp.bfloat16)
    shifts = normal_values(seeds[6], (LAYERS, 3, D), 0.2, 1.1953125, ((2, 64),))
    w_in = normal_values(seeds[7], (LAYERS, EXPERTS, D, FF), D ** -0.5, 0.21875, ((1, 32), (2, 2), (3, 2)))
    b_in = normal_values(seeds[8], (LAYERS, EXPERTS, FF), 0.3, 1.796875, ((1, 32), (2, 2)))
    w_exp_out = normal_values(seeds[9], (LAYERS, EXPERTS, FF, D), FF ** -0.5, 0.109375, ((1, 32), (2, 2), (3, 2)))
    b_out = normal_values(seeds[10], (LAYERS, EXPERTS, D), 0.3, 1.796875, ((1, 32), (2, 2)))
    cotangent = normal_values(seeds[11], (TOKENS, D), 1.0, 6.0, ((0, 64),))
    return dict(tokens_in=tokens_in, expert_ids=expert_ids, w_qkv=w_qkv, w_out=w_out, router=router, gains=gains, shifts=shifts, w_in=w_in, b_in=b_in, w_exp_out=w_exp_out, b_out=b_out, cotangent=cotangent)


@jax.custom_vjp
def low(v):
    return lax.optimization_barrier(v.astype(jnp.bfloat16)).astype(jnp.float32)

@jax.custom_vjp
def low_back(v):
    return v

def low_keep(v):
    return (low(v), None)

def low_pass(kept, grad):
    return (grad,)

def back_keep(v):
    return (v, None)

def back_low(kept, grad):
    return (low(grad),)
low.defvjp(low_keep, low_pass)
low_back.defvjp(back_keep, back_low)
EPSILON = 1e-06
HIGHEST = lax.Precision.HIGHEST

def norm_rows(values, gain, shift):
    row_mean = lax.optimization_barrier(jnp.mean(values, axis=-1, keepdims=True))
    centred = values - row_mean
    row_var = lax.optimization_barrier(jnp.mean(centred * centred, axis=-1, keepdims=True))
    return centred * lax.rsqrt(row_var + EPSILON) * gain + shift

def slot_flat(ids_rows):
    onehot = (ids_rows[..., None] == jnp.arange(EXPERTS, dtype=jnp.int32)).astype(jnp.int32)
    earlier = jnp.cumsum(onehot, axis=1).astype(jnp.int32) - onehot
    within = lax.optimization_barrier(jnp.sum(earlier * onehot, axis=-1)).astype(jnp.int32)
    return (ids_rows * CAP + within).astype(jnp.int32)

def expert_block(inputs):
    rows_e, w_in_e, b_in_e, w_out_e, b_out_e = inputs
    inner = low_back(jnp.dot(rows_e, w_in_e, precision=HIGHEST) + b_in_e)
    active = low(jax.nn.gelu(inner, approximate=False))
    produced_rows = jnp.dot(active, w_out_e, precision=HIGHEST) + b_out_e
    return low_back(low(produced_rows))

def one_layer(state, ids, w_qkv, w_out, router, gains, shifts, w_in, b_in, w_exp_out, b_out):
    groups = TOKENS // TOK_DEV
    images = TOKENS // SEQ
    head_width = HEADS * HD
    h_one = low(norm_rows(state, gains[0], shifts[0]))
    qkv_rows = jnp.dot(h_one, w_qkv.reshape(D, 3 * head_width), precision=HIGHEST)
    qkv_rows = low_back(low(qkv_rows)).reshape(images, SEQ, 3, HEADS, HD)
    query_rows = qkv_rows[:, :, 0]
    key_rows = qkv_rows[:, :, 1]
    value_rows = qkv_rows[:, :, 2]
    scores = low_back(jnp.einsum('ishd,ithd->ihst', query_rows, key_rows, precision=HIGHEST) * HD ** (-0.5))
    probs = low(jax.nn.softmax(scores, axis=-1))
    heads_out = jnp.einsum('ihst,ithd->ishd', probs, value_rows, precision=HIGHEST).reshape(TOKENS, head_width)
    heads_out = low_back(low(heads_out))
    attended = low_back(jnp.dot(heads_out, w_out, precision=HIGHEST))
    after_attn = state + attended + shifts[2]
    h_two = low(norm_rows(after_attn, gains[1], shifts[1]))
    logits = low_back(jnp.dot(h_two, router, precision=HIGHEST))
    chosen = jnp.take_along_axis(logits, ids, axis=1)
    gates = jax.nn.softmax(chosen, axis=-1)
    slots = slot_flat(ids.reshape(groups, TOK_DEV * 2))
    group_idx = jnp.arange(groups, dtype=jnp.int32)[:, None]
    token_rows = jnp.broadcast_to(h_two[:, None, :], (TOKENS, 2, D)).reshape(groups, TOK_DEV * 2, D)
    buffer = jnp.zeros((groups, EXPERTS * CAP, D), jnp.float32).at[group_idx, slots].set(token_rows)
    buffer = low_back(buffer)
    expert_rows = buffer.reshape(groups, EXPERTS, CAP, D).transpose(1, 0, 2, 3).reshape(EXPERTS, groups * CAP, D)
    produced = lax.map(jax.checkpoint(expert_block), (expert_rows, w_in, b_in, w_exp_out, b_out))
    back_rows = produced.reshape(EXPERTS, groups, CAP, D).transpose(1, 0, 2, 3).reshape(groups, EXPERTS * CAP, D)
    picked = back_rows[group_idx, slots].reshape(TOKENS, 2, D)
    combined = lax.optimization_barrier(jnp.sum(gates[:, :, None] * picked, axis=1))
    return after_attn + combined

def reference(tokens_in, expert_ids, w_qkv, w_out, router, gains, shifts, w_in, b_in, w_exp_out, b_out, cotangent):

    def forward(state, qkv_all, out_all, router_all, gains_all, shifts_all, in_all, in_bias_all, exp_out_all, out_bias_all):
        for layer_idx in range(LAYERS):
            state = one_layer(state, expert_ids[layer_idx], qkv_all[layer_idx], out_all[layer_idx], router_all[layer_idx], gains_all[layer_idx], shifts_all[layer_idx], in_all[layer_idx], in_bias_all[layer_idx], exp_out_all[layer_idx], out_bias_all[layer_idx])
        return state
    result, pullback = jax.vjp(forward, tokens_in.astype(jnp.float32), w_qkv.astype(jnp.float32), w_out.astype(jnp.float32), router.astype(jnp.float32), gains.astype(jnp.float32), shifts.astype(jnp.float32), w_in.astype(jnp.float32), b_in.astype(jnp.float32), w_exp_out.astype(jnp.float32), b_out.astype(jnp.float32))
    grads = pullback(cotangent.astype(jnp.float32))
    return (result.astype(jnp.bfloat16), grads[0], grads[1], grads[2], grads[3], grads[4], grads[5], grads[6], grads[7], grads[8], grads[9])
```

```python
import jax
import jax.numpy as jnp
from jax import lax
from jax.sharding import PartitionSpec as P

HD = 64
SEQ = 197
EPSILON = 1e-06
F32 = jnp.float32
BF16 = jnp.bfloat16


def norm_rows(values, gain, shift):
    row_mean = jnp.mean(values, axis=-1, keepdims=True)
    centred = values - row_mean
    row_var = jnp.mean(centred * centred, axis=-1, keepdims=True)
    return centred * lax.rsqrt(row_var + EPSILON) * gain + shift


def norm_back(grad, values, gain):
    row_mean = jnp.mean(values, axis=-1, keepdims=True)
    centred = values - row_mean
    row_var = jnp.mean(centred * centred, axis=-1, keepdims=True)
    scale = lax.rsqrt(row_var + EPSILON)
    unit = centred * scale
    scaled = grad * gain
    grad_in = scale * (
        scaled
        - jnp.mean(scaled, axis=-1, keepdims=True)
        - unit * jnp.mean(scaled * unit, axis=-1, keepdims=True)
    )
    return grad_in, jnp.sum(grad * unit, axis=0), jnp.sum(grad, axis=0)


def dot(a, b):
    return jnp.dot(a, b, preferred_element_type=F32)


def dot_tn(a, b):
    return lax.dot_general(a, b, (((0,), (0,)), ((), ())), preferred_element_type=F32)


def dot_nt(a, b):
    return lax.dot_general(a, b, (((1,), (1,)), ((), ())), preferred_element_type=F32)


def swap_experts(buffer):
    return lax.all_to_all(buffer, "exp", split_axis=0, concat_axis=0, tiled=True)


def other_core(values):
    return lax.ppermute(values, "rep", [(0, 1), (1, 0)])


def other_half(values):
    return lax.ppermute(values, "mdl", [(0, 1), (1, 0)])


def mdl_total(partial_rows):
    low = partial_rows.astype(BF16)
    return low.astype(F32) + other_half(low).astype(F32)


def in_order(own, other, axis):
    first = lax.axis_index("rep") == 0
    return jnp.concatenate(
        [jnp.where(first, own, other), jnp.where(first, other, own)], axis=axis
    )


def rep_total(partial, axis):
    first = lax.axis_index("rep") == 0
    low, high = jnp.split(partial, 2, axis=axis)
    other = other_core(jnp.where(first, high, low).astype(BF16))
    return jnp.where(first, low, high) + other.astype(F32)


def attend_forward(h_one, qkv_weight, score_scale):
    head_width = qkv_weight.shape[1] // 3
    qkv_rows = dot(h_one, qkv_weight).astype(BF16).reshape(SEQ, 3, head_width // HD, HD)
    query_rows, key_rows, value_rows = qkv_rows[:, 0], qkv_rows[:, 1], qkv_rows[:, 2]
    scores = (
        jnp.einsum("shd,thd->hst", query_rows, key_rows, preferred_element_type=F32) * score_scale
    )
    top_score = jnp.max(scores, axis=-1, keepdims=True)
    raw_weight = jnp.exp(scores - top_score)
    row_total = jnp.sum(raw_weight, axis=-1, keepdims=True)
    probs_low = (raw_weight / row_total).astype(BF16)
    log_total = top_score + jnp.log(row_total)
    heads_out = jnp.einsum("hst,thd->shd", probs_low, value_rows, preferred_element_type=F32)
    heads_out = heads_out.astype(BF16).reshape(SEQ, head_width)
    return (query_rows, key_rows, value_rows, log_total, heads_out)


def attend_backward(grad_heads, query_rows, key_rows, value_rows, log_total, score_scale):
    grad_heads = grad_heads.reshape(SEQ, query_rows.shape[1], HD)
    scores = (
        jnp.einsum("shd,thd->hst", query_rows, key_rows, preferred_element_type=F32) * score_scale
    )
    probs = jnp.exp(scores - log_total)
    probs_low = probs.astype(BF16)
    grad_probs = jnp.einsum("shd,thd->hst", grad_heads, value_rows, preferred_element_type=F32)
    grad_scores = probs * (grad_probs - jnp.sum(grad_probs * probs, axis=-1, keepdims=True))
    grad_scores = grad_scores.astype(BF16)
    grad_query = (
        jnp.einsum("hst,thd->shd", grad_scores, key_rows, preferred_element_type=F32) * score_scale
    )
    grad_key = (
        jnp.einsum("hst,shd->thd", grad_scores, query_rows, preferred_element_type=F32)
        * score_scale
    )
    grad_value = jnp.einsum("hst,shd->thd", probs_low, grad_heads, preferred_element_type=F32)
    grad_qkv = jnp.stack([grad_query, grad_key, grad_value], axis=1).astype(BF16)
    return grad_qkv.reshape(SEQ, -1)


def on_device(
    tokens_in,
    expert_ids,
    w_qkv,
    w_out,
    router,
    gains,
    shifts,
    w_in,
    b_in,
    w_exp_out,
    b_out,
    cotangent,
):
    tok_rows, width = tokens_in.shape
    exp_count = lax.axis_size("exp")
    experts = w_in.shape[1] * exp_count
    capacity = 2 * tok_rows // experts + 4
    score_scale = HD ** (-0.5)
    layers = w_qkv.shape[0]
    own_rows = w_qkv.shape[1]
    qkv_cols = 3 * w_qkv.shape[3]
    out_cols = w_out.shape[1]
    small_cols = 128
    slot_count = experts * capacity

    packed = jnp.concatenate(
        [
            w_qkv.reshape(layers, own_rows, qkv_cols),
            jnp.swapaxes(w_out, 1, 2),
            router,
            jnp.swapaxes(gains, 1, 2),
            jnp.swapaxes(shifts, 1, 2),
            jnp.zeros((layers, own_rows, small_cols - experts - 5), BF16),
        ],
        axis=2,
    )

    def fetch(layer_idx):
        mine = packed[layer_idx]
        got = swap_experts(jnp.broadcast_to(mine[None], (exp_count,) + mine.shape))
        whole = in_order(got, other_core(got), 0).reshape(width, -1)
        small = whole[:, qkv_cols + out_cols :]
        vectors = small[:, experts : experts + 5].T.astype(F32)
        return (
            whole[:, :qkv_cols],
            whole[:, qkv_cols : qkv_cols + out_cols],
            small[:, :experts],
            vectors,
        )

    def fetch_experts(layer_idx):
        own_in, own_out, own_b = w_in[layer_idx, 0], w_exp_out[layer_idx, 0], b_out[layer_idx]
        return (
            in_order(own_in, other_core(own_in), 0),
            in_order(own_out, other_core(own_out), 1),
            in_order(own_b, other_core(own_b), 1),
        )

    expert_cols = jnp.arange(experts, dtype=jnp.int32)
    slot_cols = jnp.arange(slot_count, dtype=jnp.int32)
    row_idx = jnp.arange(tok_rows, dtype=jnp.int32)
    before = (row_idx[:, None] > row_idx[None, :]).astype(BF16)

    def route(ids):
        hot = [(ids[:, k : k + 1] == expert_cols).astype(BF16) for k in range(2)]
        earlier = dot(before, hot[0] + hot[1])
        picks = []
        for k in range(2):
            within = jnp.sum(earlier * hot[k].astype(F32), axis=1).astype(jnp.int32)
            slots = ids[:, k] * capacity + within
            picks.append((slots[:, None] == slot_cols).astype(BF16))
        return hot, picks

    fetched = [fetch(i) for i in range(layers)]
    expert_w = [fetch_experts(i) for i in range(layers)]
    routed = [route(expert_ids[i]) for i in range(layers)]

    state = tokens_in.astype(F32)
    saved = []
    for layer_idx in range(layers):
        qkv_weight, proj_weight, router_weight, vectors = fetched[layer_idx]
        in_weight, out_weight, out_bias = expert_w[layer_idx]
        hot, picks = routed[layer_idx]
        inner_bias = b_in[layer_idx, 0].astype(F32)
        h_one = norm_rows(state, vectors[0], vectors[2]).astype(BF16)
        query_rows, key_rows, value_rows, log_total, heads_out = attend_forward(
            h_one, qkv_weight, score_scale
        )
        attended = mdl_total(dot_nt(heads_out, proj_weight))
        after_attn = state + attended + vectors[4]
        h_two = norm_rows(after_attn, vectors[1], vectors[3]).astype(BF16)
        send_rows = dot_tn(picks[0] + picks[1], h_two).astype(BF16)
        rows_in = swap_experts(send_rows.reshape(experts, capacity, width)).reshape(-1, width)
        logits = dot(h_two, router_weight)
        chosen = [jnp.sum(logits * hot[k].astype(F32), axis=1) for k in range(2)]
        gates = jax.nn.softmax(jnp.stack(chosen, axis=1), axis=-1)
        inner = dot(rows_in, in_weight) + inner_bias
        cdf = 0.5 * (1.0 + lax.erf(inner * (0.5**0.5)))
        active = (inner * cdf).astype(BF16)
        slope = cdf + inner * jnp.exp(-0.5 * inner * inner) * 0.3989422804014327
        partial_out = dot(active, out_weight) + 0.5 * out_bias[0].astype(F32)
        returned = swap_experts(
            partial_out.astype(BF16).reshape(experts, capacity, width)
        ).reshape(-1, width)
        picked = [dot(picks[k], returned) for k in range(2)]
        combined = gates[:, 0:1] * picked[0] + gates[:, 1:2] * picked[1]
        state_next = after_attn + mdl_total(combined)
        saved.append(
            (
                state,
                h_one,
                query_rows,
                key_rows,
                value_rows,
                log_total,
                heads_out,
                after_attn,
                h_two,
                gates,
                rows_in,
                slope,
                active,
                picked,
            )
        )
        state = state_next
    mixed = state.astype(BF16)
    grad_state = cotangent.astype(F32)
    attn_grads = [None] * layers
    expert_grads = [None] * layers
    for layer_idx in reversed(range(layers)):
        qkv_weight, proj_weight, router_weight, vectors = fetched[layer_idx]
        in_weight, out_weight, out_bias = expert_w[layer_idx]
        hot, picks = routed[layer_idx]
        (
            state_in,
            h_one,
            query_rows,
            key_rows,
            value_rows,
            log_total,
            heads_out,
            after_attn,
            h_two,
            gates,
            rows_in,
            slope,
            active,
            picked,
        ) = saved[layer_idx]
        grad_slot = dot_tn(picks[0], (gates[:, 0:1] * grad_state).astype(BF16)) + dot_tn(
            picks[1], (gates[:, 1:2] * grad_state).astype(BF16)
        )
        grad_produced = swap_experts(
            grad_slot.astype(BF16).reshape(experts, capacity, width)
        ).reshape(-1, width)
        part_gate = jnp.stack([jnp.sum(grad_state * picked[k], axis=-1) for k in range(2)], axis=1)
        grad_gate = part_gate + other_half(part_gate)
        grad_active = dot_nt(grad_produced, out_weight)
        grad_inner = (grad_active * slope).astype(BF16)
        grad_rows = dot_nt(grad_inner, in_weight).astype(BF16)
        grad_back = swap_experts(grad_rows.reshape(experts, capacity, width)).reshape(-1, width)
        grad_out_b = jnp.sum(grad_produced.astype(F32), axis=0)
        grad_out_w = dot_tn(active, grad_produced)
        grad_in_w = dot_tn(rows_in, grad_inner)
        grad_in_b = jnp.sum(grad_inner.astype(F32), axis=0)
        grad_chosen = gates * (grad_gate - jnp.sum(gates * grad_gate, axis=-1, keepdims=True))
        grad_logits = grad_chosen[:, 0:1] * hot[0].astype(F32) + grad_chosen[:, 1:2] * hot[
            1
        ].astype(F32)
        grad_logits = grad_logits.astype(BF16)
        grad_router = dot_tn(h_two, grad_logits)
        grad_h_two = mdl_total(dot(picks[0] + picks[1], grad_back)) + dot_nt(
            grad_logits, router_weight
        )
        grad_norm, grad_gain_two, grad_shift_two = norm_back(grad_h_two, after_attn, vectors[1])
        grad_after = grad_norm + grad_state
        grad_shift_out = jnp.sum(grad_after, axis=0)
        grad_attended = grad_after.astype(BF16)
        grad_proj = dot_tn(grad_attended, heads_out)
        grad_heads = dot(grad_attended, proj_weight)
        grad_qkv = attend_backward(
            grad_heads.astype(BF16), query_rows, key_rows, value_rows, log_total, score_scale
        )
        grad_qkv_w = dot_tn(h_one, grad_qkv)
        grad_h_one = mdl_total(dot_nt(grad_qkv, qkv_weight))
        grad_input, grad_gain_one, grad_shift_one = norm_back(grad_h_one, state_in, vectors[0])
        grad_state = grad_after + grad_input
        small = jnp.stack(
            [grad_gain_one, grad_gain_two, grad_shift_one, grad_shift_two, grad_shift_out], axis=1
        )
        whole = jnp.concatenate(
            [
                grad_qkv_w,
                grad_proj,
                grad_router,
                small,
                jnp.zeros((width, small_cols - experts - 5), F32),
            ],
            axis=1,
        )
        halved = rep_total(whole, 0).astype(BF16)
        blocks = swap_experts(halved.reshape(exp_count, own_rows, -1))
        attn_grads[layer_idx] = jnp.sum(blocks.astype(F32), axis=0)
        expert_grads[layer_idx] = (
            rep_total(grad_in_w, 0),
            rep_total(grad_out_w, 1),
            rep_total(grad_out_b[None], 1),
            grad_in_b + other_core(grad_in_b),
        )
    grads = jnp.stack(attn_grads)
    small = grads[:, :, qkv_cols + out_cols :]
    return (
        mixed,
        grad_state,
        grads[:, :, :qkv_cols].reshape(w_qkv.shape),
        jnp.swapaxes(grads[:, :, qkv_cols : qkv_cols + out_cols], 1, 2),
        small[:, :, :experts],
        jnp.swapaxes(small[:, :, experts : experts + 2], 1, 2),
        jnp.swapaxes(small[:, :, experts + 2 : experts + 5], 1, 2),
        jnp.stack([parts[0][None] for parts in expert_grads]),
        jnp.stack([parts[3][None] for parts in expert_grads]),
        jnp.stack([parts[1][None] for parts in expert_grads]),
        jnp.stack([parts[2] for parts in expert_grads]),
    )


def solution(mesh):
    tokens = P(("rep", "exp"), None)
    placed = (
        tokens,
        P(None, ("rep", "exp"), None),
        P(None, ("rep", "exp"), None, "mdl"),
        P(None, "mdl", ("rep", "exp")),
        P(None, ("rep", "exp"), None),
        P(None, None, ("rep", "exp")),
        P(None, None, ("rep", "exp")),
        P(None, "exp", "rep", "mdl"),
        P(None, "exp", "mdl"),
        P(None, "exp", "mdl", "rep"),
        P(None, "exp", "rep"),
    )
    return jax.shard_map(
        on_device,
        mesh=mesh,
        in_specs=placed + (tokens,),
        out_specs=(tokens, tokens) + placed[2:],
        check_vma=False,
    )
```

```python
import jax
import jax.numpy as jnp
from jax import lax
from jax.experimental import pallas as pl
from jax.experimental.pallas import tpu as pltpu
from jax.sharding import PartitionSpec as P

HD = 64
SEQ = 197
EPSILON = 1e-06
F32 = jnp.float32
BF16 = jnp.bfloat16


def norm_rows(values, gain, shift):
    row_mean = jnp.mean(values, axis=-1, keepdims=True)
    centred = values - row_mean
    row_var = jnp.mean(centred * centred, axis=-1, keepdims=True)
    return centred * lax.rsqrt(row_var + EPSILON) * gain + shift


def norm_back(grad, values, gain):
    row_mean = jnp.mean(values, axis=-1, keepdims=True)
    centred = values - row_mean
    row_var = jnp.mean(centred * centred, axis=-1, keepdims=True)
    scale = lax.rsqrt(row_var + EPSILON)
    unit = centred * scale
    scaled = grad * gain
    grad_in = scale * (
        scaled
        - jnp.mean(scaled, axis=-1, keepdims=True)
        - unit * jnp.mean(scaled * unit, axis=-1, keepdims=True)
    )
    return grad_in, jnp.sum(grad * unit, axis=0), jnp.sum(grad, axis=0)


def dot(a, b):
    return jnp.dot(a, b, preferred_element_type=F32)


def dot_tn(a, b):
    return lax.dot_general(a, b, (((0,), (0,)), ((), ())), preferred_element_type=F32)


def dot_nt(a, b):
    return lax.dot_general(a, b, (((1,), (1,)), ((), ())), preferred_element_type=F32)


def other_core(values):
    return lax.ppermute(values, "rep", [(0, 1), (1, 0)])


def other_half(values):
    return lax.ppermute(values, "mdl", [(0, 1), (1, 0)])


def mdl_total(partial_rows):
    low = partial_rows.astype(BF16)
    return low.astype(F32) + other_half(low).astype(F32)


def in_order(own, other, axis):
    first = lax.axis_index("rep") == 0
    return jnp.concatenate(
        [jnp.where(first, own, other), jnp.where(first, other, own)], axis=axis
    )


def rep_total(partial, axis):
    first = lax.axis_index("rep") == 0
    low, high = jnp.split(partial, 2, axis=axis)
    other = other_core(jnp.where(first, high, low).astype(BF16))
    return jnp.where(first, low, high) + other.astype(F32)


MESH = pl.DeviceIdType.MESH
BLOCK = 16
NEAR = 8
FAR = 4


def chip_place():
    rep = lax.axis_index("rep")
    exp = lax.axis_index("exp")
    near = (1 - rep) * (exp // 8 * 2 + exp // 4 % 2) + rep * (exp % 8)
    far = (1 - rep) * (exp % 4) + rep * (exp // 8)

    def chip_of(near_idx, far_idx):
        return (1 - rep) * (near_idx // 2 * 8 + near_idx % 2 * 4 + far_idx) + rep * (
            far_idx * 8 + near_idx
        )

    return rep, exp, near, far, chip_of


def greet(near, far, chip_of, rep):
    barrier = pltpu.get_barrier_semaphore()
    for step in range(1, NEAR):
        peer = chip_of((near + step) % NEAR, far)
        pl.semaphore_signal(barrier, inc=1, device_id={"exp": peer}, device_id_type=MESH)
    for step in range(1, FAR):
        peer = chip_of(near, (far + step) % FAR)
        pl.semaphore_signal(barrier, inc=1, device_id={"exp": peer}, device_id_type=MESH)
    pl.semaphore_signal(barrier, inc=1, device_id={"rep": 1 - rep}, device_id_type=MESH)
    pl.semaphore_wait(barrier, NEAR + FAR - 1)


def gather_kernel(
    mine, out, own_sem, near_send, near_recv, far_send, far_recv, core_send, core_recv
):
    rep, exp, near, far, chip_of = chip_place()

    def near_copy(step, slot):
        return pltpu.make_async_remote_copy(
            src_ref=mine,
            dst_ref=out.at[:, rep, exp],
            send_sem=near_send.at[step],
            recv_sem=near_recv.at[slot],
            device_id={"exp": chip_of((near + step) % NEAR, far)},
            device_id_type=MESH,
        )

    def far_copy(step, source, slot_near, slot_far):
        return pltpu.make_async_remote_copy(
            src_ref=out.at[:, rep, source],
            dst_ref=out.at[:, rep, source],
            send_sem=far_send.at[step, slot_near],
            recv_sem=far_recv.at[slot_far, slot_near],
            device_id={"exp": chip_of(near, (far + step) % FAR)},
            device_id_type=MESH,
        )

    def core_copy(source, part):
        return pltpu.make_async_remote_copy(
            src_ref=out.at[:, part, source],
            dst_ref=out.at[:, part, source],
            send_sem=core_send.at[source],
            recv_sem=core_recv.at[source],
            device_id={"rep": 1 - rep},
            device_id_type=MESH,
        )

    keep = pltpu.make_async_copy(mine, out.at[:, rep, exp], own_sem)
    keep.start()
    greet(near, far, chip_of, rep)

    @pl.loop(1, NEAR)
    def _(step):
        near_copy(step, near).start()

    keep.wait()

    @pl.loop(0, NEAR)
    def _(back):
        slot = (near - back + NEAR) % NEAR
        source = chip_of(slot, far)

        @pl.when(back > 0)
        def _():
            near_copy(back, slot).wait_recv()

        @pl.loop(1, FAR)
        def _(step):
            far_copy(step, source, slot, far).start()

        core_copy(source, rep).start()

    @pl.loop(0, NEAR)
    def _(back):
        slot = (near - back + NEAR) % NEAR

        @pl.loop(1, FAR)
        def _(step):
            slot_far = (far - step + FAR) % FAR
            source = chip_of(slot, slot_far)
            far_copy(step, source, slot, slot_far).wait_recv()
            core_copy(source, rep).start()

    @pl.loop(0, NEAR * FAR)
    def _(source):
        core_copy(source, 1 - rep).wait_recv()
        core_copy(source, rep).wait_send()

    @pl.loop(1, NEAR)
    def _(step):
        near_copy(step, near).wait_send()

    @pl.loop(1, FAR)
    def _(step):
        @pl.loop(0, NEAR)
        def _(slot):
            far_copy(step, chip_of(slot, far), slot, far).wait_send()


def gather_weights(packed):
    layers, rows, cols = packed.shape
    whole = pl.pallas_call(
        gather_kernel,
        out_shape=jax.ShapeDtypeStruct((layers, 2, NEAR * FAR, rows, cols), BF16),
        in_specs=[pl.BlockSpec(memory_space=pl.ANY)],
        out_specs=pl.BlockSpec(memory_space=pl.ANY),
        scratch_shapes=[
            pltpu.SemaphoreType.DMA(()),
            pltpu.SemaphoreType.DMA((NEAR,)),
            pltpu.SemaphoreType.DMA((NEAR,)),
            pltpu.SemaphoreType.DMA((FAR, NEAR)),
            pltpu.SemaphoreType.DMA((FAR, NEAR)),
            pltpu.SemaphoreType.DMA((NEAR * FAR,)),
            pltpu.SemaphoreType.DMA((NEAR * FAR,)),
        ],
        compiler_params=pltpu.CompilerParams(collective_id=0, has_side_effects=True),
        name="gather_weights",
    )(packed)
    return whole.reshape(layers, 2 * NEAR * FAR * rows, cols)


def scatter_kernel(
    lhs_qkv,
    lhs_proj,
    lhs_small,
    rhs_qkv,
    rhs_proj,
    rhs_small,
    sums,
    out,
    part,
    from_core,
    from_far,
    total,
    from_near,
    core_send,
    core_recv,
    far_send,
    far_recv,
    near_send,
    near_recv,
):
    rep, exp, near, far, chip_of = chip_place()
    qkv_cols, proj_cols = rhs_qkv.shape[1], rhs_proj.shape[1]
    cut = qkv_cols + proj_cols
    rows = BLOCK * 4
    chunks = NEAR * FAR // 4

    def multiply(core, chunk):
        at = pl.ds(pl.multiple_of((core * chunks + chunk) * rows, rows), rows)
        to = pl.ds(pl.multiple_of(chunk * rows, rows), rows)
        low = lambda lhs, rhs: jnp.dot(
            lhs[at, :], rhs[...], preferred_element_type=F32
        )
        part[core, to, :qkv_cols] = low(lhs_qkv, rhs_qkv).astype(BF16)
        part[core, to, qkv_cols:cut] = low(lhs_proj, rhs_proj).astype(BF16)
        part[core, to, cut:] = (low(lhs_small, rhs_small) + sums[at, :]).astype(BF16)

    def core_copy(chunk):
        to = pl.ds(pl.multiple_of(chunk * rows, rows), rows)
        return pltpu.make_async_remote_copy(
            src_ref=part.at[1 - rep, to],
            dst_ref=from_core.at[to],
            send_sem=core_send.at[chunk],
            recv_sem=core_recv.at[chunk],
            device_id={"rep": 1 - rep},
            device_id_type=MESH,
        )

    def far_copy(step, slot):
        return pltpu.make_async_remote_copy(
            src_ref=part.at[rep, block(chip_of(slot, (far + step) % FAR))],
            dst_ref=from_far.at[step, block(slot)],
            send_sem=far_send.at[step, slot],
            recv_sem=far_recv.at[step, slot],
            device_id={"exp": chip_of(near, (far + step) % FAR)},
            device_id_type=MESH,
        )

    def near_copy(step):
        return pltpu.make_async_remote_copy(
            src_ref=total.at[block((near + step) % NEAR)],
            dst_ref=from_near.at[step],
            send_sem=near_send.at[step],
            recv_sem=near_recv.at[step],
            device_id={"exp": chip_of((near + step) % NEAR, far)},
            device_id_type=MESH,
        )

    greet(near, far, chip_of, rep)

    @pl.loop(0, chunks)
    def _(chunk):
        multiply(1 - rep, chunk)
        core_copy(chunk).start()

    @pl.loop(0, chunks)
    def _(chunk):
        multiply(rep, chunk)

    @pl.loop(0, chunks)
    def _(chunk):
        to = pl.ds(pl.multiple_of(chunk * rows, rows), rows)
        core_copy(chunk).wait_recv()
        part[rep, to, :] = (
            part[rep, to, :].astype(F32) + from_core[to, :].astype(F32)
        ).astype(BF16)

    @pl.loop(1, FAR)
    def _(step):
        @pl.loop(1, NEAR + 1)
        def _(ahead):
            far_copy(step, (near + ahead) % NEAR).start()

    def add_far(slot):
        for step in range(1, FAR):
            far_copy(step, slot).wait_recv()
        value = part[rep, block(chip_of(slot, far)), :].astype(F32)
        for step in range(1, FAR):
            value = value + from_far[step, block(slot), :].astype(F32)
        return value

    @pl.loop(1, NEAR)
    def _(step):
        slot = (near + step) % NEAR
        total[block(slot), :] = add_far(slot).astype(BF16)
        near_copy(step).start()

    out[...] = add_far(near)

    @pl.loop(1, NEAR)
    def _(step):
        near_copy(step).wait_recv()
        out[...] += from_near[step].astype(F32)

    @pl.loop(1, NEAR)
    def _(step):
        near_copy(step).wait_send()

    @pl.loop(1, FAR)
    def _(step):
        @pl.loop(0, NEAR)
        def _(slot):
            far_copy(step, slot).wait_send()

    @pl.loop(0, chunks)
    def _(chunk):
        core_copy(chunk).wait_send()


def scatter_grads(lhs, rhs, sums):
    cols = sum(r.shape[1] for r in rhs)
    half = NEAR * FAR * BLOCK
    return pl.pallas_call(
        scatter_kernel,
        out_shape=jax.ShapeDtypeStruct((BLOCK, cols), F32),
        in_specs=[pl.BlockSpec(memory_space=pltpu.VMEM)] * 7,
        out_specs=pl.BlockSpec(memory_space=pltpu.VMEM),
        scratch_shapes=[
            pltpu.VMEM((2, half, cols), BF16),
            pltpu.VMEM((half, cols), BF16),
            pltpu.VMEM((FAR, NEAR * BLOCK, cols), BF16),
            pltpu.VMEM((NEAR * BLOCK, cols), BF16),
            pltpu.VMEM((NEAR, BLOCK, cols), BF16),
            pltpu.SemaphoreType.DMA((half // BLOCK // 4,)),
            pltpu.SemaphoreType.DMA((half // BLOCK // 4,)),
            pltpu.SemaphoreType.DMA((FAR, NEAR)),
            pltpu.SemaphoreType.DMA((FAR, NEAR)),
            pltpu.SemaphoreType.DMA((NEAR,)),
            pltpu.SemaphoreType.DMA((NEAR,)),
        ],
        compiler_params=pltpu.CompilerParams(
            collective_id=1, has_side_effects=True, vmem_limit_bytes=40 << 20
        ),
        name="scatter_grads",
    )(*lhs, *rhs, sums)


PLANES = 4
PLANE = 8


def block(source):
    return pl.ds(pl.multiple_of(source * BLOCK, BLOCK), BLOCK)


def plane_rows(plane):
    return pl.ds(pl.multiple_of(plane * (PLANE * BLOCK), PLANE * BLOCK), PLANE * BLOCK)


def plane_step(turn):
    return turn + turn // 2 - 2 * (turn // 3)


def greet_all(exp):
    barrier = pltpu.get_barrier_semaphore()

    @pl.loop(1, PLANES * PLANE)
    def _(step):
        peer = (exp + step) % (PLANES * PLANE)
        pl.semaphore_signal(barrier, inc=1, device_id={"exp": peer}, device_id_type=MESH)

    mdl = lax.axis_index("mdl")
    pl.semaphore_signal(barrier, inc=1, device_id={"mdl": 1 - mdl}, device_id_type=MESH)
    return barrier


def half_copy(src, dst, sems, idx):
    return pltpu.make_async_remote_copy(
        src_ref=src,
        dst_ref=dst,
        send_sem=sems.at[idx, 0],
        recv_sem=sems.at[idx, 1],
        device_id={"mdl": 1 - lax.axis_index("mdl")},
        device_id_type=MESH,
    )


def row_copy(src, dst, exp, send_sem, recv_sem, peer, source):
    return pltpu.make_async_remote_copy(
        src_ref=src.at[block(peer)],
        dst_ref=dst.at[block(exp)],
        send_sem=send_sem.at[peer],
        recv_sem=recv_sem.at[source],
        device_id={"exp": peer},
        device_id_type=MESH,
    )


def send_all(src, dst, exp, send_sem, recv_sem):
    @pl.loop(0, PLANES)
    def _(turn):
        plane = (exp // PLANE + plane_step(turn)) % PLANES

        @pl.loop(0, PLANE)
        def _(step):
            peer = plane * PLANE + (exp + step) % PLANE

            @pl.when(turn + step > 0)
            def _():
                row_copy(src, dst, exp, send_sem, recv_sem, peer, exp).start()

    dst[block(exp), :] = src[block(exp), :]


def each_plane(src, back_src, dst, back_dst, exp, sems, work):
    send_sem, recv_sem, back_send, back_recv = sems

    @pl.loop(0, PLANES)
    def _(turn):
        plane = (exp // PLANE - plane_step(turn) + PLANES) % PLANES

        @pl.loop(0, PLANE)
        def _(step):
            source = plane * PLANE + (exp - step + PLANE) % PLANE

            @pl.when(turn + step > 0)
            def _():
                row_copy(src, dst, exp, send_sem, recv_sem, source, source).wait_recv()

        work(plane_rows(plane))

        @pl.loop(0, PLANE)
        def _(step):
            source = plane * PLANE + (exp - step + PLANE) % PLANE

            @pl.when(turn + step > 0)
            def _():
                row_copy(back_src, back_dst, exp, back_send, back_recv, source, exp).start()

    back_dst[block(exp), :] = back_src[block(exp), :]


def wait_back(back_src, back_dst, exp, sems):
    @pl.loop(1, PLANES * PLANE)
    def _(step):
        source = (exp + step) % (PLANES * PLANE)
        row_copy(back_src, back_dst, exp, sems[2], sems[3], source, source).wait_recv()


def wait_sent(src, dst, back_src, back_dst, exp, sems):
    @pl.loop(1, PLANES * PLANE)
    def _(step):
        peer = (exp + step) % (PLANES * PLANE)
        row_copy(src, dst, exp, sems[0], sems[1], peer, peer).wait_send()
        row_copy(back_src, back_dst, exp, sems[2], sems[3], peer, peer).wait_send()


def load_weights(own_in, other_in, own_out, other_out, w_in, w_out, sems):
    rep = lax.axis_index("rep")
    depth = own_in.shape[0]
    copies = []
    for idx, (src_in, src_out, core) in enumerate(
        ((own_in, own_out, rep), (other_in, other_out, 1 - rep))
    ):
        place = pl.ds(pl.multiple_of(core * depth, 128), depth)
        copies.append(pltpu.make_async_copy(src_in, w_in.at[place, :], sems.at[idx]))
        copies.append(pltpu.make_async_copy(src_out, w_out.at[:, place], sems.at[2 + idx]))
    for copy in copies:
        copy.start()
    return copies


def lanes(values):
    rows = values[0].shape[0]
    lane = lax.broadcasted_iota(jnp.int32, (rows, 128), 1)
    total = jnp.zeros((rows, 128), F32)
    for idx, value in enumerate(values):
        total = jnp.where(lane == idx, value, total)
    return total


def expert_forward_kernel(
    state,
    attended,
    vectors,
    router,
    turned,
    pick0,
    pick1,
    hot0,
    hot1,
    own_in,
    other_in,
    own_out,
    other_out,
    b_in,
    b_out,
    after_out,
    h_out,
    gates_out,
    picked0_out,
    picked1_out,
    next_out,
    rows_out,
    slope_out,
    active_out,
    w_in,
    w_out,
    send,
    rows,
    slope,
    active,
    back_src,
    back,
    low_att,
    low_moe,
    own_moe,
    weight_sems,
    out_sems,
    half_sems,
    send_sem,
    recv_sem,
    back_send,
    back_recv,
):
    exp = lax.axis_index("exp")
    sems = (send_sem, recv_sem, back_send, back_recv)
    barrier = greet_all(exp)
    loads = load_weights(own_in, other_in, own_out, other_out, w_in, w_out, weight_sems)
    pl.semaphore_wait(barrier, PLANES * PLANE)
    first = half_copy(attended, low_att, half_sems, 0)
    first.start()
    first.wait_recv()
    partial = state[...] + (attended[...].astype(F32) + low_att[...].astype(F32)) + vectors[4:5, :]
    after_out[...] = partial
    h_two = norm_rows(partial, vectors[1:2, :], vectors[3:4, :]).astype(BF16)
    h_out[...] = h_two
    send[...] = dot(turned[...], h_two).astype(BF16)
    send_all(send, rows, exp, send_sem, recv_sem)
    logits = dot(h_two, router[...])
    chosen = [jnp.sum(logits * hot[...].astype(F32), axis=1, keepdims=True) for hot in (hot0, hot1)]
    top = jnp.maximum(chosen[0], chosen[1])
    raw = [jnp.exp(value - top) for value in chosen]
    gates = [value / (raw[0] + raw[1]) for value in raw]
    gates_out[...] = lanes(gates)
    for load in loads:
        load.wait()
    tile = 512

    def work(at):
        for col in range(0, active.shape[1], tile):
            cols = slice(col, col + tile)
            inner = dot(rows[at, :], w_in[:, cols]) + b_in[:, cols]
            cdf = 0.5 * (1.0 + lax.erf(inner * (0.5**0.5)))
            active[at, cols] = (inner * cdf).astype(BF16)
            slope[at, cols] = (
                cdf + inner * jnp.exp(-0.5 * inner * inner) * 0.3989422804014327
            ).astype(BF16)
        back_src[at, :] = (dot(active[at, :], w_out[...]) + b_out[...]).astype(BF16)

    each_plane(send, back_src, rows, back, exp, sems, work)
    saves = [
        pltpu.make_async_copy(src, dst, out_sems.at[idx])
        for idx, (src, dst) in enumerate(
            ((rows, rows_out), (slope, slope_out), (active, active_out))
        )
    ]
    for save in saves:
        save.start()
    wait_back(back_src, back, exp, sems)
    picked = [dot(pick[...], back[...]) for pick in (pick0, pick1)]
    own_moe[...] = (gates[0] * picked[0] + gates[1] * picked[1]).astype(BF16)
    second = half_copy(own_moe, low_moe, half_sems, 1)
    second.start()
    picked0_out[...] = picked[0].astype(BF16)
    picked1_out[...] = picked[1].astype(BF16)
    wait_sent(send, rows, back_src, back, exp, sems)
    second.wait_recv()
    next_out[...] = after_out[...] + (own_moe[...].astype(F32) + low_moe[...].astype(F32))
    first.wait_send()
    second.wait_send()
    for save in saves:
        save.wait()


VMEM_SPEC = pl.BlockSpec(memory_space=pltpu.VMEM)
ANY_SPEC = pl.BlockSpec(memory_space=pl.ANY)


def exchange_scratch(slots, width):
    return [
        pltpu.VMEM((slots, width), BF16),
        pltpu.VMEM((slots, width), BF16),
    ]


def row_sems():
    return [pltpu.SemaphoreType.DMA((PLANES * PLANE,))] * 4


def expert_forward(near, weights):
    state, turned = near[0], near[4]
    tokens, width = state.shape
    slots = turned.shape[0]
    hidden = weights[0].shape[1]
    shape = jax.ShapeDtypeStruct
    return pl.pallas_call(
        expert_forward_kernel,
        out_shape=(
            shape((tokens, width), F32),
            shape((tokens, width), BF16),
            shape((tokens, 128), F32),
            shape((tokens, width), BF16),
            shape((tokens, width), BF16),
            shape((tokens, width), F32),
            shape((slots, width), BF16),
            shape((slots, hidden), BF16),
            shape((slots, hidden), BF16),
        ),
        in_specs=[VMEM_SPEC] * 9 + [ANY_SPEC] * 4 + [VMEM_SPEC] * 2,
        out_specs=tuple([VMEM_SPEC] * 6 + [ANY_SPEC] * 3),
        scratch_shapes=[
            pltpu.VMEM((width, hidden), BF16),
            pltpu.VMEM((hidden, width), BF16),
            pltpu.VMEM((slots, width), BF16),
            pltpu.VMEM((slots, width), BF16),
            pltpu.VMEM((slots, hidden), BF16),
            pltpu.VMEM((slots, hidden), BF16),
            pltpu.VMEM((slots, width), BF16),
            pltpu.VMEM((slots, width), BF16),
            pltpu.VMEM((tokens, width), BF16),
            pltpu.VMEM((tokens, width), BF16),
            pltpu.VMEM((tokens, width), BF16),
            pltpu.SemaphoreType.DMA((4,)),
            pltpu.SemaphoreType.DMA((3,)),
            pltpu.SemaphoreType.DMA((2, 2)),
        ]
        + row_sems(),
        compiler_params=pltpu.CompilerParams(
            collective_id=2, has_side_effects=True, vmem_limit_bytes=48 << 20
        ),
        name="expert_forward",
    )(*near[:9], *weights, *near[9:])


def expert_backward_kernel(
    grad_state,
    gates,
    picked0,
    picked1,
    turned0,
    turned1,
    pick,
    hot0,
    hot1,
    router,
    after,
    vectors,
    own_in,
    other_in,
    own_out,
    other_out,
    slope_in,
    grad_after_out,
    grad_logits_out,
    sums_out,
    produced_out,
    inner_out,
    w_in,
    w_out,
    slope,
    send,
    rows,
    inner,
    back_src,
    back,
    own_gate,
    low_gate,
    own_h,
    low_h,
    weight_sems,
    out_sems,
    half_sems,
    send_sem,
    recv_sem,
    back_send,
    back_recv,
):
    exp = lax.axis_index("exp")
    sems = (send_sem, recv_sem, back_send, back_recv)
    barrier = greet_all(exp)
    loads = load_weights(own_in, other_in, own_out, other_out, w_in, w_out, weight_sems)
    loads.append(pltpu.make_async_copy(slope_in, slope, weight_sems.at[4]))
    loads[-1].start()
    grad = grad_state[...]
    gate0, gate1 = gates[:, 0:1], gates[:, 1:2]
    send[...] = (
        dot(turned0[...], (gate0 * grad).astype(BF16))
        + dot(turned1[...], (gate1 * grad).astype(BF16))
    ).astype(BF16)
    pl.semaphore_wait(barrier, PLANES * PLANE)
    send_all(send, rows, exp, send_sem, recv_sem)
    own_gate[...] = lanes(
        [
            jnp.sum(grad * picked[...].astype(F32), axis=1, keepdims=True)
            for picked in (picked0, picked1)
        ]
    )
    first = half_copy(own_gate, low_gate, half_sems, 0)
    first.start()
    for load in loads:
        load.wait()

    def work(at):
        grad_active = dot_nt(rows[at, :], w_out[...])
        inner[at, :] = (grad_active * slope[at, :].astype(F32)).astype(BF16)
        back_src[at, :] = dot_nt(inner[at, :], w_in[...]).astype(BF16)

    each_plane(send, back_src, rows, back, exp, sems, work)
    saves = [
        pltpu.make_async_copy(src, dst, out_sems.at[idx])
        for idx, (src, dst) in enumerate(((rows, produced_out), (inner, inner_out)))
    ]
    for save in saves:
        save.start()
    first.wait_recv()
    total = own_gate[...] + low_gate[...]
    grad0, grad1 = total[:, 0:1], total[:, 1:2]
    mean = gate0 * grad0 + gate1 * grad1
    grad_logits = (
        gate0 * (grad0 - mean) * hot0[...].astype(F32)
        + gate1 * (grad1 - mean) * hot1[...].astype(F32)
    ).astype(BF16)
    grad_logits_out[...] = grad_logits
    wait_back(back_src, back, exp, sems)
    own_h[...] = dot(pick[...], back[...]).astype(BF16)
    second = half_copy(own_h, low_h, half_sems, 1)
    second.start()
    from_router = dot_nt(grad_logits, router[...])
    values = after[...]
    row_mean = jnp.mean(values, axis=-1, keepdims=True)
    centred = values - row_mean
    row_var = jnp.mean(centred * centred, axis=-1, keepdims=True)
    scale = lax.rsqrt(row_var + EPSILON)
    unit = centred * scale
    wait_sent(send, rows, back_src, back, exp, sems)
    second.wait_recv()
    grad_h = own_h[...].astype(F32) + low_h[...].astype(F32) + from_router
    scaled = grad_h * vectors[1:2, :]
    grad_after = (
        scale
        * (
            scaled
            - jnp.mean(scaled, axis=-1, keepdims=True)
            - unit * jnp.mean(scaled * unit, axis=-1, keepdims=True)
        )
        + grad_state[...]
    )
    grad_after_out[...] = grad_after
    sums_out[...] = jnp.zeros_like(sums_out)
    sums_out[0:1, :] = jnp.sum(grad_h * unit, axis=0, keepdims=True)
    sums_out[1:2, :] = jnp.sum(grad_h, axis=0, keepdims=True)
    sums_out[2:3, :] = jnp.sum(grad_after, axis=0, keepdims=True)
    first.wait_send()
    second.wait_send()
    for save in saves:
        save.wait()


def expert_backward(near, weights, slope):
    grad_state, turned = near[0], near[4]
    tokens, width = grad_state.shape
    slots = turned.shape[0]
    hidden = weights[0].shape[1]
    shape = jax.ShapeDtypeStruct
    return pl.pallas_call(
        expert_backward_kernel,
        out_shape=(
            shape((tokens, width), F32),
            shape((tokens, 128), BF16),
            shape((8, width), F32),
            shape((slots, width), BF16),
            shape((slots, hidden), BF16),
        ),
        in_specs=[VMEM_SPEC] * 12 + [ANY_SPEC] * 5,
        out_specs=tuple([VMEM_SPEC] * 3 + [ANY_SPEC] * 2),
        scratch_shapes=[
            pltpu.VMEM((width, hidden), BF16),
            pltpu.VMEM((hidden, width), BF16),
            pltpu.VMEM((slots, hidden), BF16),
            pltpu.VMEM((slots, width), BF16),
            pltpu.VMEM((slots, width), BF16),
            pltpu.VMEM((slots, hidden), BF16),
            pltpu.VMEM((slots, width), BF16),
            pltpu.VMEM((slots, width), BF16),
            pltpu.VMEM((tokens, 128), F32),
            pltpu.VMEM((tokens, 128), F32),
            pltpu.VMEM((tokens, width), BF16),
            pltpu.VMEM((tokens, width), BF16),
            pltpu.SemaphoreType.DMA((5,)),
            pltpu.SemaphoreType.DMA((2,)),
            pltpu.SemaphoreType.DMA((2, 2)),
        ]
        + row_sems(),
        compiler_params=pltpu.CompilerParams(
            collective_id=3, has_side_effects=True, vmem_limit_bytes=48 << 20
        ),
        name="expert_backward",
    )(*near, *weights, slope)


def attend_forward(h_one, qkv_weight, score_scale):
    head_width = qkv_weight.shape[1] // 3
    qkv_rows = dot(h_one, qkv_weight).astype(BF16).reshape(SEQ, 3, head_width // HD, HD)
    query_rows, key_rows, value_rows = qkv_rows[:, 0], qkv_rows[:, 1], qkv_rows[:, 2]
    scores = (
        jnp.einsum("shd,thd->hst", query_rows, key_rows, preferred_element_type=F32) * score_scale
    )
    top_score = jnp.max(scores, axis=-1, keepdims=True)
    raw_weight = jnp.exp(scores - top_score)
    row_total = jnp.sum(raw_weight, axis=-1, keepdims=True)
    probs_low = (raw_weight / row_total).astype(BF16)
    log_total = top_score + jnp.log(row_total)
    heads_out = jnp.einsum("hst,thd->shd", probs_low, value_rows, preferred_element_type=F32)
    heads_out = heads_out.astype(BF16).reshape(SEQ, head_width)
    return (query_rows, key_rows, value_rows, log_total, heads_out)


def attend_backward(grad_heads, query_rows, key_rows, value_rows, log_total, score_scale):
    grad_heads = grad_heads.reshape(SEQ, query_rows.shape[1], HD)
    scores = (
        jnp.einsum("shd,thd->hst", query_rows, key_rows, preferred_element_type=F32) * score_scale
    )
    probs = jnp.exp(scores - log_total)
    probs_low = probs.astype(BF16)
    grad_probs = jnp.einsum("shd,thd->hst", grad_heads, value_rows, preferred_element_type=F32)
    grad_scores = probs * (grad_probs - jnp.sum(grad_probs * probs, axis=-1, keepdims=True))
    grad_scores = grad_scores.astype(BF16)
    grad_query = (
        jnp.einsum("hst,thd->shd", grad_scores, key_rows, preferred_element_type=F32) * score_scale
    )
    grad_key = (
        jnp.einsum("hst,shd->thd", grad_scores, query_rows, preferred_element_type=F32)
        * score_scale
    )
    grad_value = jnp.einsum("hst,shd->thd", probs_low, grad_heads, preferred_element_type=F32)
    grad_qkv = jnp.stack([grad_query, grad_key, grad_value], axis=1).astype(BF16)
    return grad_qkv.reshape(SEQ, -1)


def on_device(
    tokens_in,
    expert_ids,
    w_qkv,
    w_out,
    router,
    gains,
    shifts,
    w_in,
    b_in,
    w_exp_out,
    b_out,
    cotangent,
):
    tok_rows, width = tokens_in.shape
    exp_count = lax.axis_size("exp")
    experts = w_in.shape[1] * exp_count
    capacity = 2 * tok_rows // experts + 4
    score_scale = HD ** (-0.5)
    layers = w_qkv.shape[0]
    own_rows = w_qkv.shape[1]
    qkv_cols = 3 * w_qkv.shape[3]
    out_cols = w_out.shape[1]
    small_cols = 128
    slot_count = experts * capacity

    packed = jnp.concatenate(
        [
            w_qkv.reshape(layers, own_rows, qkv_cols),
            jnp.swapaxes(w_out, 1, 2),
            router,
            jnp.swapaxes(gains, 1, 2),
            jnp.swapaxes(shifts, 1, 2),
            jnp.zeros((layers, own_rows, small_cols - experts - 5), BF16),
        ],
        axis=2,
    )
    packed = jnp.pad(packed, ((0, 0), (0, BLOCK - own_rows), (0, 0)))
    gathered = gather_weights(packed)
    padded = gathered.shape[1]
    pad_row = jnp.arange(padded, dtype=jnp.int32)
    true_row = jnp.where(
        pad_row % BLOCK < own_rows, pad_row // BLOCK * own_rows + pad_row % BLOCK, -1
    )
    spread = (true_row[:, None] == jnp.arange(width, dtype=jnp.int32)).astype(BF16)

    def widen(values):
        return dot_nt(values, spread).astype(BF16)

    def narrow(values):
        return dot(values.astype(BF16), spread)

    def widen_turned(values):
        turned = dot_nt(spread, values).astype(BF16)
        return jnp.pad(turned, ((0, 0), (0, 256 - tok_rows)))

    def pad_tokens(values):
        return jnp.pad(values, ((0, 256 - tok_rows), (0, 0)))

    def fetch(layer_idx):
        whole = gathered[layer_idx]
        small = dot_tn(spread, whole[:, qkv_cols + out_cols :]).astype(BF16)
        vectors = small[:, experts : experts + 8].T.astype(F32)
        lane = jnp.arange(small_cols, dtype=jnp.int32)
        return (
            whole[:, :qkv_cols],
            whole[:, qkv_cols : qkv_cols + out_cols],
            jnp.where(lane < experts, small, jnp.zeros((), BF16)),
            vectors,
        )

    def fetch_experts(layer_idx):
        own_in, own_out, own_b = w_in[layer_idx, 0], w_exp_out[layer_idx, 0], b_out[layer_idx]
        return (
            (own_in, other_core(own_in), own_out, other_core(own_out)),
            0.5 * in_order(own_b, other_core(own_b), 1).astype(F32),
        )

    tokens_pad = -(-tok_rows // BLOCK) * BLOCK
    spare = tokens_pad - tok_rows
    expert_cols = jnp.arange(128, dtype=jnp.int32)
    slot_cols = jnp.arange(slot_count, dtype=jnp.int32)
    row_idx = jnp.arange(tokens_pad, dtype=jnp.int32)
    before = (row_idx[:, None] > row_idx[None, :]).astype(BF16)

    def route(ids):
        ids = jnp.pad(ids, ((0, spare), (0, 0)), constant_values=-1)
        hot = [(ids[:, k : k + 1] == expert_cols).astype(BF16) for k in range(2)]
        earlier = dot(before, hot[0] + hot[1])
        picks = []
        turned = []
        for k in range(2):
            within = jnp.sum(earlier * hot[k].astype(F32), axis=1).astype(jnp.int32)
            slots = ids[:, k] * capacity + within
            picks.append((slots[:, None] == slot_cols).astype(BF16))
            turned.append((slots[None, :] == slot_cols[:, None]).astype(BF16))
        return hot, picks, turned, turned[0] + turned[1], picks[0] + picks[1]

    fetched = [fetch(i) for i in range(layers)]
    expert_w = [fetch_experts(i) for i in range(layers)]
    routed = [route(expert_ids[i]) for i in range(layers)]

    state = jnp.pad(tokens_in.astype(F32), ((0, spare), (0, 0)))
    saved = []
    for layer_idx in range(layers):
        qkv_weight, proj_weight, router_weight, vectors = fetched[layer_idx]
        weights, out_bias = expert_w[layer_idx]
        hot, picks, turned, turned_both, picks_both = routed[layer_idx]
        inner_bias = b_in[layer_idx].astype(F32)
        h_one = norm_rows(state, vectors[0], vectors[2]).astype(BF16)[:tok_rows]
        query_rows, key_rows, value_rows, log_total, heads_out = attend_forward(
            widen(h_one), qkv_weight, score_scale
        )
        attended = narrow(dot_nt(heads_out, proj_weight)).astype(BF16)
        attended = jnp.pad(attended, ((0, spare), (0, 0)))
        after_attn, h_two, gates, picked0, picked1, state_next, rows_in, slope, active = (
            expert_forward(
                (
                    state,
                    attended,
                    vectors,
                    router_weight,
                    turned_both,
                    picks[0],
                    picks[1],
                    hot[0],
                    hot[1],
                    inner_bias,
                    out_bias,
                ),
                weights,
            )
        )
        saved.append(
            (
                state,
                h_one,
                query_rows,
                key_rows,
                value_rows,
                log_total,
                heads_out,
                after_attn,
                h_two,
                gates,
                rows_in,
                slope,
                active,
                (picked0, picked1),
            )
        )
        state = state_next
    mixed = state[:tok_rows].astype(BF16)
    grad_state = jnp.pad(cotangent.astype(F32), ((0, spare), (0, 0)))
    attn_grads = [None] * layers
    expert_grads = [None] * layers
    for layer_idx in reversed(range(layers)):
        qkv_weight, proj_weight, router_weight, vectors = fetched[layer_idx]
        weights, out_bias = expert_w[layer_idx]
        hot, picks, turned, turned_both, picks_both = routed[layer_idx]
        (
            state_in,
            h_one,
            query_rows,
            key_rows,
            value_rows,
            log_total,
            heads_out,
            after_attn,
            h_two,
            gates,
            rows_in,
            slope,
            active,
            picked,
        ) = saved[layer_idx]
        grad_after, grad_logits, norm_sums, grad_produced, grad_inner = expert_backward(
            (
                grad_state,
                gates,
                picked[0],
                picked[1],
                turned[0],
                turned[1],
                picks_both,
                hot[0],
                hot[1],
                router_weight,
                after_attn,
                vectors,
            ),
            weights,
            slope,
        )
        grad_out_b = jnp.sum(grad_produced.astype(F32), axis=0)
        grad_out_w = dot_tn(active, grad_produced)
        grad_in_w = dot_tn(rows_in, grad_inner)
        grad_in_b = jnp.sum(grad_inner.astype(F32), axis=0)
        grad_attended = grad_after.astype(BF16)[:tok_rows]
        grad_heads = dot(widen(grad_attended), proj_weight)
        grad_qkv = attend_backward(
            grad_heads.astype(BF16), query_rows, key_rows, value_rows, log_total, score_scale
        )
        grad_h_one = mdl_total(narrow(dot_nt(grad_qkv, qkv_weight)))
        grad_input, grad_gain_one, grad_shift_one = norm_back(
            grad_h_one, state_in[:tok_rows], vectors[0]
        )
        grad_state = grad_after + jnp.pad(grad_input, ((0, spare), (0, 0)))
        small = jnp.stack(
            [grad_gain_one, norm_sums[0], grad_shift_one, norm_sums[1], norm_sums[2]], axis=1
        )
        sums = jnp.pad(
            dot(spread, small.astype(BF16)), ((0, 0), (experts, small_cols - experts - 5))
        )
        attn_grads[layer_idx] = scatter_grads(
            (
                widen_turned(h_one),
                widen_turned(grad_attended),
                widen_turned(h_two[:tok_rows]),
            ),
            (
                pad_tokens(grad_qkv),
                pad_tokens(heads_out),
                pad_tokens(grad_logits[:tok_rows]),
            ),
            sums,
        )[:own_rows]
        expert_grads[layer_idx] = (
            rep_total(grad_in_w, 0),
            rep_total(grad_out_w, 1),
            rep_total(grad_out_b[None], 1),
            grad_in_b + other_core(grad_in_b),
        )
    grads = jnp.stack(attn_grads)
    small = grads[:, :, qkv_cols + out_cols :]
    return (
        mixed,
        grad_state[:tok_rows],
        grads[:, :, :qkv_cols].reshape(w_qkv.shape),
        jnp.swapaxes(grads[:, :, qkv_cols : qkv_cols + out_cols], 1, 2),
        small[:, :, :experts],
        jnp.swapaxes(small[:, :, experts : experts + 2], 1, 2),
        jnp.swapaxes(small[:, :, experts + 2 : experts + 5], 1, 2),
        jnp.stack([parts[0][None] for parts in expert_grads]),
        jnp.stack([parts[3][None] for parts in expert_grads]),
        jnp.stack([parts[1][None] for parts in expert_grads]),
        jnp.stack([parts[2] for parts in expert_grads]),
    )


def solution(mesh):
    tokens = P(("rep", "exp"), None)
    placed = (
        tokens,
        P(None, ("rep", "exp"), None),
        P(None, ("rep", "exp"), None, "mdl"),
        P(None, "mdl", ("rep", "exp")),
        P(None, ("rep", "exp"), None),
        P(None, None, ("rep", "exp")),
        P(None, None, ("rep", "exp")),
        P(None, "exp", "rep", "mdl"),
        P(None, "exp", "mdl"),
        P(None, "exp", "mdl", "rep"),
        P(None, "exp", "rep"),
    )
    return jax.shard_map(
        on_device,
        mesh=mesh,
        in_specs=placed + (tokens,),
        out_specs=(tokens, tokens) + placed[2:],
        check_vma=False,
    )
```

```python
import jax
import jax.numpy as jnp
from jax import lax
from jax.experimental import pallas as pl
from jax.experimental.pallas import tpu as pltpu
from jax.sharding import PartitionSpec as P

HD = 64
SEQ = 197
EPSILON = 1e-06
F32 = jnp.float32
BF16 = jnp.bfloat16


def norm_rows(values, gain, shift):
    row_mean = jnp.mean(values, axis=-1, keepdims=True)
    centred = values - row_mean
    row_var = jnp.mean(centred * centred, axis=-1, keepdims=True)
    return centred * lax.rsqrt(row_var + EPSILON) * gain + shift


def dot(a, b):
    return jnp.dot(a, b, preferred_element_type=F32)


def dot_tn(a, b):
    return lax.dot_general(a, b, (((0,), (0,)), ((), ())), preferred_element_type=F32)


def dot_nt(a, b):
    return lax.dot_general(a, b, (((1,), (1,)), ((), ())), preferred_element_type=F32)


def other_core(values):
    return lax.ppermute(values, "rep", [(0, 1), (1, 0)])


def in_order(own, other, axis):
    first = lax.axis_index("rep") == 0
    return jnp.concatenate(
        [jnp.where(first, own, other), jnp.where(first, other, own)], axis=axis
    )


MESH = pl.DeviceIdType.MESH
BLOCK = 16
NEAR = 8
FAR = 4


def chip_place():
    rep = lax.axis_index("rep")
    exp = lax.axis_index("exp")
    near = (1 - rep) * (exp // 8 * 2 + exp // 4 % 2) + rep * (exp % 8)
    far = (1 - rep) * (exp % 4) + rep * (exp // 8)

    def chip_of(near_idx, far_idx):
        return (1 - rep) * (near_idx // 2 * 8 + near_idx % 2 * 4 + far_idx) + rep * (
            far_idx * 8 + near_idx
        )

    return rep, exp, near, far, chip_of


def greet(near, far, chip_of, rep):
    barrier = pltpu.get_barrier_semaphore()
    for step in range(1, NEAR):
        peer = chip_of((near + step) % NEAR, far)
        pl.semaphore_signal(barrier, inc=1, device_id={"exp": peer}, device_id_type=MESH)
    for step in range(1, FAR):
        peer = chip_of(near, (far + step) % FAR)
        pl.semaphore_signal(barrier, inc=1, device_id={"exp": peer}, device_id_type=MESH)
    pl.semaphore_signal(barrier, inc=1, device_id={"rep": 1 - rep}, device_id_type=MESH)
    pl.semaphore_wait(barrier, NEAR + FAR - 1)


def gather_kernel(
    mine,
    whole0,
    whole1,
    own_sem,
    near_send,
    near_recv,
    far_send,
    far_recv,
    core_send,
    core_recv,
):
    rep, exp, near, far, chip_of = chip_place()
    wholes = (whole0, whole1)

    def near_copy(layer, step, slot):
        return pltpu.make_async_remote_copy(
            src_ref=mine.at[layer],
            dst_ref=wholes[layer].at[rep, exp],
            send_sem=near_send.at[layer, step],
            recv_sem=near_recv.at[layer, slot],
            device_id={"exp": chip_of((near + step) % NEAR, far)},
            device_id_type=MESH,
        )

    def far_copy(layer, step, source, slot_near, slot_far):
        return pltpu.make_async_remote_copy(
            src_ref=wholes[layer].at[rep, source],
            dst_ref=wholes[layer].at[rep, source],
            send_sem=far_send.at[layer, step, slot_near],
            recv_sem=far_recv.at[layer, slot_far, slot_near],
            device_id={"exp": chip_of(near, (far + step) % FAR)},
            device_id_type=MESH,
        )

    def core_copy(layer, source, part):
        return pltpu.make_async_remote_copy(
            src_ref=wholes[layer].at[part, source],
            dst_ref=wholes[layer].at[part, source],
            send_sem=core_send.at[layer, source],
            recv_sem=core_recv.at[layer, source],
            device_id={"rep": 1 - rep},
            device_id_type=MESH,
        )

    keeps = [
        pltpu.make_async_copy(mine.at[layer], wholes[layer].at[rep, exp], own_sem.at[layer])
        for layer in range(2)
    ]
    for keep in keeps:
        keep.start()
    greet(near, far, chip_of, rep)
    for layer in range(2):

        @pl.loop(1, NEAR)
        def _(step):
            near_copy(layer, step, near).start()

    for keep in keeps:
        keep.wait()
    for layer in range(2):

        @pl.loop(0, NEAR)
        def _(back):
            slot = (near - back + NEAR) % NEAR
            source = chip_of(slot, far)

            @pl.when(back > 0)
            def _():
                near_copy(layer, back, slot).wait_recv()

            @pl.loop(1, FAR)
            def _(step):
                far_copy(layer, step, source, slot, far).start()

            core_copy(layer, source, rep).start()

    for layer in range(2):

        @pl.loop(0, NEAR)
        def _(back):
            slot = (near - back + NEAR) % NEAR

            @pl.loop(1, FAR)
            def _(step):
                slot_far = (far - step + FAR) % FAR
                source = chip_of(slot, slot_far)
                far_copy(layer, step, source, slot, slot_far).wait_recv()
                core_copy(layer, source, rep).start()

    for layer in range(2):

        @pl.loop(0, NEAR * FAR)
        def _(source):
            core_copy(layer, source, 1 - rep).wait_recv()
            core_copy(layer, source, rep).wait_send()

        @pl.loop(1, NEAR)
        def _(step):
            near_copy(layer, step, near).wait_send()

        @pl.loop(1, FAR)
        def _(step):
            @pl.loop(0, NEAR)
            def _(slot):
                far_copy(layer, step, chip_of(slot, far), slot, far).wait_send()


def gather_weights(packed):
    layers, rows, cols = packed.shape
    whole = jax.ShapeDtypeStruct((2, NEAR * FAR, rows, cols), BF16)
    got = pl.pallas_call(
        gather_kernel,
        out_shape=(whole, whole),
        in_specs=[pl.BlockSpec(memory_space=pl.ANY)],
        out_specs=(pl.BlockSpec(memory_space=pl.ANY), pl.BlockSpec(memory_space=pl.ANY)),
        scratch_shapes=[
            pltpu.SemaphoreType.DMA((2,)),
            pltpu.SemaphoreType.DMA((2, NEAR)),
            pltpu.SemaphoreType.DMA((2, NEAR)),
            pltpu.SemaphoreType.DMA((2, FAR, NEAR)),
            pltpu.SemaphoreType.DMA((2, FAR, NEAR)),
            pltpu.SemaphoreType.DMA((2, NEAR * FAR)),
            pltpu.SemaphoreType.DMA((2, NEAR * FAR)),
        ],
        compiler_params=pltpu.CompilerParams(collective_id=0, has_side_effects=True),
        name="gather_weights",
    )(packed)
    return [value.reshape(2 * NEAR * FAR * rows, cols) for value in got]


def scatter_kernel(
    h_one,
    grad_attended,
    h_two,
    rhs_qkv,
    rhs_proj,
    rhs_small,
    sums_in,
    spread,
    out,
    lhs_qkv,
    lhs_proj,
    lhs_small,
    sums,
    part,
    from_core,
    from_far,
    total,
    from_near,
    core_send,
    core_recv,
    far_send,
    far_recv,
    near_send,
    near_recv,
):
    rep, exp, near, far, chip_of = chip_place()
    qkv_cols, proj_cols = rhs_qkv.shape[1], rhs_proj.shape[1]
    cut = qkv_cols + proj_cols
    rows = BLOCK * 4
    chunks = NEAR * FAR // 4

    def multiply(core, chunk):
        at = pl.ds(pl.multiple_of((core * chunks + chunk) * rows, rows), rows)
        to = pl.ds(pl.multiple_of(chunk * rows, rows), rows)
        low = lambda lhs, rhs: jnp.dot(
            lhs[at, :], rhs[...], preferred_element_type=F32
        )
        part[core, to, :qkv_cols] = low(lhs_qkv, rhs_qkv).astype(BF16)
        part[core, to, qkv_cols:cut] = low(lhs_proj, rhs_proj).astype(BF16)
        part[core, to, cut:] = (low(lhs_small, rhs_small) + sums[at, :]).astype(BF16)

    def core_copy(chunk):
        to = pl.ds(pl.multiple_of(chunk * rows, rows), rows)
        return pltpu.make_async_remote_copy(
            src_ref=part.at[1 - rep, to],
            dst_ref=from_core.at[to],
            send_sem=core_send.at[chunk],
            recv_sem=core_recv.at[chunk],
            device_id={"rep": 1 - rep},
            device_id_type=MESH,
        )

    def far_copy(step, slot):
        return pltpu.make_async_remote_copy(
            src_ref=part.at[rep, block(chip_of(slot, (far + step) % FAR))],
            dst_ref=from_far.at[step, block(slot)],
            send_sem=far_send.at[step, slot],
            recv_sem=far_recv.at[step, slot],
            device_id={"exp": chip_of(near, (far + step) % FAR)},
            device_id_type=MESH,
        )

    def near_copy(step):
        return pltpu.make_async_remote_copy(
            src_ref=total.at[block((near + step) % NEAR)],
            dst_ref=from_near.at[step],
            send_sem=near_send.at[step],
            recv_sem=near_recv.at[step],
            device_id={"exp": chip_of((near + step) % NEAR, far)},
            device_id_type=MESH,
        )

    lhs_qkv[...] = dot_nt(spread[...], h_one[...]).astype(BF16)
    lhs_proj[...] = dot_nt(spread[...], grad_attended[...]).astype(BF16)
    lhs_small[...] = dot_nt(spread[...], h_two[...]).astype(BF16)
    sums[...] = dot_nt(spread[...], sums_in[...].astype(BF16))
    greet(near, far, chip_of, rep)

    @pl.loop(0, chunks)
    def _(chunk):
        multiply(1 - rep, chunk)
        core_copy(chunk).start()

    @pl.loop(0, chunks)
    def _(chunk):
        multiply(rep, chunk)

    @pl.loop(0, chunks)
    def _(chunk):
        to = pl.ds(pl.multiple_of(chunk * rows, rows), rows)
        core_copy(chunk).wait_recv()
        part[rep, to, :] = (
            part[rep, to, :].astype(F32) + from_core[to, :].astype(F32)
        ).astype(BF16)

    @pl.loop(1, FAR)
    def _(step):
        @pl.loop(1, NEAR + 1)
        def _(ahead):
            far_copy(step, (near + ahead) % NEAR).start()

    def add_far(slot):
        for step in range(1, FAR):
            far_copy(step, slot).wait_recv()
        value = part[rep, block(chip_of(slot, far)), :].astype(F32)
        for step in range(1, FAR):
            value = value + from_far[step, block(slot), :].astype(F32)
        return value

    @pl.loop(1, NEAR)
    def _(step):
        slot = (near + step) % NEAR
        total[block(slot), :] = add_far(slot).astype(BF16)
        near_copy(step).start()

    out[...] = add_far(near)

    @pl.loop(1, NEAR)
    def _(step):
        near_copy(step).wait_recv()
        out[...] += from_near[step].astype(F32)

    @pl.loop(1, NEAR)
    def _(step):
        near_copy(step).wait_send()

    @pl.loop(1, FAR)
    def _(step):
        @pl.loop(0, NEAR)
        def _(slot):
            far_copy(step, slot).wait_send()

    @pl.loop(0, chunks)
    def _(chunk):
        core_copy(chunk).wait_send()


def scatter_grads(lhs, rhs, sums, spread):
    cols = sum(r.shape[1] for r in rhs)
    half = NEAR * FAR * BLOCK
    tokens = lhs[0].shape[0]
    return pl.pallas_call(
        scatter_kernel,
        out_shape=jax.ShapeDtypeStruct((BLOCK, cols), F32),
        in_specs=[pl.BlockSpec(memory_space=pltpu.VMEM)] * 8,
        out_specs=pl.BlockSpec(memory_space=pltpu.VMEM),
        scratch_shapes=[
            pltpu.VMEM((2 * half, tokens), BF16),
            pltpu.VMEM((2 * half, tokens), BF16),
            pltpu.VMEM((2 * half, tokens), BF16),
            pltpu.VMEM((2 * half, 128), F32),
            pltpu.VMEM((2, half, cols), BF16),
            pltpu.VMEM((half, cols), BF16),
            pltpu.VMEM((FAR, NEAR * BLOCK, cols), BF16),
            pltpu.VMEM((NEAR * BLOCK, cols), BF16),
            pltpu.VMEM((NEAR, BLOCK, cols), BF16),
            pltpu.SemaphoreType.DMA((half // BLOCK // 4,)),
            pltpu.SemaphoreType.DMA((half // BLOCK // 4,)),
            pltpu.SemaphoreType.DMA((FAR, NEAR)),
            pltpu.SemaphoreType.DMA((FAR, NEAR)),
            pltpu.SemaphoreType.DMA((NEAR,)),
            pltpu.SemaphoreType.DMA((NEAR,)),
        ],
        compiler_params=pltpu.CompilerParams(
            collective_id=1, has_side_effects=True, vmem_limit_bytes=40 << 20
        ),
        name="scatter_grads",
    )(*lhs, *rhs, sums, spread)


PLANES = 4
PLANE = 8


def block(source):
    return pl.ds(pl.multiple_of(source * BLOCK, BLOCK), BLOCK)


def plane_rows(plane):
    return pl.ds(pl.multiple_of(plane * (PLANE * BLOCK), PLANE * BLOCK), PLANE * BLOCK)


def plane_step(turn):
    return turn + turn // 2 - 2 * (turn // 3)


def greet_all(exp):
    barrier = pltpu.get_barrier_semaphore()

    @pl.loop(1, PLANES * PLANE)
    def _(step):
        peer = (exp + step) % (PLANES * PLANE)
        pl.semaphore_signal(barrier, inc=1, device_id={"exp": peer}, device_id_type=MESH)

    mdl = lax.axis_index("mdl")
    pl.semaphore_signal(barrier, inc=1, device_id={"mdl": 1 - mdl}, device_id_type=MESH)
    return barrier


def core_send_copy(src, dst, sems, idx):
    return pltpu.make_async_remote_copy(
        src_ref=src,
        dst_ref=dst,
        send_sem=sems.at[idx, 0],
        recv_sem=sems.at[idx, 1],
        device_id={"rep": 1 - lax.axis_index("rep")},
        device_id_type=MESH,
    )


def half_copy(src, dst, sems, idx):
    return pltpu.make_async_remote_copy(
        src_ref=src,
        dst_ref=dst,
        send_sem=sems.at[idx, 0],
        recv_sem=sems.at[idx, 1],
        device_id={"mdl": 1 - lax.axis_index("mdl")},
        device_id_type=MESH,
    )


def row_copy(src, dst, exp, send_sem, recv_sem, peer, source):
    return pltpu.make_async_remote_copy(
        src_ref=src.at[block(peer)],
        dst_ref=dst.at[block(exp)],
        send_sem=send_sem.at[peer],
        recv_sem=recv_sem.at[source],
        device_id={"exp": peer},
        device_id_type=MESH,
    )


def send_all(src, dst, exp, send_sem, recv_sem):
    @pl.loop(0, PLANES)
    def _(turn):
        plane = (exp // PLANE + plane_step(turn)) % PLANES

        @pl.loop(0, PLANE)
        def _(step):
            peer = plane * PLANE + (exp + step) % PLANE

            @pl.when(turn + step > 0)
            def _():
                row_copy(src, dst, exp, send_sem, recv_sem, peer, exp).start()

    dst[block(exp), :] = src[block(exp), :]


def each_plane(src, back_src, dst, back_dst, exp, sems, work):
    send_sem, recv_sem, back_send, back_recv = sems

    @pl.loop(0, PLANES)
    def _(turn):
        plane = (exp // PLANE - plane_step(turn) + PLANES) % PLANES

        @pl.loop(0, PLANE)
        def _(step):
            source = plane * PLANE + (exp - step + PLANE) % PLANE

            @pl.when(turn + step > 0)
            def _():
                row_copy(src, dst, exp, send_sem, recv_sem, source, source).wait_recv()

        work(plane_rows(plane))

        @pl.loop(0, PLANE)
        def _(step):
            source = plane * PLANE + (exp - step + PLANE) % PLANE

            @pl.when(turn + step > 0)
            def _():
                row_copy(back_src, back_dst, exp, back_send, back_recv, source, exp).start()

    back_dst[block(exp), :] = back_src[block(exp), :]


def wait_back(back_src, back_dst, exp, sems):
    @pl.loop(1, PLANES * PLANE)
    def _(step):
        source = (exp + step) % (PLANES * PLANE)
        row_copy(back_src, back_dst, exp, sems[2], sems[3], source, source).wait_recv()


def wait_sent(src, dst, back_src, back_dst, exp, sems):
    @pl.loop(1, PLANES * PLANE)
    def _(step):
        peer = (exp + step) % (PLANES * PLANE)
        row_copy(src, dst, exp, sems[0], sems[1], peer, peer).wait_send()
        row_copy(back_src, back_dst, exp, sems[2], sems[3], peer, peer).wait_send()


def weight_loads(own_in, other_in, own_out, other_out, w_in, w_out):
    rep = lax.axis_index("rep")
    depth = own_in.shape[0]
    pairs = []
    for src_in, src_out, core in ((own_in, own_out, rep), (other_in, other_out, 1 - rep)):
        place = pl.ds(pl.multiple_of(core * depth, 128), depth)
        pairs.append((src_in, w_in.at[place, :]))
        pairs.append((src_out, w_out.at[:, place]))
    return pairs


def lanes(values):
    rows = values[0].shape[0]
    lane = lax.broadcasted_iota(jnp.int32, (rows, 128), 1)
    total = jnp.zeros((rows, 128), F32)
    for idx, value in enumerate(values):
        total = jnp.where(lane == idx, value, total)
    return total


VMEM_SPEC = pl.BlockSpec(memory_space=pltpu.VMEM)
ANY_SPEC = pl.BlockSpec(memory_space=pl.ANY)
SMALL = 128


def row_sems():
    return [pltpu.SemaphoreType.DMA((PLANES * PLANE,))] * 4


def head_slices(head, width):
    start = head * HD
    return [slice(part * width + start, part * width + start + HD) for part in range(3)]


def masked_scores(query_rows, key_rows):
    scores = dot_nt(query_rows, key_rows) * HD ** (-0.5)
    col = lax.broadcasted_iota(jnp.int32, scores.shape, 1)
    return jnp.where(col < SEQ, scores, -1e30)


def attend_forward(qkv, heads, log_total):
    width = heads.shape[1]
    totals = []
    for head in range(width // HD):
        q_at, k_at, v_at = head_slices(head, width)
        scores = masked_scores(qkv[:, q_at], qkv[:, k_at])
        top_score = jnp.max(scores, axis=-1, keepdims=True)
        raw_weight = jnp.exp(scores - top_score)
        row_total = jnp.sum(raw_weight, axis=-1, keepdims=True)
        probs_low = (raw_weight / row_total).astype(BF16)
        totals.append(top_score + jnp.log(row_total))
        heads[:, q_at] = dot(probs_low, qkv[:, v_at]).astype(BF16)
    log_total[...] = lanes(totals)


def attend_backward(grad_heads, qkv, log_total, grad_qkv):
    width = grad_heads.shape[1]
    for head in range(width // HD):
        q_at, k_at, v_at = head_slices(head, width)
        query_rows, key_rows, value_rows = qkv[:, q_at], qkv[:, k_at], qkv[:, v_at]
        grad_out = grad_heads[:, q_at]
        probs = jnp.exp(masked_scores(query_rows, key_rows) - log_total[:, head : head + 1])
        grad_probs = dot_nt(grad_out, value_rows)
        grad_scores = probs * (grad_probs - jnp.sum(grad_probs * probs, axis=-1, keepdims=True))
        grad_scores = grad_scores.astype(BF16)
        grad_qkv[:, q_at] = (dot(grad_scores, key_rows) * HD ** (-0.5)).astype(BF16)
        grad_qkv[:, k_at] = (dot_tn(grad_scores, query_rows) * HD ** (-0.5)).astype(BF16)
        grad_qkv[:, v_at] = dot_tn(probs.astype(BF16), grad_out).astype(BF16)


def block_forward_kernel(
    state,
    spread,
    turned,
    pick0,
    pick1,
    hot0,
    hot1,
    b_in,
    b_out,
    whole_in,
    own_in,
    other_in,
    own_out,
    other_out,
    after_out,
    h_out,
    gates_out,
    picked0_out,
    picked1_out,
    next_out,
    h_one_out,
    qkv_out,
    log_out,
    heads_out,
    rows_out,
    slope_out,
    active_out,
    whole,
    w_in,
    w_out,
    send,
    rows,
    slope,
    active,
    back_src,
    back,
    own_att,
    low_att,
    own_moe,
    low_moe,
    load_sems,
    out_sems,
    half_sems,
    send_sem,
    recv_sem,
    back_send,
    back_recv,
):
    exp = lax.axis_index("exp")
    sems = (send_sem, recv_sem, back_send, back_recv)
    loads = [
        pltpu.make_async_copy(src, dst, load_sems.at[idx])
        for idx, (src, dst) in enumerate(
            [(whole_in, whole)]
            + weight_loads(own_in, other_in, own_out, other_out, w_in, w_out)
        )
    ]
    for load in loads:
        load.start()
    barrier = greet_all(exp)
    qkv_cols = qkv_out.shape[1]
    cut = qkv_cols + heads_out.shape[1]
    loads[0].wait()
    small = dot_tn(whole[:, cut:], spread[...])
    first_row = PLANES * PLANE
    gain0, gain1, shift0, shift1, shift2 = [
        small[first_row + idx : first_row + idx + 1, :] for idx in range(5)
    ]
    h_one = norm_rows(state[...], gain0, shift0).astype(BF16)
    h_one_out[...] = h_one
    wide = dot_nt(h_one, spread[...]).astype(BF16)
    qkv_out[...] = dot(wide, whole[:, :qkv_cols]).astype(BF16)
    attend_forward(qkv_out, heads_out, log_out)
    own_att[...] = dot(
        dot_nt(heads_out[...], whole[:, qkv_cols:cut]).astype(BF16), spread[...]
    ).astype(BF16)
    pl.semaphore_wait(barrier, PLANES * PLANE)
    first = half_copy(own_att, low_att, half_sems, 0)
    first.start()
    first.wait_recv()
    after = state[...] + (own_att[...].astype(F32) + low_att[...].astype(F32)) + shift2
    after_out[...] = after
    h_two = norm_rows(after, gain1, shift1).astype(BF16)
    h_out[...] = h_two
    send[...] = dot(turned[...], h_two).astype(BF16)
    send_all(send, rows, exp, send_sem, recv_sem)
    logits = dot_nt(h_two, small.astype(BF16))
    chosen = [jnp.sum(logits * hot[...].astype(F32), axis=1, keepdims=True) for hot in (hot0, hot1)]
    top = jnp.maximum(chosen[0], chosen[1])
    raw = [jnp.exp(value - top) for value in chosen]
    gates = [value / (raw[0] + raw[1]) for value in raw]
    gates_out[...] = lanes(gates)
    bias_in = b_in[...].astype(F32)
    for load in loads[1:]:
        load.wait()
    tile = 512

    def work(at):
        for col in range(0, active.shape[1], tile):
            cols = slice(col, col + tile)
            inner = dot(rows[at, :], w_in[:, cols]) + bias_in[:, cols]
            cdf = 0.5 * (1.0 + lax.erf(inner * (0.5**0.5)))
            active[at, cols] = (inner * cdf).astype(BF16)
            slope[at, cols] = (
                cdf + inner * jnp.exp(-0.5 * inner * inner) * 0.3989422804014327
            ).astype(BF16)
        back_src[at, :] = (dot(active[at, :], w_out[...]) + b_out[...]).astype(BF16)

    each_plane(send, back_src, rows, back, exp, sems, work)
    saves = [
        pltpu.make_async_copy(src, dst, out_sems.at[idx])
        for idx, (src, dst) in enumerate(
            ((rows, rows_out), (slope, slope_out), (active, active_out))
        )
    ]
    for save in saves:
        save.start()
    wait_back(back_src, back, exp, sems)
    picked = [dot(pick[...], back[...]) for pick in (pick0, pick1)]
    own_moe[...] = (gates[0] * picked[0] + gates[1] * picked[1]).astype(BF16)
    second = half_copy(own_moe, low_moe, half_sems, 1)
    second.start()
    picked0_out[...] = picked[0].astype(BF16)
    picked1_out[...] = picked[1].astype(BF16)
    wait_sent(send, rows, back_src, back, exp, sems)
    second.wait_recv()
    next_out[...] = after_out[...] + (own_moe[...].astype(F32) + low_moe[...].astype(F32))
    first.wait_send()
    second.wait_send()
    for save in saves:
        save.wait()


def block_forward(near, whole, weights):
    tokens, width = near[0].shape
    slots = near[2].shape[0]
    hidden = weights[0].shape[1]
    cols = whole.shape[1]
    proj = (cols - SMALL) // 4
    shape = jax.ShapeDtypeStruct
    return pl.pallas_call(
        block_forward_kernel,
        out_shape=(
            shape((tokens, width), F32),
            shape((tokens, width), BF16),
            shape((tokens, 128), F32),
            shape((tokens, width), BF16),
            shape((tokens, width), BF16),
            shape((tokens, width), F32),
            shape((tokens, width), BF16),
            shape((tokens, 3 * proj), BF16),
            shape((tokens, 128), F32),
            shape((tokens, proj), BF16),
            shape((slots, width), BF16),
            shape((slots, hidden), BF16),
            shape((slots, hidden), BF16),
        ),
        in_specs=[VMEM_SPEC] * 9 + [ANY_SPEC] * 5,
        out_specs=tuple([VMEM_SPEC] * 10 + [ANY_SPEC] * 3),
        scratch_shapes=[
            pltpu.VMEM(whole.shape, BF16),
            pltpu.VMEM((width, hidden), BF16),
            pltpu.VMEM((hidden, width), BF16),
            pltpu.VMEM((slots, width), BF16),
            pltpu.VMEM((slots, width), BF16),
            pltpu.VMEM((slots, hidden), BF16),
            pltpu.VMEM((slots, hidden), BF16),
            pltpu.VMEM((slots, width), BF16),
            pltpu.VMEM((slots, width), BF16),
        ]
        + [pltpu.VMEM((tokens, width), BF16)] * 4
        + [
            pltpu.SemaphoreType.DMA((5,)),
            pltpu.SemaphoreType.DMA((3,)),
            pltpu.SemaphoreType.DMA((2, 2)),
        ]
        + row_sems(),
        compiler_params=pltpu.CompilerParams(
            collective_id=2, has_side_effects=True, vmem_limit_bytes=56 << 20
        ),
        name="block_forward",
    )(*near, whole, *weights)


def norm_parts(values):
    row_mean = jnp.mean(values, axis=-1, keepdims=True)
    centred = values - row_mean
    row_var = jnp.mean(centred * centred, axis=-1, keepdims=True)
    scale = lax.rsqrt(row_var + EPSILON)
    return centred * scale, scale


def norm_grad(grad, unit, scale, gain):
    scaled = grad * gain
    return scale * (
        scaled
        - jnp.mean(scaled, axis=-1, keepdims=True)
        - unit * jnp.mean(scaled * unit, axis=-1, keepdims=True)
    )


def block_backward_kernel(
    grad_state,
    spread,
    gates,
    picked0,
    picked1,
    turned0,
    turned1,
    pick,
    hot0,
    hot1,
    after,
    state_in,
    qkv,
    log_total,
    heads,
    whole_in,
    own_in,
    other_in,
    own_out,
    other_out,
    slope_in,
    active_in,
    rows_in,
    grad_out,
    grad_att_out,
    grad_logits_out,
    sums_out,
    grad_qkv_out,
    grad_in_out,
    grad_exp_out,
    grad_b_in_out,
    grad_b_out_out,
    whole,
    w_in,
    w_out,
    slope,
    active,
    kept_rows,
    send,
    rows,
    inner,
    back_src,
    back,
    own_gate,
    low_gate,
    own_h,
    low_h,
    own_one,
    low_one,
    product,
    in_away,
    in_got,
    exp_away,
    exp_got,
    bias_own,
    bias_got,
    grad_heads,
    load_sems,
    half_sems,
    core_sems,
    send_sem,
    recv_sem,
    back_send,
    back_recv,
):
    exp = lax.axis_index("exp")
    rep = lax.axis_index("rep")
    sems = (send_sem, recv_sem, back_send, back_recv)
    loads = [
        pltpu.make_async_copy(src, dst, load_sems.at[idx])
        for idx, (src, dst) in enumerate(
            weight_loads(own_in, other_in, own_out, other_out, w_in, w_out)
            + [
                (slope_in, slope),
                (whole_in, whole),
                (active_in, active),
                (rows_in, kept_rows),
            ]
        )
    ]
    for load in loads:
        load.start()
    barrier = greet_all(exp)
    pl.semaphore_signal(barrier, inc=1, device_id={"rep": 1 - rep}, device_id_type=MESH)
    grad = grad_state[...]
    gate0, gate1 = gates[:, 0:1], gates[:, 1:2]
    send[...] = (
        dot(turned0[...], (gate0 * grad).astype(BF16))
        + dot(turned1[...], (gate1 * grad).astype(BF16))
    ).astype(BF16)
    pl.semaphore_wait(barrier, PLANES * PLANE + 1)
    send_all(send, rows, exp, send_sem, recv_sem)
    own_gate[...] = lanes(
        [
            jnp.sum(grad * picked[...].astype(F32), axis=1, keepdims=True)
            for picked in (picked0, picked1)
        ]
    )
    first = half_copy(own_gate, low_gate, half_sems, 0)
    first.start()
    for load in loads:
        load.wait()
    qkv_cols = qkv.shape[1]
    cut = qkv_cols + heads.shape[1]
    small = dot_tn(whole[:, cut:], spread[...])
    first_row = PLANES * PLANE
    gain0, gain1 = [small[first_row + idx : first_row + idx + 1, :] for idx in range(2)]

    def work(at):
        grad_active = dot_nt(rows[at, :], w_out[...])
        inner[at, :] = (grad_active * slope[at, :].astype(F32)).astype(BF16)
        back_src[at, :] = dot_nt(inner[at, :], w_in[...]).astype(BF16)

    each_plane(send, back_src, rows, back, exp, sems, work)

    half = grad_in_out.shape[0]
    hidden = inner.shape[1]
    own_at = pl.ds(pl.multiple_of(rep * half, 128), half)
    other_at = pl.ds(pl.multiple_of((1 - rep) * half, 128), half)
    in_away[...] = dot_tn(kept_rows[:, other_at], inner[...]).astype(BF16)
    in_copy = core_send_copy(in_away, in_got, core_sems, 0)
    in_copy.start()
    tall = product.shape[0]
    for start in range(0, hidden, tall):
        part = slice(start, start + tall)
        product[...] = dot_tn(active[:, part], rows[...])
        grad_exp_out[part, :] = product[:, own_at]
        exp_away[part, :] = product[:, other_at].astype(BF16)
    exp_copy = core_send_copy(exp_away, exp_got, core_sems, 1)
    exp_copy.start()
    bias_own[...] = jnp.zeros_like(bias_own)
    bias_own[0:1, :hidden] = jnp.sum(inner[...].astype(F32), axis=0, keepdims=True)
    bias_own[0:1, hidden:] = jnp.sum(rows[...].astype(F32), axis=0, keepdims=True)
    bias_copy = core_send_copy(bias_own, bias_got, core_sems, 2)
    bias_copy.start()
    grad_in_out[...] = dot_tn(kept_rows[:, own_at], inner[...])

    first.wait_recv()
    total = own_gate[...] + low_gate[...]
    grad0, grad1 = total[:, 0:1], total[:, 1:2]
    mean = gate0 * grad0 + gate1 * grad1
    grad_logits = (
        gate0 * (grad0 - mean) * hot0[...].astype(F32)
        + gate1 * (grad1 - mean) * hot1[...].astype(F32)
    ).astype(BF16)
    grad_logits_out[...] = grad_logits
    from_router = dot(grad_logits, small.astype(BF16))
    unit, scale = norm_parts(after[...])
    wait_back(back_src, back, exp, sems)
    own_h[...] = dot(pick[...], back[...]).astype(BF16)
    second = half_copy(own_h, low_h, half_sems, 1)
    second.start()
    in_copy.wait_recv()
    grad_in_out[...] += in_got[...].astype(F32)
    exp_copy.wait_recv()
    grad_exp_out[...] += exp_got[...].astype(F32)
    bias_copy.wait()
    bias_own[...] += bias_got[...]
    grad_b_in_out[...] = bias_own[0:1, :hidden]
    grad_b_out_out[...] = bias_own[
        0:1, pl.ds(pl.multiple_of(hidden + rep * half, 128), half)
    ]
    wait_sent(send, rows, back_src, back, exp, sems)
    second.wait_recv()
    grad_h = own_h[...].astype(F32) + low_h[...].astype(F32) + from_router
    grad_after = norm_grad(grad_h, unit, scale, gain1) + grad_state[...]
    grad_att = grad_after.astype(BF16)
    grad_att_out[...] = grad_att
    sums_out[...] = jnp.zeros_like(sums_out)
    put = lambda idx, value: sums_out.__setitem__(
        (slice(first_row + idx, first_row + idx + 1), slice(None)),
        jnp.sum(value, axis=0, keepdims=True),
    )
    put(1, grad_h * unit)
    put(3, grad_h)
    put(4, grad_after)
    wide = dot_nt(grad_att, spread[...]).astype(BF16)
    grad_heads[...] = dot(wide, whole[:, qkv_cols:cut]).astype(BF16)
    attend_backward(grad_heads, qkv, log_total, grad_qkv_out)
    own_one[...] = dot(
        dot_nt(grad_qkv_out[...], whole[:, :qkv_cols]).astype(BF16), spread[...]
    ).astype(BF16)
    third = half_copy(own_one, low_one, half_sems, 2)
    third.start()
    unit, scale = norm_parts(state_in[...])
    third.wait_recv()
    grad_one = own_one[...].astype(F32) + low_one[...].astype(F32)
    grad_out[...] = grad_after + norm_grad(grad_one, unit, scale, gain0)
    put(0, grad_one * unit)
    put(2, grad_one)
    for copy in (first, second, third, in_copy, exp_copy):
        copy.wait_send()


def block_backward(near, whole, weights, kept):
    tokens, width = near[0].shape
    slots = near[5].shape[0]
    hidden = weights[0].shape[1]
    cols = whole.shape[1]
    proj = (cols - SMALL) // 4
    half = width // 2
    shape = jax.ShapeDtypeStruct
    return pl.pallas_call(
        block_backward_kernel,
        out_shape=(
            shape((tokens, width), F32),
            shape((tokens, width), BF16),
            shape((tokens, 128), BF16),
            shape((128, width), F32),
            shape((tokens, 3 * proj), BF16),
            shape((half, hidden), F32),
            shape((hidden, half), F32),
            shape((1, hidden), F32),
            shape((1, half), F32),
        ),
        in_specs=[VMEM_SPEC] * 15 + [ANY_SPEC] * 8,
        out_specs=tuple([VMEM_SPEC] * 9),
        scratch_shapes=[
            pltpu.VMEM(whole.shape, BF16),
            pltpu.VMEM((width, hidden), BF16),
            pltpu.VMEM((hidden, width), BF16),
            pltpu.VMEM((slots, hidden), BF16),
            pltpu.VMEM((slots, hidden), BF16),
            pltpu.VMEM((slots, width), BF16),
            pltpu.VMEM((slots, width), BF16),
            pltpu.VMEM((slots, width), BF16),
            pltpu.VMEM((slots, hidden), BF16),
            pltpu.VMEM((slots, width), BF16),
            pltpu.VMEM((slots, width), BF16),
            pltpu.VMEM((tokens, 128), F32),
            pltpu.VMEM((tokens, 128), F32),
        ]
        + [pltpu.VMEM((tokens, width), BF16)] * 4
        + [
            pltpu.VMEM((512, width), F32),
            pltpu.VMEM((half, hidden), BF16),
            pltpu.VMEM((half, hidden), BF16),
            pltpu.VMEM((hidden, half), BF16),
            pltpu.VMEM((hidden, half), BF16),
            pltpu.VMEM((8, hidden + width), F32),
            pltpu.VMEM((8, hidden + width), F32),
            pltpu.VMEM((tokens, proj), BF16),
            pltpu.SemaphoreType.DMA((8,)),
            pltpu.SemaphoreType.DMA((3, 2)),
            pltpu.SemaphoreType.DMA((3, 2)),
        ]
        + row_sems(),
        compiler_params=pltpu.CompilerParams(
            collective_id=3, has_side_effects=True, vmem_limit_bytes=56 << 20
        ),
        name="block_backward",
    )(*near, whole, *weights, *kept)


def on_device(
    tokens_in,
    expert_ids,
    w_qkv,
    w_out,
    router,
    gains,
    shifts,
    w_in,
    b_in,
    w_exp_out,
    b_out,
    cotangent,
):
    tok_rows, width = tokens_in.shape
    exp_count = lax.axis_size("exp")
    experts = w_in.shape[1] * exp_count
    capacity = 2 * tok_rows // experts + 4
    score_scale = HD ** (-0.5)
    layers = w_qkv.shape[0]
    own_rows = w_qkv.shape[1]
    qkv_cols = 3 * w_qkv.shape[3]
    out_cols = w_out.shape[1]
    small_cols = 128
    slot_count = experts * capacity

    packed = jnp.concatenate(
        [
            w_qkv.reshape(layers, own_rows, qkv_cols),
            jnp.swapaxes(w_out, 1, 2),
            router,
            jnp.swapaxes(gains, 1, 2),
            jnp.swapaxes(shifts, 1, 2),
            jnp.zeros((layers, own_rows, small_cols - experts - 5), BF16),
        ],
        axis=2,
    )
    packed = jnp.pad(packed, ((0, 0), (0, BLOCK - own_rows), (0, 0)))
    wholes = gather_weights(packed)
    expert_w = []
    for layer_idx in range(layers):
        own_in, own_out = w_in[layer_idx, 0], w_exp_out[layer_idx, 0]
        expert_w.append((own_in, other_core(own_in), own_out, other_core(own_out)))
    padded = wholes[0].shape[0]
    pad_row = jnp.arange(padded, dtype=jnp.int32)
    true_row = jnp.where(
        pad_row % BLOCK < own_rows, pad_row // BLOCK * own_rows + pad_row % BLOCK, -1
    )
    spread = (true_row[:, None] == jnp.arange(width, dtype=jnp.int32)).astype(BF16)
    out_bias = 0.5 * in_order(b_out, other_core(b_out), 2).astype(F32)

    tokens_pad = -(-tok_rows // BLOCK) * BLOCK
    spare = tokens_pad - tok_rows
    expert_cols = jnp.arange(128, dtype=jnp.int32)
    slot_cols = jnp.arange(slot_count, dtype=jnp.int32)
    row_idx = jnp.arange(tokens_pad, dtype=jnp.int32)
    before = (row_idx[:, None] > row_idx[None, :]).astype(BF16)

    def route(ids):
        ids = jnp.pad(ids, ((0, spare), (0, 0)), constant_values=-1)
        hot = [(ids[:, k : k + 1] == expert_cols).astype(BF16) for k in range(2)]
        earlier = dot(before, hot[0] + hot[1])
        picks = []
        turned = []
        for k in range(2):
            within = jnp.sum(earlier * hot[k].astype(F32), axis=1).astype(jnp.int32)
            slots = ids[:, k] * capacity + within
            picks.append((slots[:, None] == slot_cols).astype(BF16))
            turned.append((slots[None, :] == slot_cols[:, None]).astype(BF16))
        return hot, picks, turned, turned[0] + turned[1], picks[0] + picks[1]

    routed = [route(expert_ids[i]) for i in range(layers)]

    state = jnp.pad(tokens_in.astype(F32), ((0, spare), (0, 0)))
    saved = []
    for layer_idx in range(layers):
        hot, picks, turned, turned_both, picks_both = routed[layer_idx]
        got = block_forward(
            (
                state,
                spread,
                turned_both,
                picks[0],
                picks[1],
                hot[0],
                hot[1],
                b_in[layer_idx],
                out_bias[layer_idx],
            ),
            wholes[layer_idx],
            expert_w[layer_idx],
        )
        saved.append((state,) + tuple(got))
        state = got[5]
    mixed = state[:tok_rows].astype(BF16)
    grad_state = jnp.pad(cotangent.astype(F32), ((0, spare), (0, 0)))
    attn_grads = [None] * layers
    expert_grads = [None] * layers
    for layer_idx in reversed(range(layers)):
        hot, picks, turned, turned_both, picks_both = routed[layer_idx]
        (
            state_in,
            after,
            h_two,
            gates,
            picked0,
            picked1,
            _,
            h_one,
            qkv,
            log_total,
            heads,
            rows_in,
            slope,
            active,
        ) = saved[layer_idx]
        grad_state, grad_att, grad_logits, sums, grad_qkv, *expert_grads[layer_idx] = (
            block_backward(
                (
                    grad_state,
                    spread,
                    gates,
                    picked0,
                    picked1,
                    turned[0],
                    turned[1],
                    picks_both,
                    hot[0],
                    hot[1],
                    after,
                    state_in,
                    qkv,
                    log_total,
                    heads,
                ),
                wholes[layer_idx],
                expert_w[layer_idx],
                (slope, active, rows_in),
            )
        )
        attn_grads[layer_idx] = scatter_grads(
            (h_one, grad_att, h_two), (grad_qkv, heads, grad_logits), sums, spread
        )[:own_rows]
    grads = jnp.stack(attn_grads)
    small = grads[:, :, qkv_cols + out_cols :]
    return (
        mixed,
        grad_state[:tok_rows],
        grads[:, :, :qkv_cols].reshape(w_qkv.shape),
        jnp.swapaxes(grads[:, :, qkv_cols : qkv_cols + out_cols], 1, 2),
        small[:, :, :experts],
        jnp.swapaxes(small[:, :, experts : experts + 2], 1, 2),
        jnp.swapaxes(small[:, :, experts + 2 : experts + 5], 1, 2),
        jnp.stack([parts[0][None] for parts in expert_grads]),
        jnp.stack([parts[2] for parts in expert_grads]),
        jnp.stack([parts[1][None] for parts in expert_grads]),
        jnp.stack([parts[3] for parts in expert_grads]),
    )


def solution(mesh):
    tokens = P(("rep", "exp"), None)
    placed = (
        tokens,
        P(None, ("rep", "exp"), None),
        P(None, ("rep", "exp"), None, "mdl"),
        P(None, "mdl", ("rep", "exp")),
        P(None, ("rep", "exp"), None),
        P(None, None, ("rep", "exp")),
        P(None, None, ("rep", "exp")),
        P(None, "exp", "rep", "mdl"),
        P(None, "exp", "mdl"),
        P(None, "exp", "mdl", "rep"),
        P(None, "exp", "rep"),
    )
    return jax.shard_map(
        on_device,
        mesh=mesh,
        in_specs=placed + (tokens,),
        out_specs=(tokens, tokens) + placed[2:],
        check_vma=False,
    )
```

```python
import jax
import jax.numpy as jnp
from jax import lax
from jax.experimental import pallas as pl
from jax.experimental.pallas import tpu as pltpu
from jax.sharding import PartitionSpec as P

HD = 64
SEQ = 197
EPSILON = 1e-06
F32 = jnp.float32
BF16 = jnp.bfloat16


def norm_rows(values, gain, shift):
    row_mean = jnp.mean(values, axis=-1, keepdims=True)
    centred = values - row_mean
    row_var = jnp.mean(centred * centred, axis=-1, keepdims=True)
    return centred * lax.rsqrt(row_var + EPSILON) * gain + shift


def dot(a, b):
    return jnp.dot(a, b, preferred_element_type=F32)


def dot_tn(a, b):
    return lax.dot_general(a, b, (((0,), (0,)), ((), ())), preferred_element_type=F32)


def dot_nt(a, b):
    return lax.dot_general(a, b, (((1,), (1,)), ((), ())), preferred_element_type=F32)


def other_core(values):
    return lax.ppermute(values, "rep", [(0, 1), (1, 0)])


def in_order(own, other, axis):
    first = lax.axis_index("rep") == 0
    return jnp.concatenate(
        [jnp.where(first, own, other), jnp.where(first, other, own)], axis=axis
    )


MESH = pl.DeviceIdType.MESH
BLOCK = 16
VMEM_SPEC = pl.BlockSpec(memory_space=pltpu.VMEM)
ANY_SPEC = pl.BlockSpec(memory_space=pl.ANY)
SMALL = 128
NEAR = 8
FAR = 4


def chip_place():
    rep = lax.axis_index("rep")
    exp = lax.axis_index("exp")
    near = (1 - rep) * (exp // 8 * 2 + exp // 4 % 2) + rep * (exp % 8)
    far = (1 - rep) * (exp % 4) + rep * (exp // 8)

    def chip_of(near_idx, far_idx):
        return (1 - rep) * (near_idx // 2 * 8 + near_idx % 2 * 4 + far_idx) + rep * (
            far_idx * 8 + near_idx
        )

    return rep, exp, near, far, chip_of


def greet(near, far, chip_of, rep):
    barrier = pltpu.get_barrier_semaphore()
    for step in range(1, NEAR):
        peer = chip_of((near + step) % NEAR, far)
        pl.semaphore_signal(barrier, inc=1, device_id={"exp": peer}, device_id_type=MESH)
    for step in range(1, FAR):
        peer = chip_of(near, (far + step) % FAR)
        pl.semaphore_signal(barrier, inc=1, device_id={"exp": peer}, device_id_type=MESH)
    pl.semaphore_signal(barrier, inc=1, device_id={"rep": 1 - rep}, device_id_type=MESH)
    return barrier


GREETED = NEAR + FAR - 1


def gather_kernel(
    w_qkv,
    w_out,
    router,
    gains,
    shifts,
    whole0,
    whole1,
    spread,
    mine,
    filled,
    vectors,
    own_sem,
    near_send,
    near_recv,
    far_send,
    far_recv,
    core_send,
    core_recv,
):
    rep, exp, near, far, chip_of = chip_place()
    wholes = (whole0, whole1)

    def near_copy(layer, step, slot):
        return pltpu.make_async_remote_copy(
            src_ref=mine.at[layer],
            dst_ref=wholes[layer].at[rep, exp],
            send_sem=near_send.at[layer, step],
            recv_sem=near_recv.at[layer, slot],
            device_id={"exp": chip_of((near + step) % NEAR, far)},
            device_id_type=MESH,
        )

    def far_copy(layer, step, source, slot_near, slot_far):
        return pltpu.make_async_remote_copy(
            src_ref=wholes[layer].at[rep, source],
            dst_ref=wholes[layer].at[rep, source],
            send_sem=far_send.at[layer, step, slot_near],
            recv_sem=far_recv.at[layer, slot_far, slot_near],
            device_id={"exp": chip_of(near, (far + step) % FAR)},
            device_id_type=MESH,
        )

    def core_copy(layer, source, part):
        return pltpu.make_async_remote_copy(
            src_ref=wholes[layer].at[part, source],
            dst_ref=wholes[layer].at[part, source],
            send_sem=core_send.at[layer, source],
            recv_sem=core_recv.at[layer, source],
            device_id={"rep": 1 - rep},
            device_id_type=MESH,
        )

    keeps = [
        pltpu.make_async_copy(mine.at[layer], wholes[layer].at[rep, exp], own_sem.at[layer])
        for layer in range(2)
    ]
    barrier = greet(near, far, chip_of, rep)
    layers, own_rows, parts, part_cols = w_qkv.shape
    qkv_cols = parts * part_cols
    cut = qkv_cols + w_out.shape[1]
    experts = router.shape[2]
    turn = (
        lax.broadcasted_iota(jnp.int32, (BLOCK, own_rows), 0)
        == lax.broadcasted_iota(jnp.int32, (BLOCK, own_rows), 1)
    )
    turn = jnp.where(turn, 1.0, 0.0).astype(BF16)
    filled[...] = jnp.zeros_like(filled)
    vectors[...] = jnp.zeros_like(vectors)
    for layer in range(layers):
        for part in range(parts):
            filled[:own_rows, part * part_cols : (part + 1) * part_cols] = w_qkv[
                layer, :, part, :
            ].astype(F32)
        filled[:, qkv_cols:cut] = dot_nt(turn, w_out[layer])
        vectors[experts : experts + 2, :] = gains[layer].astype(F32)
        vectors[experts + 2 : experts + 5, :] = shifts[layer].astype(F32)
        filled[:, cut:] = dot_nt(turn, vectors[...].astype(BF16))
        filled[:own_rows, cut : cut + experts] = router[layer].astype(F32)
        mine[layer] = filled[...].astype(BF16)
    for keep in keeps:
        keep.start()
    pl.semaphore_wait(barrier, GREETED)
    for layer in range(2):

        @pl.loop(1, NEAR)
        def _(step):
            near_copy(layer, step, near).start()

    row = lax.broadcasted_iota(jnp.int32, spread.shape, 0)
    col = lax.broadcasted_iota(jnp.int32, spread.shape, 1)
    inside = row & (BLOCK - 1)
    true_row = (row >> 4) * own_rows + inside
    spread[...] = jnp.where((inside < own_rows) & (true_row == col), 1.0, 0.0).astype(BF16)
    for keep in keeps:
        keep.wait()
    for layer in range(2):

        @pl.loop(0, NEAR)
        def _(back):
            slot = (near - back + NEAR) % NEAR
            source = chip_of(slot, far)

            @pl.when(back > 0)
            def _():
                near_copy(layer, back, slot).wait_recv()

            @pl.loop(1, FAR)
            def _(step):
                far_copy(layer, step, source, slot, far).start()

            core_copy(layer, source, rep).start()

    for layer in range(2):

        @pl.loop(0, NEAR)
        def _(back):
            slot = (near - back + NEAR) % NEAR

            @pl.loop(1, FAR)
            def _(step):
                slot_far = (far - step + FAR) % FAR
                source = chip_of(slot, slot_far)
                far_copy(layer, step, source, slot, slot_far).wait_recv()
                core_copy(layer, source, rep).start()

    for layer in range(2):

        @pl.loop(0, NEAR * FAR)
        def _(source):
            core_copy(layer, source, 1 - rep).wait_recv()
            core_copy(layer, source, rep).wait_send()

        @pl.loop(1, NEAR)
        def _(step):
            near_copy(layer, step, near).wait_send()

        @pl.loop(1, FAR)
        def _(step):
            @pl.loop(0, NEAR)
            def _(slot):
                far_copy(layer, step, chip_of(slot, far), slot, far).wait_send()


def gather_weights(w_qkv, w_out, router, gains, shifts):
    layers, own_rows, parts, part_cols = w_qkv.shape
    cols = parts * part_cols + w_out.shape[1] + SMALL
    devices = 2 * NEAR * FAR
    whole = jax.ShapeDtypeStruct((2, NEAR * FAR, BLOCK, cols), BF16)
    got = pl.pallas_call(
        gather_kernel,
        out_shape=(
            whole,
            whole,
            jax.ShapeDtypeStruct((devices * BLOCK, devices * own_rows), BF16),
        ),
        in_specs=[VMEM_SPEC] * 5,
        out_specs=(ANY_SPEC, ANY_SPEC, VMEM_SPEC),
        scratch_shapes=[
            pltpu.VMEM((layers, BLOCK, cols), BF16),
            pltpu.VMEM((BLOCK, cols), F32),
            pltpu.VMEM((SMALL, own_rows), F32),
            pltpu.SemaphoreType.DMA((2,)),
            pltpu.SemaphoreType.DMA((2, NEAR)),
            pltpu.SemaphoreType.DMA((2, NEAR)),
            pltpu.SemaphoreType.DMA((2, FAR, NEAR)),
            pltpu.SemaphoreType.DMA((2, FAR, NEAR)),
            pltpu.SemaphoreType.DMA((2, NEAR * FAR)),
            pltpu.SemaphoreType.DMA((2, NEAR * FAR)),
        ],
        compiler_params=pltpu.CompilerParams(
            collective_id=0, has_side_effects=True, vmem_limit_bytes=32 << 20
        ),
        name="gather_weights",
    )(w_qkv, w_out, router, gains, shifts)
    return [value.reshape(devices * BLOCK, cols) for value in got[:2]], got[2]


def scatter_kernel(*refs):
    per_layer = [refs[7 * layer : 7 * layer + 7] for layer in range(2)]
    spread = refs[14]
    biases = refs[15:19]
    experts = refs[19:23]
    out_qkv, out_rest, out_b_in, out_b_out, out_in, out_exp = refs[23:29]
    (
        lhs_qkv,
        lhs_proj,
        lhs_small,
        sums,
        part,
        from_core,
        from_far,
        total,
        from_near,
        stage_in,
        stage_exp,
        stage_sems,
        core_send,
        core_recv,
        far_send,
        far_recv,
        near_send,
        near_recv,
    ) = refs[29:]
    rep, exp, near, far, chip_of = chip_place()
    qkv_cols, proj_cols = per_layer[0][3].shape[1], per_layer[0][4].shape[1]
    cut = qkv_cols + proj_cols
    rows = BLOCK * 8
    chunks = NEAR * FAR // 8
    loads, stores = [], []
    for layer in range(2):
        for kind, (stage, out) in enumerate(((stage_in, out_in), (stage_exp, out_exp))):
            idx = 2 * layer + kind
            loads.append(
                pltpu.make_async_copy(experts[idx], stage.at[layer], stage_sems.at[idx])
            )
            stores.append(
                pltpu.make_async_copy(stage.at[layer], out.at[layer, 0], stage_sems.at[idx])
            )
    for load in loads:
        load.start()

    def multiply(layer, core, chunk):
        rhs_qkv, rhs_proj, rhs_small = per_layer[layer][3:6]
        at = pl.ds(pl.multiple_of((core * chunks + chunk) * rows, rows), rows)
        to = pl.ds(pl.multiple_of(chunk * rows, rows), rows)
        part[layer, core, to, :qkv_cols] = dot(lhs_qkv[at, :], rhs_qkv[...]).astype(BF16)
        part[layer, core, to, qkv_cols:cut] = dot(lhs_proj[at, :], rhs_proj[...]).astype(BF16)
        part[layer, core, to, cut:] = (
            dot(lhs_small[at, :], rhs_small[...]) + sums[at, :]
        ).astype(BF16)

    def core_copy(layer, chunk):
        to = pl.ds(pl.multiple_of(chunk * rows, rows), rows)
        return pltpu.make_async_remote_copy(
            src_ref=part.at[layer, 1 - rep, to],
            dst_ref=from_core.at[layer, to],
            send_sem=core_send.at[layer, chunk],
            recv_sem=core_recv.at[layer, chunk],
            device_id={"rep": 1 - rep},
            device_id_type=MESH,
        )

    def far_copy(layer, step, slot):
        return pltpu.make_async_remote_copy(
            src_ref=part.at[layer, rep, block(chip_of(slot, (far + step) % FAR))],
            dst_ref=from_far.at[layer, step, block(slot)],
            send_sem=far_send.at[layer, step, slot],
            recv_sem=far_recv.at[layer, step, slot],
            device_id={"exp": chip_of(near, (far + step) % FAR)},
            device_id_type=MESH,
        )

    def near_copy(layer, step):
        return pltpu.make_async_remote_copy(
            src_ref=total.at[layer, block((near + step) % NEAR)],
            dst_ref=from_near.at[layer, step],
            send_sem=near_send.at[layer, step],
            recv_sem=near_recv.at[layer, step],
            device_id={"exp": chip_of((near + step) % NEAR, far)},
            device_id_type=MESH,
        )

    barrier = greet(near, far, chip_of, rep)
    for layer in range(2):
        h_one, grad_att, h_two = per_layer[layer][:3]
        lhs_qkv[...] = dot_nt(spread[...], h_one[...]).astype(BF16)
        lhs_proj[...] = dot_nt(spread[...], grad_att[...]).astype(BF16)
        lhs_small[...] = dot_nt(spread[...], h_two[...]).astype(BF16)
        sums[...] = dot_nt(spread[...], per_layer[layer][6][...].astype(BF16))
        if layer == 0:
            pl.semaphore_wait(barrier, GREETED)

        @pl.loop(0, chunks)
        def _(chunk):
            multiply(layer, 1 - rep, chunk)
            core_copy(layer, chunk).start()

        @pl.loop(0, chunks)
        def _(chunk):
            multiply(layer, rep, chunk)

    for layer in range(2):

        @pl.loop(0, chunks)
        def _(chunk):
            to = pl.ds(pl.multiple_of(chunk * rows, rows), rows)
            core_copy(layer, chunk).wait_recv()
            part[layer, rep, to, :] = (
                part[layer, rep, to, :].astype(F32) + from_core[layer, to, :].astype(F32)
            ).astype(BF16)

        @pl.loop(1, NEAR + 1)
        def _(ahead):
            @pl.loop(1, FAR)
            def _(step):
                far_copy(layer, step, (near + ahead) % NEAR).start()

    for load in loads:
        load.wait()
    for store in stores:
        store.start()
    for layer in range(2):
        out_b_in[layer] = biases[2 * layer][...]
        out_b_out[layer] = biases[2 * layer + 1][...]

    def add_far(layer, slot):
        for step in range(1, FAR):
            far_copy(layer, step, slot).wait_recv()
        value = part[layer, rep, block(chip_of(slot, far)), :].astype(F32)
        for step in range(1, FAR):
            value = value + from_far[layer, step, block(slot), :].astype(F32)
        return value

    for layer in range(2):

        @pl.loop(1, NEAR)
        def _(step):
            slot = (near + step) % NEAR
            total[layer, block(slot), :] = add_far(layer, slot).astype(BF16)
            near_copy(layer, step).start()

    own_rows = out_qkv.shape[1]
    part_cols = qkv_cols // 3
    for layer in range(2):
        value = add_far(layer, near)
        for step in range(1, NEAR):
            near_copy(layer, step).wait_recv()
            value = value + from_near[layer, step].astype(F32)
        for idx in range(3):
            out_qkv[layer, :, idx, :] = value[:own_rows, idx * part_cols : (idx + 1) * part_cols]
        out_rest[layer] = value[:, qkv_cols:]

    for layer in range(2):

        @pl.loop(1, NEAR)
        def _(step):
            near_copy(layer, step).wait_send()

        @pl.loop(1, FAR)
        def _(step):
            @pl.loop(0, NEAR)
            def _(slot):
                far_copy(layer, step, slot).wait_send()

        @pl.loop(0, chunks)
        def _(chunk):
            core_copy(layer, chunk).wait_send()

    for store in stores:
        store.wait()


def scatter_grads(attn, spread, experts, own_rows):
    tokens = attn[0][0].shape[0]
    qkv_cols, proj_cols = attn[0][3].shape[1], attn[0][4].shape[1]
    cols = qkv_cols + proj_cols + SMALL
    half = NEAR * FAR * BLOCK
    grad_in, grad_exp, grad_b_in, grad_b_out = experts[0]
    shape = jax.ShapeDtypeStruct
    chunks = NEAR * FAR // 8
    return pl.pallas_call(
        scatter_kernel,
        out_shape=(
            shape((2, own_rows, 3, qkv_cols // 3), F32),
            shape((2, BLOCK, proj_cols + SMALL), F32),
            shape((2,) + grad_b_in.shape, F32),
            shape((2,) + grad_b_out.shape, F32),
            shape((2, 1) + grad_in.shape, F32),
            shape((2, 1) + grad_exp.shape, F32),
        ),
        in_specs=[VMEM_SPEC] * 19 + [ANY_SPEC] * 4,
        out_specs=tuple([VMEM_SPEC] * 4 + [ANY_SPEC] * 2),
        scratch_shapes=[
            pltpu.VMEM((2 * half, tokens), BF16),
            pltpu.VMEM((2 * half, tokens), BF16),
            pltpu.VMEM((2 * half, tokens), BF16),
            pltpu.VMEM((2 * half, SMALL), F32),
            pltpu.VMEM((2, 2, half, cols), BF16),
            pltpu.VMEM((2, half, cols), BF16),
            pltpu.VMEM((2, FAR, NEAR * BLOCK, cols), BF16),
            pltpu.VMEM((2, NEAR * BLOCK, cols), BF16),
            pltpu.VMEM((2, NEAR, BLOCK, cols), BF16),
            pltpu.VMEM((2,) + grad_in.shape, F32),
            pltpu.VMEM((2,) + grad_exp.shape, F32),
            pltpu.SemaphoreType.DMA((4,)),
            pltpu.SemaphoreType.DMA((2, chunks)),
            pltpu.SemaphoreType.DMA((2, chunks)),
            pltpu.SemaphoreType.DMA((2, FAR, NEAR)),
            pltpu.SemaphoreType.DMA((2, FAR, NEAR)),
            pltpu.SemaphoreType.DMA((2, NEAR)),
            pltpu.SemaphoreType.DMA((2, NEAR)),
        ],
        compiler_params=pltpu.CompilerParams(
            collective_id=1, has_side_effects=True, vmem_limit_bytes=56 << 20
        ),
        name="scatter_grads",
    )(
        *attn[0],
        *attn[1],
        spread,
        *(value for parts in experts for value in parts[2:]),
        *(value for parts in experts for value in parts[:2]),
    )


PLANES = 4
PLANE = 8


def block(source):
    return pl.ds(pl.multiple_of(source * BLOCK, BLOCK), BLOCK)


def plane_rows(plane):
    return pl.ds(pl.multiple_of(plane * (PLANE * BLOCK), PLANE * BLOCK), PLANE * BLOCK)


def plane_step(turn):
    return turn + turn // 2 - 2 * (turn // 3)


def greet_all(exp):
    barrier = pltpu.get_barrier_semaphore()

    @pl.loop(1, PLANES * PLANE)
    def _(step):
        peer = (exp + step) % (PLANES * PLANE)
        pl.semaphore_signal(barrier, inc=1, device_id={"exp": peer}, device_id_type=MESH)

    mdl = lax.axis_index("mdl")
    pl.semaphore_signal(barrier, inc=1, device_id={"mdl": 1 - mdl}, device_id_type=MESH)
    return barrier


def core_send_copy(src, dst, sems, idx):
    return pltpu.make_async_remote_copy(
        src_ref=src,
        dst_ref=dst,
        send_sem=sems.at[idx, 0],
        recv_sem=sems.at[idx, 1],
        device_id={"rep": 1 - lax.axis_index("rep")},
        device_id_type=MESH,
    )


def half_copy(src, dst, sems, idx):
    return pltpu.make_async_remote_copy(
        src_ref=src,
        dst_ref=dst,
        send_sem=sems.at[idx, 0],
        recv_sem=sems.at[idx, 1],
        device_id={"mdl": 1 - lax.axis_index("mdl")},
        device_id_type=MESH,
    )


def row_copy(src, dst, exp, send_sem, recv_sem, peer, source):
    return pltpu.make_async_remote_copy(
        src_ref=src.at[block(peer)],
        dst_ref=dst.at[block(exp)],
        send_sem=send_sem.at[peer],
        recv_sem=recv_sem.at[source],
        device_id={"exp": peer},
        device_id_type=MESH,
    )


def send_all(src, dst, exp, send_sem, recv_sem):
    @pl.loop(0, PLANES)
    def _(turn):
        plane = (exp // PLANE + plane_step(turn)) % PLANES

        @pl.loop(0, PLANE)
        def _(step):
            peer = plane * PLANE + (exp + step) % PLANE

            @pl.when(turn + step > 0)
            def _():
                row_copy(src, dst, exp, send_sem, recv_sem, peer, exp).start()

    dst[block(exp), :] = src[block(exp), :]


def each_plane(src, back_src, dst, back_dst, exp, sems, work):
    send_sem, recv_sem, back_send, back_recv = sems

    @pl.loop(0, PLANES)
    def _(turn):
        plane = (exp // PLANE - plane_step(turn) + PLANES) % PLANES

        @pl.loop(0, PLANE)
        def _(step):
            source = plane * PLANE + (exp - step + PLANE) % PLANE

            @pl.when(turn + step > 0)
            def _():
                row_copy(src, dst, exp, send_sem, recv_sem, source, source).wait_recv()

        work(plane_rows(plane))

        @pl.loop(0, PLANE)
        def _(step):
            source = plane * PLANE + (exp - step + PLANE) % PLANE

            @pl.when(turn + step > 0)
            def _():
                row_copy(back_src, back_dst, exp, back_send, back_recv, source, exp).start()

    back_dst[block(exp), :] = back_src[block(exp), :]


def wait_back(back_src, back_dst, exp, sems):
    @pl.loop(1, PLANES * PLANE)
    def _(step):
        source = (exp + step) % (PLANES * PLANE)
        row_copy(back_src, back_dst, exp, sems[2], sems[3], source, source).wait_recv()


def wait_sent(src, dst, back_src, back_dst, exp, sems):
    @pl.loop(1, PLANES * PLANE)
    def _(step):
        peer = (exp + step) % (PLANES * PLANE)
        row_copy(src, dst, exp, sems[0], sems[1], peer, peer).wait_send()
        row_copy(back_src, back_dst, exp, sems[2], sems[3], peer, peer).wait_send()


def weight_loads(own_in, other_in, own_out, other_out, w_in, w_out):
    rep = lax.axis_index("rep")
    depth = own_in.shape[0]
    pairs = []
    for src_in, src_out, core in ((own_in, own_out, rep), (other_in, other_out, 1 - rep)):
        place = pl.ds(pl.multiple_of(core * depth, 128), depth)
        pairs.append((src_in, w_in.at[place, :]))
        pairs.append((src_out, w_out.at[:, place]))
    return pairs


def lanes(values):
    rows = values[0].shape[0]
    lane = lax.broadcasted_iota(jnp.int32, (rows, 128), 1)
    total = jnp.zeros((rows, 128), F32)
    for idx, value in enumerate(values):
        total = jnp.where(lane == idx, value, total)
    return total


def row_sems():
    return [pltpu.SemaphoreType.DMA((PLANES * PLANE,))] * 4


def head_slices(head, width):
    start = head * HD
    return [slice(part * width + start, part * width + start + HD) for part in range(3)]


def masked_scores(query_rows, key_rows):
    scores = dot_nt(query_rows, key_rows) * HD ** (-0.5)
    col = lax.broadcasted_iota(jnp.int32, scores.shape, 1)
    return jnp.where(col < SEQ, scores, -1e30)


def route(ids, hot0, hot1, pick0, pick1):
    tokens, slots = pick0.shape
    lane = lax.broadcasted_iota(jnp.int32, (tokens, 128), 1)
    hots = [jnp.where(ids[:, k : k + 1] == lane, 1.0, 0.0) for k in range(2)]
    hot0[...], hot1[...] = hots[0].astype(BF16), hots[1].astype(BF16)
    row = lax.broadcasted_iota(jnp.int32, (tokens, tokens), 0)
    col = lax.broadcasted_iota(jnp.int32, (tokens, tokens), 1)
    before = jnp.where(row > col, 1.0, 0.0).astype(BF16)
    earlier = dot(before, (hots[0] + hots[1]).astype(BF16))
    place = lax.broadcasted_iota(jnp.int32, (tokens, slots), 1).astype(F32)
    for k, pick in enumerate((pick0, pick1)):
        within = jnp.sum(earlier * hots[k], axis=1, keepdims=True)
        slot = ids[:, k : k + 1].astype(F32) * BLOCK + within
        pick[...] = jnp.where(slot == place, 1.0, 0.0).astype(BF16)


def attend_forward(qkv, heads, log_total):
    width = heads.shape[1]
    totals = []
    for head in range(width // HD):
        q_at, k_at, v_at = head_slices(head, width)
        scores = masked_scores(qkv[:, q_at], qkv[:, k_at])
        top_score = jnp.max(scores, axis=-1, keepdims=True)
        raw_weight = jnp.exp(scores - top_score)
        row_total = jnp.sum(raw_weight, axis=-1, keepdims=True)
        probs_low = (raw_weight / row_total).astype(BF16)
        totals.append(top_score + jnp.log(row_total))
        heads[:, q_at] = dot(probs_low, qkv[:, v_at]).astype(BF16)
    log_total[...] = lanes(totals)


def attend_backward(grad_heads, qkv, log_total, grad_qkv):
    width = grad_heads.shape[1]
    for head in range(width // HD):
        q_at, k_at, v_at = head_slices(head, width)
        query_rows, key_rows, value_rows = qkv[:, q_at], qkv[:, k_at], qkv[:, v_at]
        grad_out = grad_heads[:, q_at]
        probs = jnp.exp(masked_scores(query_rows, key_rows) - log_total[:, head : head + 1])
        grad_probs = dot_nt(grad_out, value_rows)
        grad_scores = probs * (grad_probs - jnp.sum(grad_probs * probs, axis=-1, keepdims=True))
        grad_scores = grad_scores.astype(BF16)
        grad_qkv[:, q_at] = (dot(grad_scores, key_rows) * HD ** (-0.5)).astype(BF16)
        grad_qkv[:, k_at] = (dot_tn(grad_scores, query_rows) * HD ** (-0.5)).astype(BF16)
        grad_qkv[:, v_at] = dot_tn(probs.astype(BF16), grad_out).astype(BF16)


def block_forward_kernel(
    state,
    spread,
    ids,
    b_in,
    b_out,
    whole_in,
    own_in,
    other_in,
    own_out,
    other_out,
    after_out,
    h_out,
    gates_out,
    picked0_out,
    picked1_out,
    next_out,
    h_one_out,
    qkv_out,
    log_out,
    heads_out,
    rows_out,
    slope_out,
    active_out,
    hot0,
    hot1,
    pick0,
    pick1,
    whole,
    w_in,
    w_out,
    send,
    rows,
    slope,
    active,
    back_src,
    back,
    own_att,
    low_att,
    own_moe,
    low_moe,
    load_sems,
    out_sems,
    half_sems,
    send_sem,
    recv_sem,
    back_send,
    back_recv,
):
    exp = lax.axis_index("exp")
    sems = (send_sem, recv_sem, back_send, back_recv)
    loads = [
        pltpu.make_async_copy(src, dst, load_sems.at[idx])
        for idx, (src, dst) in enumerate(
            [(whole_in, whole)]
            + weight_loads(own_in, other_in, own_out, other_out, w_in, w_out)
        )
    ]
    for load in loads:
        load.start()
    barrier = greet_all(exp)
    qkv_cols = qkv_out.shape[1]
    cut = qkv_cols + heads_out.shape[1]
    loads[0].wait()
    small = dot_tn(whole[:, cut:], spread[...])
    first_row = PLANES * PLANE
    gain0, gain1, shift0, shift1, shift2 = [
        small[first_row + idx : first_row + idx + 1, :] for idx in range(5)
    ]
    h_one = norm_rows(state[...], gain0, shift0).astype(BF16)
    h_one_out[...] = h_one
    wide = dot_nt(h_one, spread[...]).astype(BF16)
    qkv_out[...] = dot(wide, whole[:, :qkv_cols]).astype(BF16)
    attend_forward(qkv_out, heads_out, log_out)
    route(ids, hot0, hot1, pick0, pick1)
    own_att[...] = dot(
        dot_nt(heads_out[...], whole[:, qkv_cols:cut]).astype(BF16), spread[...]
    ).astype(BF16)
    pl.semaphore_wait(barrier, PLANES * PLANE)
    first = half_copy(own_att, low_att, half_sems, 0)
    first.start()
    first.wait_recv()
    after = state[...] + (own_att[...].astype(F32) + low_att[...].astype(F32)) + shift2
    after_out[...] = after
    h_two = norm_rows(after, gain1, shift1).astype(BF16)
    h_out[...] = h_two
    send[...] = dot_tn(pick0[...] + pick1[...], h_two).astype(BF16)
    send_all(send, rows, exp, send_sem, recv_sem)
    logits = dot_nt(h_two, small.astype(BF16))
    chosen = [jnp.sum(logits * hot[...].astype(F32), axis=1, keepdims=True) for hot in (hot0, hot1)]
    top = jnp.maximum(chosen[0], chosen[1])
    raw = [jnp.exp(value - top) for value in chosen]
    gates = [value / (raw[0] + raw[1]) for value in raw]
    gates_out[...] = lanes(gates)
    bias_in = b_in[...].astype(F32)
    for load in loads[1:]:
        load.wait()
    tile = 512

    def work(at):
        for col in range(0, active.shape[1], tile):
            cols = slice(col, col + tile)
            inner = dot(rows[at, :], w_in[:, cols]) + bias_in[:, cols]
            cdf = 0.5 * (1.0 + lax.erf(inner * (0.5**0.5)))
            active[at, cols] = (inner * cdf).astype(BF16)
            slope[at, cols] = (
                cdf + inner * jnp.exp(-0.5 * inner * inner) * 0.3989422804014327
            ).astype(BF16)
        back_src[at, :] = (dot(active[at, :], w_out[...]) + b_out[...]).astype(BF16)

    each_plane(send, back_src, rows, back, exp, sems, work)
    saves = [
        pltpu.make_async_copy(src, dst, out_sems.at[idx])
        for idx, (src, dst) in enumerate(
            ((rows, rows_out), (slope, slope_out), (active, active_out))
        )
    ]
    for save in saves:
        save.start()
    wait_back(back_src, back, exp, sems)
    picked = [dot(pick[...], back[...]) for pick in (pick0, pick1)]
    own_moe[...] = (gates[0] * picked[0] + gates[1] * picked[1]).astype(BF16)
    second = half_copy(own_moe, low_moe, half_sems, 1)
    second.start()
    picked0_out[...] = picked[0].astype(BF16)
    picked1_out[...] = picked[1].astype(BF16)
    wait_sent(send, rows, back_src, back, exp, sems)
    second.wait_recv()
    next_out[...] = after_out[...] + (own_moe[...].astype(F32) + low_moe[...].astype(F32))
    first.wait_send()
    second.wait_send()
    for save in saves:
        save.wait()


def block_forward(near, whole, weights):
    tokens, width = near[0].shape
    slots = BLOCK * PLANES * PLANE
    hidden = weights[0].shape[1]
    cols = whole.shape[1]
    proj = (cols - SMALL) // 4
    shape = jax.ShapeDtypeStruct
    return pl.pallas_call(
        block_forward_kernel,
        out_shape=(
            shape((tokens, width), F32),
            shape((tokens, width), BF16),
            shape((tokens, 128), F32),
            shape((tokens, width), BF16),
            shape((tokens, width), BF16),
            shape((tokens, width), F32),
            shape((tokens, width), BF16),
            shape((tokens, 3 * proj), BF16),
            shape((tokens, 128), F32),
            shape((tokens, proj), BF16),
            shape((slots, width), BF16),
            shape((slots, hidden), BF16),
            shape((slots, hidden), BF16),
        ),
        in_specs=[VMEM_SPEC] * 5 + [ANY_SPEC] * 5,
        out_specs=tuple([VMEM_SPEC] * 10 + [ANY_SPEC] * 3),
        scratch_shapes=[
            pltpu.VMEM((tokens, 128), BF16),
            pltpu.VMEM((tokens, 128), BF16),
            pltpu.VMEM((tokens, slots), BF16),
            pltpu.VMEM((tokens, slots), BF16),
            pltpu.VMEM(whole.shape, BF16),
            pltpu.VMEM((width, hidden), BF16),
            pltpu.VMEM((hidden, width), BF16),
            pltpu.VMEM((slots, width), BF16),
            pltpu.VMEM((slots, width), BF16),
            pltpu.VMEM((slots, hidden), BF16),
            pltpu.VMEM((slots, hidden), BF16),
            pltpu.VMEM((slots, width), BF16),
            pltpu.VMEM((slots, width), BF16),
        ]
        + [pltpu.VMEM((tokens, width), BF16)] * 4
        + [
            pltpu.SemaphoreType.DMA((5,)),
            pltpu.SemaphoreType.DMA((3,)),
            pltpu.SemaphoreType.DMA((2, 2)),
        ]
        + row_sems(),
        compiler_params=pltpu.CompilerParams(
            collective_id=2, has_side_effects=True, vmem_limit_bytes=56 << 20
        ),
        name="block_forward",
    )(*near, whole, *weights)


def norm_parts(values):
    row_mean = jnp.mean(values, axis=-1, keepdims=True)
    centred = values - row_mean
    row_var = jnp.mean(centred * centred, axis=-1, keepdims=True)
    scale = lax.rsqrt(row_var + EPSILON)
    return centred * scale, scale


def norm_grad(grad, unit, scale, gain):
    scaled = grad * gain
    return scale * (
        scaled
        - jnp.mean(scaled, axis=-1, keepdims=True)
        - unit * jnp.mean(scaled * unit, axis=-1, keepdims=True)
    )


def block_backward_kernel(
    grad_state,
    spread,
    ids,
    gates,
    picked0,
    picked1,
    after,
    state_in,
    qkv,
    log_total,
    heads,
    whole_in,
    own_in,
    other_in,
    own_out,
    other_out,
    slope_in,
    active_in,
    rows_in,
    grad_out,
    grad_att_out,
    grad_logits_out,
    sums_out,
    grad_qkv_out,
    grad_in_out,
    grad_exp_out,
    grad_b_in_out,
    grad_b_out_out,
    hot0,
    hot1,
    pick0,
    pick1,
    whole,
    w_in,
    w_out,
    slope,
    active,
    kept_rows,
    send,
    rows,
    inner,
    back_src,
    back,
    own_gate,
    low_gate,
    own_h,
    low_h,
    own_one,
    low_one,
    product,
    in_away,
    in_got,
    exp_away,
    exp_got,
    bias_own,
    bias_got,
    grad_heads,
    load_sems,
    half_sems,
    core_sems,
    send_sem,
    recv_sem,
    back_send,
    back_recv,
):
    exp = lax.axis_index("exp")
    rep = lax.axis_index("rep")
    sems = (send_sem, recv_sem, back_send, back_recv)
    loads = [
        pltpu.make_async_copy(src, dst, load_sems.at[idx])
        for idx, (src, dst) in enumerate(
            weight_loads(own_in, other_in, own_out, other_out, w_in, w_out)
            + [
                (slope_in, slope),
                (whole_in, whole),
                (active_in, active),
                (rows_in, kept_rows),
            ]
        )
    ]
    for load in loads:
        load.start()
    barrier = greet_all(exp)
    pl.semaphore_signal(barrier, inc=1, device_id={"rep": 1 - rep}, device_id_type=MESH)
    grad = grad_state[...]
    gate0, gate1 = gates[:, 0:1], gates[:, 1:2]
    route(ids, hot0, hot1, pick0, pick1)
    send[...] = (
        dot_tn(pick0[...], (gate0 * grad).astype(BF16))
        + dot_tn(pick1[...], (gate1 * grad).astype(BF16))
    ).astype(BF16)
    pl.semaphore_wait(barrier, PLANES * PLANE + 1)
    send_all(send, rows, exp, send_sem, recv_sem)
    own_gate[...] = lanes(
        [
            jnp.sum(grad * picked[...].astype(F32), axis=1, keepdims=True)
            for picked in (picked0, picked1)
        ]
    )
    first = half_copy(own_gate, low_gate, half_sems, 0)
    first.start()
    for load in loads:
        load.wait()
    qkv_cols = qkv.shape[1]
    cut = qkv_cols + heads.shape[1]
    small = dot_tn(whole[:, cut:], spread[...])
    first_row = PLANES * PLANE
    gain0, gain1 = [small[first_row + idx : first_row + idx + 1, :] for idx in range(2)]

    def work(at):
        grad_active = dot_nt(rows[at, :], w_out[...])
        inner[at, :] = (grad_active * slope[at, :].astype(F32)).astype(BF16)
        back_src[at, :] = dot_nt(inner[at, :], w_in[...]).astype(BF16)

    each_plane(send, back_src, rows, back, exp, sems, work)

    half = grad_in_out.shape[0]
    hidden = inner.shape[1]
    own_at = pl.ds(pl.multiple_of(rep * half, 128), half)
    other_at = pl.ds(pl.multiple_of((1 - rep) * half, 128), half)
    in_away[...] = dot_tn(kept_rows[:, other_at], inner[...]).astype(BF16)
    in_copy = core_send_copy(in_away, in_got, core_sems, 0)
    in_copy.start()
    tall = product.shape[0]
    for start in range(0, hidden, tall):
        part = slice(start, start + tall)
        product[...] = dot_tn(active[:, part], rows[...])
        grad_exp_out[part, :] = product[:, own_at]
        exp_away[part, :] = product[:, other_at].astype(BF16)
    exp_copy = core_send_copy(exp_away, exp_got, core_sems, 1)
    exp_copy.start()
    bias_own[...] = jnp.zeros_like(bias_own)
    bias_own[0:1, :hidden] = jnp.sum(inner[...].astype(F32), axis=0, keepdims=True)
    bias_own[0:1, hidden:] = jnp.sum(rows[...].astype(F32), axis=0, keepdims=True)
    bias_copy = core_send_copy(bias_own, bias_got, core_sems, 2)
    bias_copy.start()
    grad_in_out[...] = dot_tn(kept_rows[:, own_at], inner[...])

    first.wait_recv()
    total = own_gate[...] + low_gate[...]
    grad0, grad1 = total[:, 0:1], total[:, 1:2]
    mean = gate0 * grad0 + gate1 * grad1
    grad_logits = (
        gate0 * (grad0 - mean) * hot0[...].astype(F32)
        + gate1 * (grad1 - mean) * hot1[...].astype(F32)
    ).astype(BF16)
    grad_logits_out[...] = grad_logits
    from_router = dot(grad_logits, small.astype(BF16))
    unit, scale = norm_parts(after[...])
    wait_back(back_src, back, exp, sems)
    own_h[...] = dot(pick0[...] + pick1[...], back[...]).astype(BF16)
    second = half_copy(own_h, low_h, half_sems, 1)
    second.start()
    in_copy.wait_recv()
    grad_in_out[...] += in_got[...].astype(F32)
    exp_copy.wait_recv()
    grad_exp_out[...] += exp_got[...].astype(F32)
    bias_copy.wait()
    bias_own[...] += bias_got[...]
    grad_b_in_out[...] = bias_own[0:1, :hidden]
    grad_b_out_out[...] = bias_own[
        0:1, pl.ds(pl.multiple_of(hidden + rep * half, 128), half)
    ]
    wait_sent(send, rows, back_src, back, exp, sems)
    second.wait_recv()
    grad_h = own_h[...].astype(F32) + low_h[...].astype(F32) + from_router
    grad_after = norm_grad(grad_h, unit, scale, gain1) + grad_state[...]
    grad_att = grad_after.astype(BF16)
    grad_att_out[...] = grad_att
    sums_out[...] = jnp.zeros_like(sums_out)
    put = lambda idx, value: sums_out.__setitem__(
        (slice(first_row + idx, first_row + idx + 1), slice(None)),
        jnp.sum(value, axis=0, keepdims=True),
    )
    put(1, grad_h * unit)
    put(3, grad_h)
    put(4, grad_after)
    wide = dot_nt(grad_att, spread[...]).astype(BF16)
    grad_heads[...] = dot(wide, whole[:, qkv_cols:cut]).astype(BF16)
    attend_backward(grad_heads, qkv, log_total, grad_qkv_out)
    own_one[...] = dot(
        dot_nt(grad_qkv_out[...], whole[:, :qkv_cols]).astype(BF16), spread[...]
    ).astype(BF16)
    third = half_copy(own_one, low_one, half_sems, 2)
    third.start()
    unit, scale = norm_parts(state_in[...])
    third.wait_recv()
    grad_one = own_one[...].astype(F32) + low_one[...].astype(F32)
    grad_out[...] = grad_after + norm_grad(grad_one, unit, scale, gain0)
    put(0, grad_one * unit)
    put(2, grad_one)
    for copy in (first, second, third, in_copy, exp_copy):
        copy.wait_send()


def block_backward(near, whole, weights, kept):
    tokens, width = near[0].shape
    slots = BLOCK * PLANES * PLANE
    hidden = weights[0].shape[1]
    cols = whole.shape[1]
    proj = (cols - SMALL) // 4
    half = width // 2
    shape = jax.ShapeDtypeStruct
    return pl.pallas_call(
        block_backward_kernel,
        out_shape=(
            shape((tokens, width), F32),
            shape((tokens, width), BF16),
            shape((tokens, 128), BF16),
            shape((128, width), F32),
            shape((tokens, 3 * proj), BF16),
            shape((half, hidden), F32),
            shape((hidden, half), F32),
            shape((1, hidden), F32),
            shape((1, half), F32),
        ),
        in_specs=[VMEM_SPEC] * 11 + [ANY_SPEC] * 8,
        out_specs=tuple([VMEM_SPEC] * 9),
        scratch_shapes=[
            pltpu.VMEM((tokens, 128), BF16),
            pltpu.VMEM((tokens, 128), BF16),
            pltpu.VMEM((tokens, slots), BF16),
            pltpu.VMEM((tokens, slots), BF16),
            pltpu.VMEM(whole.shape, BF16),
            pltpu.VMEM((width, hidden), BF16),
            pltpu.VMEM((hidden, width), BF16),
            pltpu.VMEM((slots, hidden), BF16),
            pltpu.VMEM((slots, hidden), BF16),
            pltpu.VMEM((slots, width), BF16),
            pltpu.VMEM((slots, width), BF16),
            pltpu.VMEM((slots, width), BF16),
            pltpu.VMEM((slots, hidden), BF16),
            pltpu.VMEM((slots, width), BF16),
            pltpu.VMEM((slots, width), BF16),
            pltpu.VMEM((tokens, 128), F32),
            pltpu.VMEM((tokens, 128), F32),
        ]
        + [pltpu.VMEM((tokens, width), BF16)] * 4
        + [
            pltpu.VMEM((512, width), F32),
            pltpu.VMEM((half, hidden), BF16),
            pltpu.VMEM((half, hidden), BF16),
            pltpu.VMEM((hidden, half), BF16),
            pltpu.VMEM((hidden, half), BF16),
            pltpu.VMEM((8, hidden + width), F32),
            pltpu.VMEM((8, hidden + width), F32),
            pltpu.VMEM((tokens, proj), BF16),
            pltpu.SemaphoreType.DMA((8,)),
            pltpu.SemaphoreType.DMA((3, 2)),
            pltpu.SemaphoreType.DMA((3, 2)),
        ]
        + row_sems(),
        compiler_params=pltpu.CompilerParams(
            collective_id=3, has_side_effects=True, vmem_limit_bytes=56 << 20
        ),
        name="block_backward",
    )(*near, whole, *weights, *kept)


def on_device(
    tokens_in,
    expert_ids,
    w_qkv,
    w_out,
    router,
    gains,
    shifts,
    w_in,
    b_in,
    w_exp_out,
    b_out,
    cotangent,
):
    tok_rows, width = tokens_in.shape
    layers = w_qkv.shape[0]
    own_rows = w_qkv.shape[1]
    out_cols = w_out.shape[1]
    experts = w_in.shape[1] * lax.axis_size("exp")
    wholes, spread = gather_weights(w_qkv, w_out, router, gains, shifts)
    expert_w = []
    for layer_idx in range(layers):
        own_in, own_out = w_in[layer_idx, 0], w_exp_out[layer_idx, 0]
        expert_w.append((own_in, other_core(own_in), own_out, other_core(own_out)))
    out_bias = 0.5 * in_order(b_out, other_core(b_out), 2).astype(F32)

    spare = -tok_rows % BLOCK
    ids = jnp.pad(expert_ids, ((0, 0), (0, spare), (0, 0)), constant_values=-1)
    state = jnp.pad(tokens_in.astype(F32), ((0, spare), (0, 0)))
    saved = []
    for layer_idx in range(layers):
        got = block_forward(
            (
                state,
                spread,
                ids[layer_idx],
                b_in[layer_idx],
                out_bias[layer_idx],
            ),
            wholes[layer_idx],
            expert_w[layer_idx],
        )
        saved.append((state,) + tuple(got))
        state = got[5]
    mixed = state[:tok_rows].astype(BF16)
    grad_state = jnp.pad(cotangent.astype(F32), ((0, spare), (0, 0)))
    attn_grads = [None] * layers
    expert_grads = [None] * layers
    for layer_idx in reversed(range(layers)):
        (
            state_in,
            after,
            h_two,
            gates,
            picked0,
            picked1,
            _,
            h_one,
            qkv,
            log_total,
            heads,
            rows_in,
            slope,
            active,
        ) = saved[layer_idx]
        grad_state, grad_att, grad_logits, sums, grad_qkv, *expert_grads[layer_idx] = (
            block_backward(
                (
                    grad_state,
                    spread,
                    ids[layer_idx],
                    gates,
                    picked0,
                    picked1,
                    after,
                    state_in,
                    qkv,
                    log_total,
                    heads,
                ),
                wholes[layer_idx],
                expert_w[layer_idx],
                (slope, active, rows_in),
            )
        )
        attn_grads[layer_idx] = (h_one, grad_att, h_two, grad_qkv, heads, grad_logits, sums)
    grad_w_qkv, rest, grad_b_in, grad_b_out, grad_w_in, grad_w_exp_out = scatter_grads(
        attn_grads, spread, expert_grads, own_rows
    )
    rest = rest[:, :own_rows]
    small = rest[:, :, out_cols:]
    return (
        mixed,
        grad_state[:tok_rows],
        grad_w_qkv,
        jnp.swapaxes(rest[:, :, :out_cols], 1, 2),
        small[:, :, :experts],
        jnp.swapaxes(small[:, :, experts : experts + 2], 1, 2),
        jnp.swapaxes(small[:, :, experts + 2 : experts + 5], 1, 2),
        grad_w_in,
        grad_b_in,
        grad_w_exp_out,
        grad_b_out,
    )


def solution(mesh):
    tokens = P(("rep", "exp"), None)
    placed = (
        tokens,
        P(None, ("rep", "exp"), None),
        P(None, ("rep", "exp"), None, "mdl"),
        P(None, "mdl", ("rep", "exp")),
        P(None, ("rep", "exp"), None),
        P(None, None, ("rep", "exp")),
        P(None, None, ("rep", "exp")),
        P(None, "exp", "rep", "mdl"),
        P(None, "exp", "mdl"),
        P(None, "exp", "mdl", "rep"),
        P(None, "exp", "rep"),
    )
    return jax.shard_map(
        on_device,
        mesh=mesh,
        in_specs=placed + (tokens,),
        out_specs=(tokens, tokens) + placed[2:],
        check_vma=False,
    )
```

```python
import jax
import jax.numpy as jnp
from jax import lax
from jax.experimental import pallas as pl
from jax.experimental.pallas import tpu as pltpu
from jax.sharding import PartitionSpec as P

HD = 64
SEQ = 197
EPSILON = 1e-06
F32 = jnp.float32
BF16 = jnp.bfloat16


def norm_rows(values, gain, shift):
    row_mean = jnp.mean(values, axis=-1, keepdims=True)
    centred = values - row_mean
    row_var = jnp.mean(centred * centred, axis=-1, keepdims=True)
    return centred * lax.rsqrt(row_var + EPSILON) * gain + shift


def dot(a, b):
    return jnp.dot(a, b, preferred_element_type=F32)


def dot_tn(a, b):
    return lax.dot_general(a, b, (((0,), (0,)), ((), ())), preferred_element_type=F32)


def dot_nt(a, b):
    return lax.dot_general(a, b, (((1,), (1,)), ((), ())), preferred_element_type=F32)


def other_core(values):
    return lax.ppermute(values, "rep", [(0, 1), (1, 0)])


def in_order(own, other, axis):
    first = lax.axis_index("rep") == 0
    return jnp.concatenate(
        [jnp.where(first, own, other), jnp.where(first, other, own)], axis=axis
    )


MESH = pl.DeviceIdType.MESH
BLOCK = 16
VMEM_SPEC = pl.BlockSpec(memory_space=pltpu.VMEM)
ANY_SPEC = pl.BlockSpec(memory_space=pl.ANY)
SMALL = 128
NEAR = 8
FAR = 4


def chip_place():
    rep = lax.axis_index("rep")
    exp = lax.axis_index("exp")
    near = (1 - rep) * (exp // 8 * 2 + exp // 4 % 2) + rep * (exp % 8)
    far = (1 - rep) * (exp % 4) + rep * (exp // 8)

    def chip_of(near_idx, far_idx):
        return (1 - rep) * (near_idx // 2 * 8 + near_idx % 2 * 4 + far_idx) + rep * (
            far_idx * 8 + near_idx
        )

    return rep, exp, near, far, chip_of


def greet(near, far, chip_of, rep):
    barrier = pltpu.get_barrier_semaphore()
    for step in range(1, NEAR):
        peer = chip_of((near + step) % NEAR, far)
        pl.semaphore_signal(barrier, inc=1, device_id={"exp": peer}, device_id_type=MESH)
    for step in range(1, FAR):
        peer = chip_of(near, (far + step) % FAR)
        pl.semaphore_signal(barrier, inc=1, device_id={"exp": peer}, device_id_type=MESH)
    pl.semaphore_signal(barrier, inc=1, device_id={"rep": 1 - rep}, device_id_type=MESH)
    return barrier


GREETED = NEAR + FAR - 1


def gather_kernel(
    w_qkv,
    w_out,
    router,
    gains,
    shifts,
    whole0,
    later,
    spread,
    mine,
    filled,
    vectors,
    own_sem,
    near_send,
    near_recv,
    far_send,
    far_recv,
    core_send,
    core_recv,
):
    rep, exp, near, far, chip_of = chip_place()
    wholes = (whole0,)

    def near_copy(layer, step, slot):
        return pltpu.make_async_remote_copy(
            src_ref=mine.at[layer],
            dst_ref=wholes[layer].at[rep, exp],
            send_sem=near_send.at[layer, step],
            recv_sem=near_recv.at[layer, slot],
            device_id={"exp": chip_of((near + step) % NEAR, far)},
            device_id_type=MESH,
        )

    def far_copy(layer, step, source, slot_near, slot_far):
        return pltpu.make_async_remote_copy(
            src_ref=wholes[layer].at[rep, source],
            dst_ref=wholes[layer].at[rep, source],
            send_sem=far_send.at[layer, step, slot_near],
            recv_sem=far_recv.at[layer, slot_far, slot_near],
            device_id={"exp": chip_of(near, (far + step) % FAR)},
            device_id_type=MESH,
        )

    def core_copy(layer, source, part):
        return pltpu.make_async_remote_copy(
            src_ref=wholes[layer].at[part, source],
            dst_ref=wholes[layer].at[part, source],
            send_sem=core_send.at[layer, source],
            recv_sem=core_recv.at[layer, source],
            device_id={"rep": 1 - rep},
            device_id_type=MESH,
        )

    keeps = [
        pltpu.make_async_copy(mine.at[layer], wholes[layer].at[rep, exp], own_sem.at[layer])
        for layer in range(1)
    ]
    barrier = greet(near, far, chip_of, rep)
    layers, own_rows, parts, part_cols = w_qkv.shape
    qkv_cols = parts * part_cols
    cut = qkv_cols + w_out.shape[1]
    experts = router.shape[2]
    turn = (
        lax.broadcasted_iota(jnp.int32, (BLOCK, own_rows), 0)
        == lax.broadcasted_iota(jnp.int32, (BLOCK, own_rows), 1)
    )
    turn = jnp.where(turn, 1.0, 0.0).astype(BF16)
    filled[...] = jnp.zeros_like(filled)
    vectors[...] = jnp.zeros_like(vectors)
    for layer in range(layers):
        for part in range(parts):
            filled[:own_rows, part * part_cols : (part + 1) * part_cols] = w_qkv[
                layer, :, part, :
            ].astype(F32)
        filled[:, qkv_cols:cut] = dot_nt(turn, w_out[layer])
        vectors[experts : experts + 2, :] = gains[layer].astype(F32)
        vectors[experts + 2 : experts + 5, :] = shifts[layer].astype(F32)
        filled[:, cut:] = dot_nt(turn, vectors[...].astype(BF16))
        filled[:own_rows, cut : cut + experts] = router[layer].astype(F32)
        if layer == 0:
            mine[layer] = filled[...].astype(BF16)
        else:
            later[...] = filled[...].astype(BF16)
    for keep in keeps:
        keep.start()
    pl.semaphore_wait(barrier, GREETED)
    for layer in range(1):

        @pl.loop(1, NEAR)
        def _(step):
            near_copy(layer, step, near).start()

    row = lax.broadcasted_iota(jnp.int32, spread.shape, 0)
    col = lax.broadcasted_iota(jnp.int32, spread.shape, 1)
    inside = row & (BLOCK - 1)
    true_row = (row >> 4) * own_rows + inside
    spread[...] = jnp.where((inside < own_rows) & (true_row == col), 1.0, 0.0).astype(BF16)
    for keep in keeps:
        keep.wait()
    for layer in range(1):

        @pl.loop(0, NEAR)
        def _(back):
            slot = (near - back + NEAR) % NEAR
            source = chip_of(slot, far)

            @pl.when(back > 0)
            def _():
                near_copy(layer, back, slot).wait_recv()

            @pl.loop(1, FAR)
            def _(step):
                far_copy(layer, step, source, slot, far).start()

            core_copy(layer, source, rep).start()

    for layer in range(1):

        @pl.loop(0, NEAR)
        def _(back):
            slot = (near - back + NEAR) % NEAR

            @pl.loop(1, FAR)
            def _(step):
                slot_far = (far - step + FAR) % FAR
                source = chip_of(slot, slot_far)
                far_copy(layer, step, source, slot, slot_far).wait_recv()
                core_copy(layer, source, rep).start()

    for layer in range(1):

        @pl.loop(0, NEAR * FAR)
        def _(source):
            core_copy(layer, source, 1 - rep).wait_recv()
            core_copy(layer, source, rep).wait_send()

        @pl.loop(1, NEAR)
        def _(step):
            near_copy(layer, step, near).wait_send()

        @pl.loop(1, FAR)
        def _(step):
            @pl.loop(0, NEAR)
            def _(slot):
                far_copy(layer, step, chip_of(slot, far), slot, far).wait_send()


def gather_weights(w_qkv, w_out, router, gains, shifts):
    layers, own_rows, parts, part_cols = w_qkv.shape
    cols = parts * part_cols + w_out.shape[1] + SMALL
    devices = 2 * NEAR * FAR
    whole = jax.ShapeDtypeStruct((2, NEAR * FAR, BLOCK, cols), BF16)
    got = pl.pallas_call(
        gather_kernel,
        out_shape=(
            whole,
            jax.ShapeDtypeStruct((BLOCK, cols), BF16),
            jax.ShapeDtypeStruct((devices * BLOCK, devices * own_rows), BF16),
        ),
        in_specs=[VMEM_SPEC] * 5,
        out_specs=(ANY_SPEC, VMEM_SPEC, VMEM_SPEC),
        scratch_shapes=[
            pltpu.VMEM((1, BLOCK, cols), BF16),
            pltpu.VMEM((BLOCK, cols), F32),
            pltpu.VMEM((SMALL, own_rows), F32),
            pltpu.SemaphoreType.DMA((1,)),
            pltpu.SemaphoreType.DMA((1, NEAR)),
            pltpu.SemaphoreType.DMA((1, NEAR)),
            pltpu.SemaphoreType.DMA((1, FAR, NEAR)),
            pltpu.SemaphoreType.DMA((1, FAR, NEAR)),
            pltpu.SemaphoreType.DMA((1, NEAR * FAR)),
            pltpu.SemaphoreType.DMA((1, NEAR * FAR)),
        ],
        compiler_params=pltpu.CompilerParams(
            collective_id=0, has_side_effects=True, vmem_limit_bytes=60 << 20
        ),
        name="gather_weights",
    )(w_qkv, w_out, router, gains, shifts)
    return got[0].reshape(devices * BLOCK, cols), got[1], got[2]


def scatter_kernel(*refs):
    per_layer = [refs[:7]]
    done = refs[7]
    spread = refs[8]
    biases = refs[9:13]
    experts = refs[13:17]
    out_qkv, out_rest, out_b_in, out_b_out, out_in, out_exp = refs[17:23]
    (
        lhs_qkv,
        lhs_proj,
        lhs_small,
        sums,
        part,
        from_core,
        from_far,
        total,
        from_near,
        stage_in,
        stage_exp,
        stage_sems,
        core_send,
        core_recv,
        far_send,
        far_recv,
        near_send,
        near_recv,
    ) = refs[23:]
    rep, exp, near, far, chip_of = chip_place()
    qkv_cols, proj_cols = per_layer[0][3].shape[1], per_layer[0][4].shape[1]
    cut = qkv_cols + proj_cols
    rows = BLOCK * 8
    chunks = NEAR * FAR // 8
    loads, stores = [], []
    for layer in range(2):
        for kind, (stage, out) in enumerate(((stage_in, out_in), (stage_exp, out_exp))):
            idx = 2 * layer + kind
            loads.append(
                pltpu.make_async_copy(experts[idx], stage.at[layer], stage_sems.at[idx])
            )
            stores.append(
                pltpu.make_async_copy(stage.at[layer], out.at[layer, 0], stage_sems.at[idx])
            )
    for load in loads:
        load.start()

    def multiply(layer, core, chunk):
        rhs_qkv, rhs_proj, rhs_small = per_layer[layer][3:6]
        at = pl.ds(pl.multiple_of((core * chunks + chunk) * rows, rows), rows)
        to = pl.ds(pl.multiple_of(chunk * rows, rows), rows)
        part[layer, core, to, :qkv_cols] = dot(lhs_qkv[at, :], rhs_qkv[...]).astype(BF16)
        part[layer, core, to, qkv_cols:cut] = dot(lhs_proj[at, :], rhs_proj[...]).astype(BF16)
        part[layer, core, to, cut:] = (
            dot(lhs_small[at, :], rhs_small[...]) + sums[at, :]
        ).astype(BF16)

    def core_copy(layer, chunk):
        to = pl.ds(pl.multiple_of(chunk * rows, rows), rows)
        return pltpu.make_async_remote_copy(
            src_ref=part.at[layer, 1 - rep, to],
            dst_ref=from_core.at[layer, to],
            send_sem=core_send.at[layer, chunk],
            recv_sem=core_recv.at[layer, chunk],
            device_id={"rep": 1 - rep},
            device_id_type=MESH,
        )

    def far_copy(layer, step, slot):
        return pltpu.make_async_remote_copy(
            src_ref=part.at[layer, rep, block(chip_of(slot, (far + step) % FAR))],
            dst_ref=from_far.at[layer, step, block(slot)],
            send_sem=far_send.at[layer, step, slot],
            recv_sem=far_recv.at[layer, step, slot],
            device_id={"exp": chip_of(near, (far + step) % FAR)},
            device_id_type=MESH,
        )

    def near_copy(layer, step):
        return pltpu.make_async_remote_copy(
            src_ref=total.at[layer, block((near + step) % NEAR)],
            dst_ref=from_near.at[layer, step],
            send_sem=near_send.at[layer, step],
            recv_sem=near_recv.at[layer, step],
            device_id={"exp": chip_of((near + step) % NEAR, far)},
            device_id_type=MESH,
        )

    barrier = greet(near, far, chip_of, rep)
    for layer in range(1):
        h_one, grad_att, h_two = per_layer[layer][:3]
        lhs_qkv[...] = dot_nt(spread[...], h_one[...]).astype(BF16)
        lhs_proj[...] = dot_nt(spread[...], grad_att[...]).astype(BF16)
        lhs_small[...] = dot_nt(spread[...], h_two[...]).astype(BF16)
        sums[...] = dot_nt(spread[...], per_layer[layer][6][...].astype(BF16))
        if layer == 0:
            pl.semaphore_wait(barrier, GREETED)

        @pl.loop(0, chunks)
        def _(chunk):
            multiply(layer, 1 - rep, chunk)
            core_copy(layer, chunk).start()

        @pl.loop(0, chunks)
        def _(chunk):
            multiply(layer, rep, chunk)

    for layer in range(1):

        @pl.loop(0, chunks)
        def _(chunk):
            to = pl.ds(pl.multiple_of(chunk * rows, rows), rows)
            core_copy(layer, chunk).wait_recv()
            part[layer, rep, to, :] = (
                part[layer, rep, to, :].astype(F32) + from_core[layer, to, :].astype(F32)
            ).astype(BF16)

        @pl.loop(1, NEAR + 1)
        def _(ahead):
            @pl.loop(1, FAR)
            def _(step):
                far_copy(layer, step, (near + ahead) % NEAR).start()

    for load in loads:
        load.wait()
    for store in stores:
        store.start()
    for layer in range(2):
        out_b_in[layer] = biases[2 * layer][...]
        out_b_out[layer] = biases[2 * layer + 1][...]

    def add_far(layer, slot):
        for step in range(1, FAR):
            far_copy(layer, step, slot).wait_recv()
        value = part[layer, rep, block(chip_of(slot, far)), :].astype(F32)
        for step in range(1, FAR):
            value = value + from_far[layer, step, block(slot), :].astype(F32)
        return value

    for layer in range(1):

        @pl.loop(1, NEAR)
        def _(step):
            slot = (near + step) % NEAR
            total[layer, block(slot), :] = add_far(layer, slot).astype(BF16)
            near_copy(layer, step).start()

    own_rows = out_qkv.shape[1]
    part_cols = qkv_cols // 3
    for layer in range(2):
        if layer == 0:
            value = add_far(layer, near)
            for step in range(1, NEAR):
                near_copy(layer, step).wait_recv()
                value = value + from_near[layer, step].astype(F32)
        else:
            value = done[...]
        for idx in range(3):
            out_qkv[layer, :, idx, :] = value[:own_rows, idx * part_cols : (idx + 1) * part_cols]
        out_rest[layer] = value[:, qkv_cols:]

    for layer in range(1):

        @pl.loop(1, NEAR)
        def _(step):
            near_copy(layer, step).wait_send()

        @pl.loop(1, FAR)
        def _(step):
            @pl.loop(0, NEAR)
            def _(slot):
                far_copy(layer, step, slot).wait_send()

        @pl.loop(0, chunks)
        def _(chunk):
            core_copy(layer, chunk).wait_send()

    for store in stores:
        store.wait()


def scatter_grads(attn, done, spread, experts, own_rows):
    tokens = attn[0].shape[0]
    qkv_cols, proj_cols = attn[3].shape[1], attn[4].shape[1]
    cols = qkv_cols + proj_cols + SMALL
    half = NEAR * FAR * BLOCK
    grad_in, grad_exp, grad_b_in, grad_b_out = experts[0]
    shape = jax.ShapeDtypeStruct
    chunks = NEAR * FAR // 8
    return pl.pallas_call(
        scatter_kernel,
        out_shape=(
            shape((2, own_rows, 3, qkv_cols // 3), F32),
            shape((2, BLOCK, proj_cols + SMALL), F32),
            shape((2,) + grad_b_in.shape, F32),
            shape((2,) + grad_b_out.shape, F32),
            shape((2, 1) + grad_in.shape, F32),
            shape((2, 1) + grad_exp.shape, F32),
        ),
        in_specs=[VMEM_SPEC] * 13 + [ANY_SPEC] * 4,
        out_specs=tuple([VMEM_SPEC] * 4 + [ANY_SPEC] * 2),
        scratch_shapes=[
            pltpu.VMEM((2 * half, tokens), BF16),
            pltpu.VMEM((2 * half, tokens), BF16),
            pltpu.VMEM((2 * half, tokens), BF16),
            pltpu.VMEM((2 * half, SMALL), F32),
            pltpu.VMEM((1, 2, half, cols), BF16),
            pltpu.VMEM((1, half, cols), BF16),
            pltpu.VMEM((1, FAR, NEAR * BLOCK, cols), BF16),
            pltpu.VMEM((1, NEAR * BLOCK, cols), BF16),
            pltpu.VMEM((1, NEAR, BLOCK, cols), BF16),
            pltpu.VMEM((2,) + grad_in.shape, F32),
            pltpu.VMEM((2,) + grad_exp.shape, F32),
            pltpu.SemaphoreType.DMA((4,)),
            pltpu.SemaphoreType.DMA((2, chunks)),
            pltpu.SemaphoreType.DMA((2, chunks)),
            pltpu.SemaphoreType.DMA((2, FAR, NEAR)),
            pltpu.SemaphoreType.DMA((2, FAR, NEAR)),
            pltpu.SemaphoreType.DMA((2, NEAR)),
            pltpu.SemaphoreType.DMA((2, NEAR)),
        ],
        compiler_params=pltpu.CompilerParams(
            collective_id=1, has_side_effects=True, vmem_limit_bytes=60 << 20
        ),
        name="scatter_grads",
    )(
        *attn,
        done,
        spread,
        *(value for parts in experts for value in parts[2:]),
        *(value for parts in experts for value in parts[:2]),
    )


PLANES = 4
PLANE = 8


def block(source):
    return pl.ds(pl.multiple_of(source * BLOCK, BLOCK), BLOCK)


def plane_rows(plane):
    return pl.ds(pl.multiple_of(plane * (PLANE * BLOCK), PLANE * BLOCK), PLANE * BLOCK)


def plane_step(turn):
    return turn + turn // 2 - 2 * (turn // 3)


def greet_all(exp):
    barrier = pltpu.get_barrier_semaphore()

    @pl.loop(1, PLANES * PLANE)
    def _(step):
        peer = (exp + step) % (PLANES * PLANE)
        pl.semaphore_signal(barrier, inc=1, device_id={"exp": peer}, device_id_type=MESH)

    mdl = lax.axis_index("mdl")
    pl.semaphore_signal(barrier, inc=1, device_id={"mdl": 1 - mdl}, device_id_type=MESH)
    return barrier


def core_send_copy(src, dst, sems, idx):
    return pltpu.make_async_remote_copy(
        src_ref=src,
        dst_ref=dst,
        send_sem=sems.at[idx, 0],
        recv_sem=sems.at[idx, 1],
        device_id={"rep": 1 - lax.axis_index("rep")},
        device_id_type=MESH,
    )


def half_copy(src, dst, sems, idx):
    return pltpu.make_async_remote_copy(
        src_ref=src,
        dst_ref=dst,
        send_sem=sems.at[idx, 0],
        recv_sem=sems.at[idx, 1],
        device_id={"mdl": 1 - lax.axis_index("mdl")},
        device_id_type=MESH,
    )


def row_copy(src, dst, exp, send_sem, recv_sem, peer, source):
    return pltpu.make_async_remote_copy(
        src_ref=src.at[block(peer)],
        dst_ref=dst.at[block(exp)],
        send_sem=send_sem.at[peer],
        recv_sem=recv_sem.at[source],
        device_id={"exp": peer},
        device_id_type=MESH,
    )


def send_all(src, dst, exp, send_sem, recv_sem):
    @pl.loop(0, PLANES)
    def _(turn):
        plane = (exp // PLANE + plane_step(turn)) % PLANES

        @pl.loop(0, PLANE)
        def _(step):
            peer = plane * PLANE + (exp + step) % PLANE

            @pl.when(turn + step > 0)
            def _():
                row_copy(src, dst, exp, send_sem, recv_sem, peer, exp).start()

    dst[block(exp), :] = src[block(exp), :]


def each_plane(src, back_src, dst, back_dst, exp, sems, work):
    send_sem, recv_sem, back_send, back_recv = sems

    @pl.loop(0, PLANES)
    def _(turn):
        plane = (exp // PLANE - plane_step(turn) + PLANES) % PLANES

        @pl.loop(0, PLANE)
        def _(step):
            source = plane * PLANE + (exp - step + PLANE) % PLANE

            @pl.when(turn + step > 0)
            def _():
                row_copy(src, dst, exp, send_sem, recv_sem, source, source).wait_recv()

        work(plane_rows(plane))

        @pl.loop(0, PLANE)
        def _(step):
            source = plane * PLANE + (exp - step + PLANE) % PLANE

            @pl.when(turn + step > 0)
            def _():
                row_copy(back_src, back_dst, exp, back_send, back_recv, source, exp).start()

    back_dst[block(exp), :] = back_src[block(exp), :]


def wait_back(back_src, back_dst, exp, sems):
    @pl.loop(1, PLANES * PLANE)
    def _(step):
        source = (exp + step) % (PLANES * PLANE)
        row_copy(back_src, back_dst, exp, sems[2], sems[3], source, source).wait_recv()


def wait_sent(src, dst, back_src, back_dst, exp, sems):
    @pl.loop(1, PLANES * PLANE)
    def _(step):
        peer = (exp + step) % (PLANES * PLANE)
        row_copy(src, dst, exp, sems[0], sems[1], peer, peer).wait_send()
        row_copy(back_src, back_dst, exp, sems[2], sems[3], peer, peer).wait_send()


def weight_loads(own_in, other_in, own_out, other_out, w_in, w_out):
    rep = lax.axis_index("rep")
    depth = own_in.shape[0]
    pairs = []
    for src_in, src_out, core in ((own_in, own_out, rep), (other_in, other_out, 1 - rep)):
        place = pl.ds(pl.multiple_of(core * depth, 128), depth)
        pairs.append((src_in, w_in.at[place, :]))
        pairs.append((src_out, w_out.at[:, place]))
    return pairs


def lanes(values):
    rows = values[0].shape[0]
    lane = lax.broadcasted_iota(jnp.int32, (rows, 128), 1)
    total = jnp.zeros((rows, 128), F32)
    for idx, value in enumerate(values):
        total = jnp.where(lane == idx, value, total)
    return total


def row_sems():
    return [pltpu.SemaphoreType.DMA((PLANES * PLANE,))] * 4


def head_slices(head, width):
    start = head * HD
    return [slice(part * width + start, part * width + start + HD) for part in range(3)]


def masked_scores(query_rows, key_rows):
    scores = dot_nt(query_rows, key_rows) * HD ** (-0.5)
    col = lax.broadcasted_iota(jnp.int32, scores.shape, 1)
    return jnp.where(col < SEQ, scores, -1e30)


def route(ids, hot0, hot1, pick0, pick1):
    tokens, slots = pick0.shape
    lane = lax.broadcasted_iota(jnp.int32, (tokens, 128), 1)
    hots = [jnp.where(ids[:, k : k + 1] == lane, 1.0, 0.0) for k in range(2)]
    hot0[...], hot1[...] = hots[0].astype(BF16), hots[1].astype(BF16)
    row = lax.broadcasted_iota(jnp.int32, (tokens, tokens), 0)
    col = lax.broadcasted_iota(jnp.int32, (tokens, tokens), 1)
    before = jnp.where(row > col, 1.0, 0.0).astype(BF16)
    earlier = dot(before, (hots[0] + hots[1]).astype(BF16))
    place = lax.broadcasted_iota(jnp.int32, (tokens, slots), 1).astype(F32)
    for k, pick in enumerate((pick0, pick1)):
        within = jnp.sum(earlier * hots[k], axis=1, keepdims=True)
        slot = ids[:, k : k + 1].astype(F32) * BLOCK + within
        pick[...] = jnp.where(slot == place, 1.0, 0.0).astype(BF16)


def attend_forward(qkv, heads, log_total):
    width = heads.shape[1]
    totals = []
    for head in range(width // HD):
        q_at, k_at, v_at = head_slices(head, width)
        scores = masked_scores(qkv[:, q_at], qkv[:, k_at])
        top_score = jnp.max(scores, axis=-1, keepdims=True)
        raw_weight = jnp.exp(scores - top_score)
        row_total = jnp.sum(raw_weight, axis=-1, keepdims=True)
        probs_low = (raw_weight / row_total).astype(BF16)
        totals.append(top_score + jnp.log(row_total))
        heads[:, q_at] = dot(probs_low, qkv[:, v_at]).astype(BF16)
    log_total[...] = lanes(totals)


def attend_backward(grad_heads, qkv, log_total, grad_qkv):
    width = grad_heads.shape[1]
    for head in range(width // HD):
        q_at, k_at, v_at = head_slices(head, width)
        query_rows, key_rows, value_rows = qkv[:, q_at], qkv[:, k_at], qkv[:, v_at]
        grad_out = grad_heads[:, q_at]
        probs = jnp.exp(masked_scores(query_rows, key_rows) - log_total[:, head : head + 1])
        grad_probs = dot_nt(grad_out, value_rows)
        grad_scores = probs * (grad_probs - jnp.sum(grad_probs * probs, axis=-1, keepdims=True))
        grad_scores = grad_scores.astype(BF16)
        grad_qkv[:, q_at] = (dot(grad_scores, key_rows) * HD ** (-0.5)).astype(BF16)
        grad_qkv[:, k_at] = (dot_tn(grad_scores, query_rows) * HD ** (-0.5)).astype(BF16)
        grad_qkv[:, v_at] = dot_tn(probs.astype(BF16), grad_out).astype(BF16)


def block_forward_kernel(
    state,
    spread,
    ids,
    b_in,
    b_out,
    whole_in,
    own_in,
    other_in,
    own_out,
    other_out,
    after_out,
    h_out,
    gates_out,
    picked0_out,
    picked1_out,
    next_out,
    h_one_out,
    qkv_out,
    log_out,
    heads_out,
    rows_out,
    slope_out,
    active_out,
    hot0,
    hot1,
    pick0,
    pick1,
    whole,
    w_in,
    w_out,
    send,
    rows,
    slope,
    active,
    back_src,
    back,
    own_att,
    low_att,
    own_moe,
    low_moe,
    load_sems,
    out_sems,
    half_sems,
    send_sem,
    recv_sem,
    back_send,
    back_recv,
    extra=None,
):
    exp = lax.axis_index("exp")
    sems = (send_sem, recv_sem, back_send, back_recv)
    loads = [
        pltpu.make_async_copy(src, dst, load_sems.at[idx])
        for idx, (src, dst) in enumerate(
            [(whole_in, whole)]
            + weight_loads(own_in, other_in, own_out, other_out, w_in, w_out)
        )
    ]
    for load in loads:
        load.start()
    barrier = greet_all(exp)
    if extra:
        extra.greet(barrier)
    qkv_cols = qkv_out.shape[1]
    cut = qkv_cols + heads_out.shape[1]
    loads[0].wait()
    small = dot_tn(whole[:, cut:], spread[...])
    first_row = PLANES * PLANE
    gain0, gain1, shift0, shift1, shift2 = [
        small[first_row + idx : first_row + idx + 1, :] for idx in range(5)
    ]
    h_one = norm_rows(state[...], gain0, shift0).astype(BF16)
    h_one_out[...] = h_one
    wide = dot_nt(h_one, spread[...]).astype(BF16)
    qkv_out[...] = dot(wide, whole[:, :qkv_cols]).astype(BF16)
    if extra:
        pl.semaphore_wait(barrier, PLANES * PLANE + 1)
        extra.send()
    attend_forward(qkv_out, heads_out, log_out)
    route(ids, hot0, hot1, pick0, pick1)
    own_att[...] = dot(
        dot_nt(heads_out[...], whole[:, qkv_cols:cut]).astype(BF16), spread[...]
    ).astype(BF16)
    if not extra:
        pl.semaphore_wait(barrier, PLANES * PLANE)
    first = half_copy(own_att, low_att, half_sems, 0)
    first.start()
    first.wait_recv()
    after = state[...] + (own_att[...].astype(F32) + low_att[...].astype(F32)) + shift2
    after_out[...] = after
    h_two = norm_rows(after, gain1, shift1).astype(BF16)
    h_out[...] = h_two
    send[...] = dot_tn(pick0[...] + pick1[...], h_two).astype(BF16)
    send_all(send, rows, exp, send_sem, recv_sem)
    logits = dot_nt(h_two, small.astype(BF16))
    chosen = [jnp.sum(logits * hot[...].astype(F32), axis=1, keepdims=True) for hot in (hot0, hot1)]
    top = jnp.maximum(chosen[0], chosen[1])
    raw = [jnp.exp(value - top) for value in chosen]
    gates = [value / (raw[0] + raw[1]) for value in raw]
    gates_out[...] = lanes(gates)
    bias_in = b_in[...].astype(F32)
    for load in loads[1:]:
        load.wait()
    tile = 512

    def work(at):
        for col in range(0, active.shape[1], tile):
            cols = slice(col, col + tile)
            inner = dot(rows[at, :], w_in[:, cols]) + bias_in[:, cols]
            cdf = 0.5 * (1.0 + lax.erf(inner * (0.5**0.5)))
            active[at, cols] = (inner * cdf).astype(BF16)
            slope[at, cols] = (
                cdf + inner * jnp.exp(-0.5 * inner * inner) * 0.3989422804014327
            ).astype(BF16)
        back_src[at, :] = (dot(active[at, :], w_out[...]) + b_out[...]).astype(BF16)

    each_plane(send, back_src, rows, back, exp, sems, work)
    saves = [
        pltpu.make_async_copy(src, dst, out_sems.at[idx])
        for idx, (src, dst) in enumerate(
            ((rows, rows_out), (slope, slope_out), (active, active_out))
        )
    ]
    for save in saves:
        save.start()
    wait_back(back_src, back, exp, sems)
    picked = [dot(pick[...], back[...]) for pick in (pick0, pick1)]
    own_moe[...] = (gates[0] * picked[0] + gates[1] * picked[1]).astype(BF16)
    second = half_copy(own_moe, low_moe, half_sems, 1)
    second.start()
    picked0_out[...] = picked[0].astype(BF16)
    picked1_out[...] = picked[1].astype(BF16)
    if extra:
        extra.forward()
    wait_sent(send, rows, back_src, back, exp, sems)
    second.wait_recv()
    next_out[...] = after_out[...] + (own_moe[...].astype(F32) + low_moe[...].astype(F32))
    first.wait_send()
    second.wait_send()
    for save in saves:
        save.wait()
    if extra:
        extra.finish()


class SpreadRows:
    def __init__(self, mine, whole, own_sem, send_sem, recv_sem, core_sems):
        self.rep, self.exp = lax.axis_index("rep"), lax.axis_index("exp")
        self.mine, self.whole = mine, whole
        self.send_sem, self.recv_sem = send_sem, recv_sem
        self.keep = pltpu.make_async_copy(mine, whole.at[self.rep, self.exp], own_sem)
        self.core = core_send_copy(whole.at[self.rep], whole.at[self.rep], core_sems, 0)

    def copy(self, peer, source):
        return pltpu.make_async_remote_copy(
            src_ref=self.mine,
            dst_ref=self.whole.at[self.rep, self.exp],
            send_sem=self.send_sem.at[peer],
            recv_sem=self.recv_sem.at[source],
            device_id={"exp": peer},
            device_id_type=MESH,
        )

    def greet(self, barrier):
        pl.semaphore_signal(
            barrier, inc=1, device_id={"rep": 1 - self.rep}, device_id_type=MESH
        )

    def send(self):
        self.keep.start()

        @pl.loop(1, PLANES * PLANE)
        def _(step):
            self.copy((self.exp + step) % (PLANES * PLANE), self.exp).start()

    def forward(self):
        @pl.loop(1, PLANES * PLANE)
        def _(step):
            source = (self.exp + step) % (PLANES * PLANE)
            self.copy(source, source).wait_recv()

        self.keep.wait()
        self.core.start()

    def finish(self):
        self.core.wait()

        @pl.loop(1, PLANES * PLANE)
        def _(step):
            peer = (self.exp + step) % (PLANES * PLANE)
            self.copy(peer, peer).wait_send()


def first_forward_kernel(*refs):
    inputs, outputs, scratch = refs[:11], refs[11:25], refs[25:]
    extra = SpreadRows(inputs[10], outputs[13], *scratch[-4:])
    block_forward_kernel(*inputs[:10], *outputs[:13], *scratch[:-4], extra=extra)


def block_forward(near, whole, weights, mine=None):
    more = mine is not None
    tokens, width = near[0].shape
    slots = BLOCK * PLANES * PLANE
    hidden = weights[0].shape[1]
    cols = whole.shape[1]
    proj = (cols - SMALL) // 4
    shape = jax.ShapeDtypeStruct
    return pl.pallas_call(
        first_forward_kernel if more else block_forward_kernel,
        out_shape=(
            shape((tokens, width), F32),
            shape((tokens, width), BF16),
            shape((tokens, 128), F32),
            shape((tokens, width), BF16),
            shape((tokens, width), BF16),
            shape((tokens, width), F32),
            shape((tokens, width), BF16),
            shape((tokens, 3 * proj), BF16),
            shape((tokens, 128), F32),
            shape((tokens, proj), BF16),
            shape((slots, width), BF16),
            shape((slots, hidden), BF16),
            shape((slots, hidden), BF16),
        )
        + ((shape((2, PLANES * PLANE, BLOCK, cols), BF16),) if more else ()),
        in_specs=[VMEM_SPEC] * 5 + [ANY_SPEC] * (6 if more else 5),
        out_specs=tuple([VMEM_SPEC] * 10 + [ANY_SPEC] * (4 if more else 3)),
        scratch_shapes=[
            pltpu.VMEM((tokens, 128), BF16),
            pltpu.VMEM((tokens, 128), BF16),
            pltpu.VMEM((tokens, slots), BF16),
            pltpu.VMEM((tokens, slots), BF16),
            pltpu.VMEM(whole.shape, BF16),
            pltpu.VMEM((width, hidden), BF16),
            pltpu.VMEM((hidden, width), BF16),
            pltpu.VMEM((slots, width), BF16),
            pltpu.VMEM((slots, width), BF16),
            pltpu.VMEM((slots, hidden), BF16),
            pltpu.VMEM((slots, hidden), BF16),
            pltpu.VMEM((slots, width), BF16),
            pltpu.VMEM((slots, width), BF16),
        ]
        + [pltpu.VMEM((tokens, width), BF16)] * 4
        + [
            pltpu.SemaphoreType.DMA((5,)),
            pltpu.SemaphoreType.DMA((3,)),
            pltpu.SemaphoreType.DMA((2, 2)),
        ]
        + row_sems()
        + (
            [pltpu.SemaphoreType.DMA(())] + row_sems()[:2] + [pltpu.SemaphoreType.DMA((1, 2))]
            if more
            else []
        ),
        compiler_params=pltpu.CompilerParams(
            collective_id=4 if more else 2, has_side_effects=True, vmem_limit_bytes=60 << 20
        ),
        name="first_forward" if more else "block_forward",
    )(*near, whole, *weights, *([mine] if more else []))


def norm_parts(values):
    row_mean = jnp.mean(values, axis=-1, keepdims=True)
    centred = values - row_mean
    row_var = jnp.mean(centred * centred, axis=-1, keepdims=True)
    scale = lax.rsqrt(row_var + EPSILON)
    return centred * scale, scale


def norm_grad(grad, unit, scale, gain):
    scaled = grad * gain
    return scale * (
        scaled
        - jnp.mean(scaled, axis=-1, keepdims=True)
        - unit * jnp.mean(scaled * unit, axis=-1, keepdims=True)
    )


def block_backward_kernel(
    grad_state,
    spread,
    ids,
    gates,
    picked0,
    picked1,
    after,
    state_in,
    qkv,
    log_total,
    heads,
    whole_in,
    own_in,
    other_in,
    own_out,
    other_out,
    slope_in,
    active_in,
    rows_in,
    grad_out,
    grad_att_out,
    grad_logits_out,
    sums_out,
    grad_qkv_out,
    grad_in_out,
    grad_exp_out,
    grad_b_in_out,
    grad_b_out_out,
    hot0,
    hot1,
    pick0,
    pick1,
    whole,
    w_in,
    w_out,
    slope,
    active,
    kept_rows,
    send,
    rows,
    inner,
    back_src,
    back,
    own_gate,
    low_gate,
    own_h,
    low_h,
    own_one,
    low_one,
    product,
    in_away,
    in_got,
    exp_away,
    exp_got,
    bias_own,
    bias_got,
    grad_heads,
    load_sems,
    half_sems,
    core_sems,
    send_sem,
    recv_sem,
    back_send,
    back_recv,
    extra=None,
):
    exp = lax.axis_index("exp")
    rep = lax.axis_index("rep")
    sems = (send_sem, recv_sem, back_send, back_recv)
    loads = [
        pltpu.make_async_copy(src, dst, load_sems.at[idx])
        for idx, (src, dst) in enumerate(
            weight_loads(own_in, other_in, own_out, other_out, w_in, w_out)
            + [
                (slope_in, slope),
                (whole_in, whole),
                (active_in, active),
                (rows_in, kept_rows),
            ]
        )
    ]
    for load in loads:
        load.start()
    barrier = greet_all(exp)
    pl.semaphore_signal(barrier, inc=1, device_id={"rep": 1 - rep}, device_id_type=MESH)
    grad = grad_state[...]
    gate0, gate1 = gates[:, 0:1], gates[:, 1:2]
    route(ids, hot0, hot1, pick0, pick1)
    send[...] = (
        dot_tn(pick0[...], (gate0 * grad).astype(BF16))
        + dot_tn(pick1[...], (gate1 * grad).astype(BF16))
    ).astype(BF16)
    pl.semaphore_wait(barrier, PLANES * PLANE + 1)
    send_all(send, rows, exp, send_sem, recv_sem)
    own_gate[...] = lanes(
        [
            jnp.sum(grad * picked[...].astype(F32), axis=1, keepdims=True)
            for picked in (picked0, picked1)
        ]
    )
    first = half_copy(own_gate, low_gate, half_sems, 0)
    first.start()
    for load in loads:
        load.wait()
    qkv_cols = qkv.shape[1]
    cut = qkv_cols + heads.shape[1]
    small = dot_tn(whole[:, cut:], spread[...])
    first_row = PLANES * PLANE
    gain0, gain1 = [small[first_row + idx : first_row + idx + 1, :] for idx in range(2)]

    def work(at):
        grad_active = dot_nt(rows[at, :], w_out[...])
        inner[at, :] = (grad_active * slope[at, :].astype(F32)).astype(BF16)
        back_src[at, :] = dot_nt(inner[at, :], w_in[...]).astype(BF16)

    each_plane(send, back_src, rows, back, exp, sems, work)

    half = grad_in_out.shape[0]
    hidden = inner.shape[1]
    own_at = pl.ds(pl.multiple_of(rep * half, 128), half)
    other_at = pl.ds(pl.multiple_of((1 - rep) * half, 128), half)
    in_away[...] = dot_tn(kept_rows[:, other_at], inner[...]).astype(BF16)
    in_copy = core_send_copy(in_away, in_got, core_sems, 0)
    in_copy.start()
    tall = product.shape[0]
    for start in range(0, hidden, tall):
        part = slice(start, start + tall)
        product[...] = dot_tn(active[:, part], rows[...])
        grad_exp_out[part, :] = product[:, own_at]
        exp_away[part, :] = product[:, other_at].astype(BF16)
    exp_copy = core_send_copy(exp_away, exp_got, core_sems, 1)
    exp_copy.start()
    bias_own[...] = jnp.zeros_like(bias_own)
    bias_own[0:1, :hidden] = jnp.sum(inner[...].astype(F32), axis=0, keepdims=True)
    bias_own[0:1, hidden:] = jnp.sum(rows[...].astype(F32), axis=0, keepdims=True)
    bias_copy = core_send_copy(bias_own, bias_got, core_sems, 2)
    bias_copy.start()
    grad_in_out[...] = dot_tn(kept_rows[:, own_at], inner[...])

    if extra:
        extra.multiply(spread)
    first.wait_recv()
    total = own_gate[...] + low_gate[...]
    grad0, grad1 = total[:, 0:1], total[:, 1:2]
    mean = gate0 * grad0 + gate1 * grad1
    grad_logits = (
        gate0 * (grad0 - mean) * hot0[...].astype(F32)
        + gate1 * (grad1 - mean) * hot1[...].astype(F32)
    ).astype(BF16)
    grad_logits_out[...] = grad_logits
    from_router = dot(grad_logits, small.astype(BF16))
    unit, scale = norm_parts(after[...])
    wait_back(back_src, back, exp, sems)
    own_h[...] = dot(pick0[...] + pick1[...], back[...]).astype(BF16)
    second = half_copy(own_h, low_h, half_sems, 1)
    second.start()
    in_copy.wait_recv()
    grad_in_out[...] += in_got[...].astype(F32)
    exp_copy.wait_recv()
    grad_exp_out[...] += exp_got[...].astype(F32)
    bias_copy.wait()
    bias_own[...] += bias_got[...]
    grad_b_in_out[...] = bias_own[0:1, :hidden]
    grad_b_out_out[...] = bias_own[
        0:1, pl.ds(pl.multiple_of(hidden + rep * half, 128), half)
    ]
    if extra:
        extra.send()
    wait_sent(send, rows, back_src, back, exp, sems)
    second.wait_recv()
    grad_h = own_h[...].astype(F32) + low_h[...].astype(F32) + from_router
    grad_after = norm_grad(grad_h, unit, scale, gain1) + grad_state[...]
    grad_att = grad_after.astype(BF16)
    grad_att_out[...] = grad_att
    sums_out[...] = jnp.zeros_like(sums_out)
    put = lambda idx, value: sums_out.__setitem__(
        (slice(first_row + idx, first_row + idx + 1), slice(None)),
        jnp.sum(value, axis=0, keepdims=True),
    )
    put(1, grad_h * unit)
    put(3, grad_h)
    put(4, grad_after)
    wide = dot_nt(grad_att, spread[...]).astype(BF16)
    grad_heads[...] = dot(wide, whole[:, qkv_cols:cut]).astype(BF16)
    attend_backward(grad_heads, qkv, log_total, grad_qkv_out)
    own_one[...] = dot(
        dot_nt(grad_qkv_out[...], whole[:, :qkv_cols]).astype(BF16), spread[...]
    ).astype(BF16)
    third = half_copy(own_one, low_one, half_sems, 2)
    third.start()
    unit, scale = norm_parts(state_in[...])
    third.wait_recv()
    grad_one = own_one[...].astype(F32) + low_one[...].astype(F32)
    grad_out[...] = grad_after + norm_grad(grad_one, unit, scale, gain0)
    put(0, grad_one * unit)
    put(2, grad_one)
    for copy in (first, second, third, in_copy, exp_copy):
        copy.wait_send()
    if extra:
        extra.finish()


class SumRows:
    def __init__(
        self,
        inputs,
        out,
        lhs_qkv,
        lhs_proj,
        lhs_small,
        sums,
        part,
        from_core,
        from_all,
        core_sems,
        send_sem,
        recv_sem,
    ):
        self.rep, self.exp = lax.axis_index("rep"), lax.axis_index("exp")
        self.inputs, self.out = inputs, out
        self.lhs, self.sums = (lhs_qkv, lhs_proj, lhs_small), sums
        self.part, self.from_core, self.from_all = part, from_core, from_all
        self.send_sem, self.recv_sem = send_sem, recv_sem
        self.core = core_send_copy(part.at[1 - self.rep], from_core, core_sems, 0)

    def multiply(self, spread):
        rhs = self.inputs[3:6]
        qkv_cols, cut = rhs[0].shape[1], rhs[0].shape[1] + rhs[1].shape[1]
        for lhs, rows in zip(self.lhs, self.inputs[:3]):
            lhs[...] = dot_nt(spread[...], rows[...]).astype(BF16)
        self.sums[...] = dot_nt(spread[...], self.inputs[6][...].astype(BF16))
        half = self.from_core.shape[0]
        rows = BLOCK * 8
        chunks = half // rows
        for core in (1 - self.rep, self.rep):

            @pl.loop(0, chunks)
            def _(chunk):
                at = pl.ds(pl.multiple_of(core * half + chunk * rows, rows), rows)
                to = pl.ds(pl.multiple_of(chunk * rows, rows), rows)
                products = [dot(lhs[at, :], value[...]) for lhs, value in zip(self.lhs, rhs)]
                self.part[core, to, :qkv_cols] = products[0].astype(BF16)
                self.part[core, to, qkv_cols:cut] = products[1].astype(BF16)
                self.part[core, to, cut:] = (products[2] + self.sums[at, :]).astype(BF16)

            if core is not self.rep:
                self.core.start()

    def copy(self, peer, source):
        return pltpu.make_async_remote_copy(
            src_ref=self.part.at[self.rep, block(peer)],
            dst_ref=self.from_all.at[block(self.exp)],
            send_sem=self.send_sem.at[peer],
            recv_sem=self.recv_sem.at[source],
            device_id={"exp": peer},
            device_id_type=MESH,
        )

    def send(self):
        self.core.wait_recv()
        rows = BLOCK * 8

        @pl.loop(0, self.from_core.shape[0] // rows)
        def _(chunk):
            to = pl.ds(pl.multiple_of(chunk * rows, rows), rows)
            self.part[self.rep, to, :] = (
                self.part[self.rep, to, :].astype(F32) + self.from_core[to, :].astype(F32)
            ).astype(BF16)

        @pl.loop(1, PLANES * PLANE)
        def _(step):
            self.copy((self.exp + step) % (PLANES * PLANE), self.exp).start()

    def finish(self):
        self.from_all[block(self.exp), :] = self.part[self.rep, block(self.exp), :]

        @pl.loop(1, PLANES * PLANE)
        def _(step):
            source = (self.exp + step) % (PLANES * PLANE)
            self.copy(source, source).wait_recv()

        self.out[...] = jnp.zeros_like(self.out)

        @pl.loop(0, PLANES * PLANE)
        def _(source):
            self.out[...] += self.from_all[block(source), :].astype(F32)

        @pl.loop(1, PLANES * PLANE)
        def _(step):
            peer = (self.exp + step) % (PLANES * PLANE)
            self.copy(peer, peer).wait_send()

        self.core.wait_send()


def last_backward_kernel(*refs):
    inputs, outputs, scratch = refs[:26], refs[26:36], refs[36:]
    extra = SumRows(inputs[19:], outputs[9], *scratch[-10:])
    block_backward_kernel(*inputs[:19], *outputs[:9], *scratch[:-10], extra=extra)


def block_backward(near, whole, weights, kept, later=()):
    more = len(later) > 0
    tokens, width = near[0].shape
    slots = BLOCK * PLANES * PLANE
    hidden = weights[0].shape[1]
    cols = whole.shape[1]
    proj = (cols - SMALL) // 4
    half = width // 2
    shape = jax.ShapeDtypeStruct
    return pl.pallas_call(
        last_backward_kernel if more else block_backward_kernel,
        out_shape=(
            shape((tokens, width), F32),
            shape((tokens, width), BF16),
            shape((tokens, 128), BF16),
            shape((128, width), F32),
            shape((tokens, 3 * proj), BF16),
            shape((half, hidden), F32),
            shape((hidden, half), F32),
            shape((1, hidden), F32),
            shape((1, half), F32),
        )
        + ((shape((BLOCK, cols), F32),) if more else ()),
        in_specs=[VMEM_SPEC] * 11 + [ANY_SPEC] * 8 + [VMEM_SPEC] * len(later),
        out_specs=tuple([VMEM_SPEC] * (10 if more else 9)),
        scratch_shapes=[
            pltpu.VMEM((tokens, 128), BF16),
            pltpu.VMEM((tokens, 128), BF16),
            pltpu.VMEM((tokens, slots), BF16),
            pltpu.VMEM((tokens, slots), BF16),
            pltpu.VMEM(whole.shape, BF16),
            pltpu.VMEM((width, hidden), BF16),
            pltpu.VMEM((hidden, width), BF16),
            pltpu.VMEM((slots, hidden), BF16),
            pltpu.VMEM((slots, hidden), BF16),
            pltpu.VMEM((slots, width), BF16),
            pltpu.VMEM((slots, width), BF16),
            pltpu.VMEM((slots, width), BF16),
            pltpu.VMEM((slots, hidden), BF16),
            pltpu.VMEM((slots, width), BF16),
            pltpu.VMEM((slots, width), BF16),
            pltpu.VMEM((tokens, 128), F32),
            pltpu.VMEM((tokens, 128), F32),
        ]
        + [pltpu.VMEM((tokens, width), BF16)] * 4
        + [
            pltpu.VMEM((512, width), F32),
            pltpu.VMEM((half, hidden), BF16),
            pltpu.VMEM((half, hidden), BF16),
            pltpu.VMEM((hidden, half), BF16),
            pltpu.VMEM((hidden, half), BF16),
            pltpu.VMEM((8, hidden + width), F32),
            pltpu.VMEM((8, hidden + width), F32),
            pltpu.VMEM((tokens, proj), BF16),
            pltpu.SemaphoreType.DMA((8,)),
            pltpu.SemaphoreType.DMA((3, 2)),
            pltpu.SemaphoreType.DMA((3, 2)),
        ]
        + row_sems()
        + (
            [pltpu.VMEM((2 * slots, tokens), BF16)] * 3
            + [
                pltpu.VMEM((2 * slots, SMALL), F32),
                pltpu.VMEM((2, slots, cols), BF16),
                pltpu.VMEM((slots, cols), BF16),
                pltpu.VMEM((slots, cols), BF16),
                pltpu.SemaphoreType.DMA((1, 2)),
            ]
            + row_sems()[:2]
            if more
            else []
        ),
        compiler_params=pltpu.CompilerParams(
            collective_id=5 if more else 3, has_side_effects=True, vmem_limit_bytes=60 << 20
        ),
        name="last_backward" if more else "block_backward",
    )(*near, whole, *weights, *kept, *later)


def on_device(
    tokens_in,
    expert_ids,
    w_qkv,
    w_out,
    router,
    gains,
    shifts,
    w_in,
    b_in,
    w_exp_out,
    b_out,
    cotangent,
):
    tok_rows, width = tokens_in.shape
    layers = w_qkv.shape[0]
    own_rows = w_qkv.shape[1]
    out_cols = w_out.shape[1]
    experts = w_in.shape[1] * lax.axis_size("exp")
    whole, later_rows, spread = gather_weights(w_qkv, w_out, router, gains, shifts)
    expert_w = []
    for layer_idx in range(layers):
        own_in, own_out = w_in[layer_idx, 0], w_exp_out[layer_idx, 0]
        expert_w.append((own_in, other_core(own_in), own_out, other_core(own_out)))
    out_bias = 0.5 * in_order(b_out, other_core(b_out), 2).astype(F32)

    spare = -tok_rows % BLOCK
    ids = jnp.pad(expert_ids, ((0, 0), (0, spare), (0, 0)), constant_values=-1)
    state = jnp.pad(tokens_in.astype(F32), ((0, spare), (0, 0)))
    saved = []
    for layer_idx in range(layers):
        got = block_forward(
            (
                state,
                spread,
                ids[layer_idx],
                b_in[layer_idx],
                out_bias[layer_idx],
            ),
            whole,
            expert_w[layer_idx],
            later_rows if layer_idx == 0 else None,
        )
        saved.append((state, whole) + tuple(got[:13]))
        if layer_idx == 0:
            whole = got[13].reshape(whole.shape)
        state = got[5]
    mixed = state[:tok_rows].astype(BF16)
    grad_state = jnp.pad(cotangent.astype(F32), ((0, spare), (0, 0)))
    attn_grads = [None] * layers
    expert_grads = [None] * layers
    for layer_idx in reversed(range(layers)):
        (
            state_in,
            whole,
            after,
            h_two,
            gates,
            picked0,
            picked1,
            _,
            h_one,
            qkv,
            log_total,
            heads,
            rows_in,
            slope,
            active,
        ) = saved[layer_idx]
        grad_state, grad_att, grad_logits, sums, grad_qkv, *rest = (
            block_backward(
                (
                    grad_state,
                    spread,
                    ids[layer_idx],
                    gates,
                    picked0,
                    picked1,
                    after,
                    state_in,
                    qkv,
                    log_total,
                    heads,
                ),
                whole,
                expert_w[layer_idx],
                (slope, active, rows_in),
                attn_grads[layer_idx + 1] if layer_idx + 1 < layers else (),
            )
        )
        expert_grads[layer_idx] = rest[:4]
        attn_grads[layer_idx] = (h_one, grad_att, h_two, grad_qkv, heads, grad_logits, sums)
    grad_w_qkv, rest, grad_b_in, grad_b_out, grad_w_in, grad_w_exp_out = scatter_grads(
        attn_grads[0], rest[4], spread, expert_grads, own_rows
    )
    rest = rest[:, :own_rows]
    small = rest[:, :, out_cols:]
    return (
        mixed,
        grad_state[:tok_rows],
        grad_w_qkv,
        jnp.swapaxes(rest[:, :, :out_cols], 1, 2),
        small[:, :, :experts],
        jnp.swapaxes(small[:, :, experts : experts + 2], 1, 2),
        jnp.swapaxes(small[:, :, experts + 2 : experts + 5], 1, 2),
        grad_w_in,
        grad_b_in,
        grad_w_exp_out,
        grad_b_out,
    )


def solution(mesh):
    tokens = P(("rep", "exp"), None)
    placed = (
        tokens,
        P(None, ("rep", "exp"), None),
        P(None, ("rep", "exp"), None, "mdl"),
        P(None, "mdl", ("rep", "exp")),
        P(None, ("rep", "exp"), None),
        P(None, None, ("rep", "exp")),
        P(None, None, ("rep", "exp")),
        P(None, "exp", "rep", "mdl"),
        P(None, "exp", "mdl"),
        P(None, "exp", "mdl", "rep"),
        P(None, "exp", "rep"),
    )
    return jax.shard_map(
        on_device,
        mesh=mesh,
        in_specs=placed + (tokens,),
        out_specs=(tokens, tokens) + placed[2:],
        check_vma=False,
    )
```

```python
import jax
import jax.numpy as jnp
from jax import lax
from jax.experimental import pallas as pl
from jax.experimental.pallas import tpu as pltpu
from jax.sharding import PartitionSpec as P

HD = 64
SEQ = 197
EPSILON = 1e-06
F32 = jnp.float32
BF16 = jnp.bfloat16


def norm_rows(values, gain, shift):
    row_mean = jnp.mean(values, axis=-1, keepdims=True)
    centred = values - row_mean
    row_var = jnp.mean(centred * centred, axis=-1, keepdims=True)
    return centred * lax.rsqrt(row_var + EPSILON) * gain + shift


def dot(a, b):
    return jnp.dot(a, b, preferred_element_type=F32)


def dot_tn(a, b):
    return lax.dot_general(a, b, (((0,), (0,)), ((), ())), preferred_element_type=F32)


def dot_nt(a, b):
    return lax.dot_general(a, b, (((1,), (1,)), ((), ())), preferred_element_type=F32)


def other_core(values):
    return lax.ppermute(values, "rep", [(0, 1), (1, 0)])


def in_order(own, other, axis):
    first = lax.axis_index("rep") == 0
    return jnp.concatenate(
        [jnp.where(first, own, other), jnp.where(first, other, own)], axis=axis
    )


MESH = pl.DeviceIdType.MESH
BLOCK = 16
VMEM_SPEC = pl.BlockSpec(memory_space=pltpu.VMEM)
ANY_SPEC = pl.BlockSpec(memory_space=pl.ANY)
HBM_SPEC = pl.BlockSpec(memory_space=pltpu.HBM)
SMALL = 128
NEAR = 8
FAR = 4


def chip_place():
    rep = lax.axis_index("rep")
    exp = lax.axis_index("exp")
    near = (1 - rep) * (exp // 8 * 2 + exp // 4 % 2) + rep * (exp % 8)
    far = (1 - rep) * (exp % 4) + rep * (exp // 8)

    def chip_of(near_idx, far_idx):
        return (1 - rep) * (near_idx // 2 * 8 + near_idx % 2 * 4 + far_idx) + rep * (
            far_idx * 8 + near_idx
        )

    return rep, exp, near, far, chip_of


def greet(near, far, chip_of, rep):
    barrier = pltpu.get_barrier_semaphore()
    for step in range(1, NEAR):
        peer = chip_of((near + step) % NEAR, far)
        pl.semaphore_signal(barrier, inc=1, device_id={"exp": peer}, device_id_type=MESH)
    for step in range(1, FAR):
        peer = chip_of(near, (far + step) % FAR)
        pl.semaphore_signal(barrier, inc=1, device_id={"exp": peer}, device_id_type=MESH)
    pl.semaphore_signal(barrier, inc=1, device_id={"rep": 1 - rep}, device_id_type=MESH)
    return barrier


GREETED = NEAR + FAR - 1


def gather_kernel(
    w_qkv,
    w_out,
    router,
    gains,
    shifts,
    whole0,
    whole1,
    spread,
    mine,
    filled,
    vectors,
    own_sem,
    near_send,
    near_recv,
    far_send,
    far_recv,
    core_send,
    core_recv,
):
    rep, exp, near, far, chip_of = chip_place()
    wholes = (whole0, whole1)

    def near_copy(layer, step, slot):
        return pltpu.make_async_remote_copy(
            src_ref=mine.at[layer],
            dst_ref=wholes[layer].at[rep, exp],
            send_sem=near_send.at[layer, step],
            recv_sem=near_recv.at[layer, slot],
            device_id={"exp": chip_of((near + step) % NEAR, far)},
            device_id_type=MESH,
        )

    def far_copy(layer, step, source, slot_near, slot_far):
        return pltpu.make_async_remote_copy(
            src_ref=wholes[layer].at[rep, source],
            dst_ref=wholes[layer].at[rep, source],
            send_sem=far_send.at[layer, step, slot_near],
            recv_sem=far_recv.at[layer, slot_far, slot_near],
            device_id={"exp": chip_of(near, (far + step) % FAR)},
            device_id_type=MESH,
        )

    def core_copy(layer, source, part):
        return pltpu.make_async_remote_copy(
            src_ref=wholes[layer].at[part, source],
            dst_ref=wholes[layer].at[part, source],
            send_sem=core_send.at[layer, source],
            recv_sem=core_recv.at[layer, source],
            device_id={"rep": 1 - rep},
            device_id_type=MESH,
        )

    keeps = [
        pltpu.make_async_copy(mine.at[layer], wholes[layer].at[rep, exp], own_sem.at[layer])
        for layer in range(2)
    ]
    barrier = greet(near, far, chip_of, rep)
    layers, own_rows, parts, part_cols = w_qkv.shape
    qkv_cols = parts * part_cols
    cut = qkv_cols + w_out.shape[1]
    experts = router.shape[2]
    turn = (
        lax.broadcasted_iota(jnp.int32, (BLOCK, own_rows), 0)
        == lax.broadcasted_iota(jnp.int32, (BLOCK, own_rows), 1)
    )
    turn = jnp.where(turn, 1.0, 0.0).astype(BF16)
    filled[...] = jnp.zeros_like(filled)
    vectors[...] = jnp.zeros_like(vectors)
    for layer in range(layers):
        for part in range(parts):
            filled[:own_rows, part * part_cols : (part + 1) * part_cols] = w_qkv[
                layer, :, part, :
            ].astype(F32)
        filled[:, qkv_cols:cut] = dot_nt(turn, w_out[layer])
        vectors[experts : experts + 2, :] = gains[layer].astype(F32)
        vectors[experts + 2 : experts + 5, :] = shifts[layer].astype(F32)
        filled[:, cut:] = dot_nt(turn, vectors[...].astype(BF16))
        filled[:own_rows, cut : cut + experts] = router[layer].astype(F32)
        mine[layer] = filled[...].astype(BF16)
    for keep in keeps:
        keep.start()
    pl.semaphore_wait(barrier, GREETED)
    for layer in range(2):

        @pl.loop(1, NEAR)
        def _(step):
            near_copy(layer, step, near).start()

    row = lax.broadcasted_iota(jnp.int32, spread.shape, 0)
    col = lax.broadcasted_iota(jnp.int32, spread.shape, 1)
    inside = row & (BLOCK - 1)
    true_row = (row >> 4) * own_rows + inside
    spread[...] = jnp.where((inside < own_rows) & (true_row == col), 1.0, 0.0).astype(BF16)
    for keep in keeps:
        keep.wait()
    for layer in range(2):

        @pl.loop(0, NEAR)
        def _(back):
            slot = (near - back + NEAR) % NEAR
            source = chip_of(slot, far)

            @pl.when(back > 0)
            def _():
                near_copy(layer, back, slot).wait_recv()

            @pl.loop(1, FAR)
            def _(step):
                far_copy(layer, step, source, slot, far).start()

            core_copy(layer, source, rep).start()

    for layer in range(2):

        @pl.loop(0, NEAR)
        def _(back):
            slot = (near - back + NEAR) % NEAR

            @pl.loop(1, FAR)
            def _(step):
                slot_far = (far - step + FAR) % FAR
                source = chip_of(slot, slot_far)
                far_copy(layer, step, source, slot, slot_far).wait_recv()
                core_copy(layer, source, rep).start()

    for layer in range(2):

        @pl.loop(0, NEAR * FAR)
        def _(source):
            core_copy(layer, source, 1 - rep).wait_recv()
            core_copy(layer, source, rep).wait_send()

        @pl.loop(1, NEAR)
        def _(step):
            near_copy(layer, step, near).wait_send()

        @pl.loop(1, FAR)
        def _(step):
            @pl.loop(0, NEAR)
            def _(slot):
                far_copy(layer, step, chip_of(slot, far), slot, far).wait_send()


def gather_weights(w_qkv, w_out, router, gains, shifts):
    layers, own_rows, parts, part_cols = w_qkv.shape
    cols = parts * part_cols + w_out.shape[1] + SMALL
    devices = 2 * NEAR * FAR
    whole = jax.ShapeDtypeStruct((2, NEAR * FAR, BLOCK, cols), BF16)
    got = pl.pallas_call(
        gather_kernel,
        out_shape=(
            whole,
            whole,
            jax.ShapeDtypeStruct((devices * BLOCK, devices * own_rows), BF16),
        ),
        in_specs=[VMEM_SPEC] * 5,
        out_specs=(HBM_SPEC, HBM_SPEC, VMEM_SPEC),
        scratch_shapes=[
            pltpu.VMEM((layers, BLOCK, cols), BF16),
            pltpu.VMEM((BLOCK, cols), F32),
            pltpu.VMEM((SMALL, own_rows), F32),
            pltpu.SemaphoreType.DMA((2,)),
            pltpu.SemaphoreType.DMA((2, NEAR)),
            pltpu.SemaphoreType.DMA((2, NEAR)),
            pltpu.SemaphoreType.DMA((2, FAR, NEAR)),
            pltpu.SemaphoreType.DMA((2, FAR, NEAR)),
            pltpu.SemaphoreType.DMA((2, NEAR * FAR)),
            pltpu.SemaphoreType.DMA((2, NEAR * FAR)),
        ],
        compiler_params=pltpu.CompilerParams(
            collective_id=0, has_side_effects=True, vmem_limit_bytes=32 << 20
        ),
        name="gather_weights",
    )(w_qkv, w_out, router, gains, shifts)
    return [value.reshape(devices * BLOCK, cols) for value in got[:2]], got[2]


def scatter_kernel(*refs):
    per_layer = [refs[7 * layer : 7 * layer + 7] for layer in range(2)]
    spread = refs[14]
    biases = refs[15:19]
    experts = refs[19:23]
    out_qkv, out_proj, out_router, out_gains, out_shifts = refs[23:28]
    out_b_in, out_b_out, out_in, out_exp = refs[28:32]
    (
        lhs_qkv,
        lhs_proj,
        lhs_small,
        sums,
        part,
        from_core,
        from_far,
        total,
        from_near,
        stage_in,
        stage_exp,
        stage_sems,
        core_send,
        core_recv,
        far_send,
        far_recv,
        near_send,
        near_recv,
    ) = refs[32:]
    rep, exp, near, far, chip_of = chip_place()
    qkv_cols, proj_cols = per_layer[0][3].shape[1], per_layer[0][4].shape[1]
    cut = qkv_cols + proj_cols
    rows = BLOCK * 8
    chunks = NEAR * FAR // 8
    loads, stores = [], []
    for layer in range(2):
        for kind, (stage, out) in enumerate(((stage_in, out_in), (stage_exp, out_exp))):
            idx = 2 * layer + kind
            loads.append(
                pltpu.make_async_copy(experts[idx], stage.at[layer], stage_sems.at[idx])
            )
            stores.append(
                pltpu.make_async_copy(stage.at[layer], out.at[layer, 0], stage_sems.at[idx])
            )
    for load in loads:
        load.start()

    def multiply(layer, core, chunk):
        rhs_qkv, rhs_proj, rhs_small = per_layer[layer][3:6]
        at = pl.ds(pl.multiple_of((core * chunks + chunk) * rows, rows), rows)
        to = pl.ds(pl.multiple_of(chunk * rows, rows), rows)
        part[layer, core, to, :qkv_cols] = dot(lhs_qkv[at, :], rhs_qkv[...]).astype(BF16)
        part[layer, core, to, qkv_cols:cut] = dot(lhs_proj[at, :], rhs_proj[...]).astype(BF16)
        part[layer, core, to, cut:] = (
            dot(lhs_small[at, :], rhs_small[...]) + sums[at, :]
        ).astype(BF16)

    def core_copy(layer, chunk):
        to = pl.ds(pl.multiple_of(chunk * rows, rows), rows)
        return pltpu.make_async_remote_copy(
            src_ref=part.at[layer, 1 - rep, to],
            dst_ref=from_core.at[layer, to],
            send_sem=core_send.at[layer, chunk],
            recv_sem=core_recv.at[layer, chunk],
            device_id={"rep": 1 - rep},
            device_id_type=MESH,
        )

    def far_copy(layer, step, slot):
        return pltpu.make_async_remote_copy(
            src_ref=part.at[layer, rep, block(chip_of(slot, (far + step) % FAR))],
            dst_ref=from_far.at[layer, step, block(slot)],
            send_sem=far_send.at[layer, step, slot],
            recv_sem=far_recv.at[layer, step, slot],
            device_id={"exp": chip_of(near, (far + step) % FAR)},
            device_id_type=MESH,
        )

    def near_copy(layer, step):
        return pltpu.make_async_remote_copy(
            src_ref=total.at[layer, block((near + step) % NEAR)],
            dst_ref=from_near.at[layer, step],
            send_sem=near_send.at[layer, step],
            recv_sem=near_recv.at[layer, step],
            device_id={"exp": chip_of((near + step) % NEAR, far)},
            device_id_type=MESH,
        )

    def flush(layer):
        @pl.loop(0, chunks)
        def _(chunk):
            to = pl.ds(pl.multiple_of(chunk * rows, rows), rows)
            core_copy(layer, chunk).wait_recv()
            part[layer, rep, to, :] = (
                part[layer, rep, to, :].astype(F32) + from_core[layer, to, :].astype(F32)
            ).astype(BF16)

        @pl.loop(1, NEAR + 1)
        def _(ahead):
            @pl.loop(1, FAR)
            def _(step):
                far_copy(layer, step, (near + ahead) % NEAR).start()

    barrier = greet(near, far, chip_of, rep)
    for layer in range(2):
        h_one, grad_att, h_two = per_layer[layer][:3]
        lhs_qkv[...] = dot_nt(spread[...], h_one[...]).astype(BF16)
        lhs_proj[...] = dot_nt(spread[...], grad_att[...]).astype(BF16)
        lhs_small[...] = dot_nt(spread[...], h_two[...]).astype(BF16)
        sums[...] = dot_nt(spread[...], per_layer[layer][6][...].astype(BF16))
        if layer == 0:
            pl.semaphore_wait(barrier, GREETED)

        @pl.loop(0, chunks)
        def _(chunk):
            multiply(layer, 1 - rep, chunk)
            core_copy(layer, chunk).start()

        if layer == 1:
            flush(0)

        @pl.loop(0, chunks)
        def _(chunk):
            multiply(layer, rep, chunk)

    flush(1)
    for load in loads:
        load.wait()
    for store in stores:
        store.start()
    for layer in range(2):
        out_b_in[layer] = biases[2 * layer][...]
        out_b_out[layer] = biases[2 * layer + 1][...]

    def add_far(layer, slot):
        for step in range(1, FAR):
            far_copy(layer, step, slot).wait_recv()
        value = part[layer, rep, block(chip_of(slot, far)), :].astype(F32)
        for step in range(1, FAR):
            value = value + from_far[layer, step, block(slot), :].astype(F32)
        return value

    for layer in range(2):

        @pl.loop(1, NEAR)
        def _(step):
            slot = (near + step) % NEAR
            total[layer, block(slot), :] = add_far(layer, slot).astype(BF16)
            near_copy(layer, step).start()

    own_rows = out_qkv.shape[1]
    part_cols = qkv_cols // 3
    turn = jnp.where(
        lax.broadcasted_iota(jnp.int32, (BLOCK, own_rows), 0)
        == lax.broadcasted_iota(jnp.int32, (BLOCK, own_rows), 1),
        1.0,
        0.0,
    )
    for layer in range(2):
        value = add_far(layer, near)
        for step in range(1, NEAR):
            near_copy(layer, step).wait_recv()
            value = value + from_near[layer, step].astype(F32)
        for idx in range(3):
            out_qkv[layer, :, idx, :] = value[:own_rows, idx * part_cols : (idx + 1) * part_cols]
        turned = lax.dot_general(
            value[:, qkv_cols:],
            turn,
            (((0,), (0,)), ((), ())),
            precision=lax.Precision.HIGHEST,
            preferred_element_type=F32,
        )
        out_proj[layer] = turned[:proj_cols]
        first = proj_cols + out_router.shape[2]
        out_router[layer] = value[:own_rows, cut : cut + out_router.shape[2]]
        out_gains[layer] = turned[first : first + 2]
        out_shifts[layer] = turned[first + 2 : first + 5]

    for layer in range(2):

        @pl.loop(1, NEAR)
        def _(step):
            near_copy(layer, step).wait_send()

        @pl.loop(1, FAR)
        def _(step):
            @pl.loop(0, NEAR)
            def _(slot):
                far_copy(layer, step, slot).wait_send()

        @pl.loop(0, chunks)
        def _(chunk):
            core_copy(layer, chunk).wait_send()

    for store in stores:
        store.wait()


def scatter_grads(attn, spread, experts, own_rows):
    tokens = attn[0][0].shape[0]
    qkv_cols, proj_cols = attn[0][3].shape[1], attn[0][4].shape[1]
    cols = qkv_cols + proj_cols + SMALL
    half = NEAR * FAR * BLOCK
    grad_in, grad_exp, grad_b_in, grad_b_out = experts[0]
    shape = jax.ShapeDtypeStruct
    chunks = NEAR * FAR // 8
    return pl.pallas_call(
        scatter_kernel,
        out_shape=(
            shape((2, own_rows, 3, qkv_cols // 3), F32),
            shape((2, proj_cols, own_rows), F32),
            shape((2, own_rows, NEAR * FAR), F32),
            shape((2, 2, own_rows), F32),
            shape((2, 3, own_rows), F32),
            shape((2,) + grad_b_in.shape, F32),
            shape((2,) + grad_b_out.shape, F32),
            shape((2, 1) + grad_in.shape, F32),
            shape((2, 1) + grad_exp.shape, F32),
        ),
        in_specs=[VMEM_SPEC] * 19 + [ANY_SPEC] * 4,
        out_specs=tuple([VMEM_SPEC] * 7 + [ANY_SPEC] * 2),
        scratch_shapes=[
            pltpu.VMEM((2 * half, tokens), BF16),
            pltpu.VMEM((2 * half, tokens), BF16),
            pltpu.VMEM((2 * half, tokens), BF16),
            pltpu.VMEM((2 * half, SMALL), F32),
            pltpu.VMEM((2, 2, half, cols), BF16),
            pltpu.VMEM((2, half, cols), BF16),
            pltpu.VMEM((2, FAR, NEAR * BLOCK, cols), BF16),
            pltpu.VMEM((2, NEAR * BLOCK, cols), BF16),
            pltpu.VMEM((2, NEAR, BLOCK, cols), BF16),
            pltpu.VMEM((2,) + grad_in.shape, F32),
            pltpu.VMEM((2,) + grad_exp.shape, F32),
            pltpu.SemaphoreType.DMA((4,)),
            pltpu.SemaphoreType.DMA((2, chunks)),
            pltpu.SemaphoreType.DMA((2, chunks)),
            pltpu.SemaphoreType.DMA((2, FAR, NEAR)),
            pltpu.SemaphoreType.DMA((2, FAR, NEAR)),
            pltpu.SemaphoreType.DMA((2, NEAR)),
            pltpu.SemaphoreType.DMA((2, NEAR)),
        ],
        compiler_params=pltpu.CompilerParams(
            collective_id=1, has_side_effects=True, vmem_limit_bytes=56 << 20
        ),
        name="scatter_grads",
    )(
        *attn[0],
        *attn[1],
        spread,
        *(value for parts in experts for value in parts[2:]),
        *(value for parts in experts for value in parts[:2]),
    )


PLANES = 4
PLANE = 8


def block(source):
    return pl.ds(pl.multiple_of(source * BLOCK, BLOCK), BLOCK)


def plane_rows(plane):
    return pl.ds(pl.multiple_of(plane * (PLANE * BLOCK), PLANE * BLOCK), PLANE * BLOCK)


def plane_step(turn):
    return turn + turn // 2 - 2 * (turn // 3)


def greet_all(exp):
    barrier = pltpu.get_barrier_semaphore()

    @pl.loop(1, PLANES * PLANE)
    def _(step):
        peer = (exp + step) % (PLANES * PLANE)
        pl.semaphore_signal(barrier, inc=1, device_id={"exp": peer}, device_id_type=MESH)

    mdl = lax.axis_index("mdl")
    pl.semaphore_signal(barrier, inc=1, device_id={"mdl": 1 - mdl}, device_id_type=MESH)
    return barrier


def core_send_copy(src, dst, sems, idx):
    return pltpu.make_async_remote_copy(
        src_ref=src,
        dst_ref=dst,
        send_sem=sems.at[idx, 0],
        recv_sem=sems.at[idx, 1],
        device_id={"rep": 1 - lax.axis_index("rep")},
        device_id_type=MESH,
    )


def half_copy(src, dst, sems, idx):
    return pltpu.make_async_remote_copy(
        src_ref=src,
        dst_ref=dst,
        send_sem=sems.at[idx, 0],
        recv_sem=sems.at[idx, 1],
        device_id={"mdl": 1 - lax.axis_index("mdl")},
        device_id_type=MESH,
    )


def row_copy(src, dst, exp, send_sem, recv_sem, peer, source):
    return pltpu.make_async_remote_copy(
        src_ref=src.at[block(peer)],
        dst_ref=dst.at[block(exp)],
        send_sem=send_sem.at[peer],
        recv_sem=recv_sem.at[source],
        device_id={"exp": peer},
        device_id_type=MESH,
    )


def send_all(src, dst, exp, send_sem, recv_sem):
    @pl.loop(0, PLANES)
    def _(turn):
        plane = (exp // PLANE + plane_step(turn)) % PLANES

        @pl.loop(0, PLANE)
        def _(step):
            peer = plane * PLANE + (exp + step) % PLANE

            @pl.when(turn + step > 0)
            def _():
                row_copy(src, dst, exp, send_sem, recv_sem, peer, exp).start()

    dst[block(exp), :] = src[block(exp), :]


def each_plane(src, back_src, dst, back_dst, exp, sems, work):
    send_sem, recv_sem, back_send, back_recv = sems

    @pl.loop(0, PLANES)
    def _(turn):
        plane = (exp // PLANE - plane_step(turn) + PLANES) % PLANES

        @pl.loop(0, PLANE)
        def _(step):
            source = plane * PLANE + (exp - step + PLANE) % PLANE

            @pl.when(turn + step > 0)
            def _():
                row_copy(src, dst, exp, send_sem, recv_sem, source, source).wait_recv()

        work(plane_rows(plane))

        @pl.loop(0, PLANE)
        def _(step):
            source = plane * PLANE + (exp - step + PLANE) % PLANE

            @pl.when(turn + step > 0)
            def _():
                row_copy(back_src, back_dst, exp, back_send, back_recv, source, exp).start()

    back_dst[block(exp), :] = back_src[block(exp), :]


def wait_back(back_src, back_dst, exp, sems):
    @pl.loop(1, PLANES * PLANE)
    def _(step):
        source = (exp + step) % (PLANES * PLANE)
        row_copy(back_src, back_dst, exp, sems[2], sems[3], source, source).wait_recv()


def wait_sent(src, dst, back_src, back_dst, exp, sems):
    @pl.loop(1, PLANES * PLANE)
    def _(step):
        peer = (exp + step) % (PLANES * PLANE)
        row_copy(src, dst, exp, sems[0], sems[1], peer, peer).wait_send()
        row_copy(back_src, back_dst, exp, sems[2], sems[3], peer, peer).wait_send()


def weight_loads(own_in, other_in, own_out, other_out, w_in, w_out):
    rep = lax.axis_index("rep")
    depth = own_in.shape[0]
    pairs = []
    for src_in, src_out, core in ((own_in, own_out, rep), (other_in, other_out, 1 - rep)):
        place = pl.ds(pl.multiple_of(core * depth, 128), depth)
        pairs.append((src_in, w_in.at[place, :]))
        pairs.append((src_out, w_out.at[:, place]))
    return pairs


def lanes(values):
    rows = values[0].shape[0]
    lane = lax.broadcasted_iota(jnp.int32, (rows, 128), 1)
    total = jnp.zeros((rows, 128), F32)
    for idx, value in enumerate(values):
        total = jnp.where(lane == idx, value, total)
    return total


def row_sems():
    return [pltpu.SemaphoreType.DMA((PLANES * PLANE,))] * 4


def head_slices(head, width):
    start = head * HD
    return [slice(part * width + start, part * width + start + HD) for part in range(3)]


def masked_scores(query_rows, key_rows):
    scores = dot_nt(query_rows, key_rows) * HD ** (-0.5)
    col = lax.broadcasted_iota(jnp.int32, scores.shape, 1)
    return jnp.where(col < SEQ, scores, -1e30)


def route(ids, hot0, hot1, pick0, pick1):
    tokens, slots = pick0.shape
    lane = lax.broadcasted_iota(jnp.int32, (tokens, 128), 1)
    hots = [jnp.where(ids[:, k : k + 1] == lane, 1.0, 0.0) for k in range(2)]
    hot0[...], hot1[...] = hots[0].astype(BF16), hots[1].astype(BF16)
    row = lax.broadcasted_iota(jnp.int32, (tokens, tokens), 0)
    col = lax.broadcasted_iota(jnp.int32, (tokens, tokens), 1)
    before = jnp.where(row > col, 1.0, 0.0).astype(BF16)
    earlier = dot(before, (hots[0] + hots[1]).astype(BF16))
    place = lax.broadcasted_iota(jnp.int32, (tokens, slots), 1).astype(F32)
    for k, pick in enumerate((pick0, pick1)):
        within = jnp.sum(earlier * hots[k], axis=1, keepdims=True)
        slot = ids[:, k : k + 1].astype(F32) * BLOCK + within
        pick[...] = jnp.where(slot == place, 1.0, 0.0).astype(BF16)


def attend_forward(qkv, heads, log_total, at):
    width = heads.shape[1]
    totals = []
    for head in range(width // HD):
        q_at, k_at, v_at = head_slices(head, width)
        scores = masked_scores(qkv[at, q_at], qkv[:, k_at])
        top_score = jnp.max(scores, axis=-1, keepdims=True)
        raw_weight = jnp.exp(scores - top_score)
        row_total = jnp.sum(raw_weight, axis=-1, keepdims=True)
        probs_low = (raw_weight / row_total).astype(BF16)
        totals.append(top_score + jnp.log(row_total))
        heads[at, q_at] = dot(probs_low, qkv[:, v_at]).astype(BF16)
    log_total[at, :] = lanes(totals)


def attend_backward(grad_heads, qkv, log_total, grad_qkv):
    width = grad_heads.shape[1]
    for head in range(width // HD):
        q_at, k_at, v_at = head_slices(head, width)
        query_rows, key_rows, value_rows = qkv[:, q_at], qkv[:, k_at], qkv[:, v_at]
        grad_out = grad_heads[:, q_at]
        probs = jnp.exp(masked_scores(query_rows, key_rows) - log_total[:, head : head + 1])
        grad_probs = dot_nt(grad_out, value_rows)
        grad_scores = probs * (grad_probs - jnp.sum(grad_probs * probs, axis=-1, keepdims=True))
        grad_scores = grad_scores.astype(BF16)
        grad_qkv[:, q_at] = (dot(grad_scores, key_rows) * HD ** (-0.5)).astype(BF16)
        grad_qkv[:, k_at] = (dot_tn(grad_scores, query_rows) * HD ** (-0.5)).astype(BF16)
        grad_qkv[:, v_at] = dot_tn(probs.astype(BF16), grad_out).astype(BF16)


def block_forward_kernel(
    state,
    spread,
    ids,
    b_in,
    b_out,
    whole_in,
    own_in,
    other_in,
    own_out,
    other_out,
    after_out,
    h_out,
    gates_out,
    picked0_out,
    picked1_out,
    next_out,
    h_one_out,
    qkv_out,
    log_out,
    heads_out,
    rows_out,
    slope_out,
    active_out,
    hot0,
    hot1,
    pick0,
    pick1,
    whole,
    w_in,
    w_out,
    send,
    rows,
    slope,
    active,
    back_src,
    back,
    own_att,
    low_att,
    own_moe,
    low_moe,
    load_sems,
    out_sems,
    half_sems,
    send_sem,
    recv_sem,
    back_send,
    back_recv,
):
    exp = lax.axis_index("exp")
    sems = (send_sem, recv_sem, back_send, back_recv)
    loads = [
        pltpu.make_async_copy(src, dst, load_sems.at[idx])
        for idx, (src, dst) in enumerate(
            [(whole_in, whole)]
            + weight_loads(own_in, other_in, own_out, other_out, w_in, w_out)
        )
    ]
    for load in loads:
        load.start()
    barrier = greet_all(exp)
    qkv_cols = qkv_out.shape[1]
    cut = qkv_cols + heads_out.shape[1]
    loads[0].wait()
    small = dot_tn(whole[:, cut:], spread[...])
    first_row = PLANES * PLANE
    gain0, gain1, shift0, shift1, shift2 = [
        small[first_row + idx : first_row + idx + 1, :] for idx in range(5)
    ]
    h_one = norm_rows(state[...], gain0, shift0).astype(BF16)
    h_one_out[...] = h_one
    wide = dot_nt(h_one, spread[...]).astype(BF16)
    qkv_out[...] = dot(wide, whole[:, :qkv_cols]).astype(BF16)
    tokens = state.shape[0]
    middle = -(-tokens // (2 * BLOCK)) * BLOCK
    halves = (pl.ds(0, middle), pl.ds(middle, tokens - middle))
    pair_copies = []
    for idx, at in enumerate(halves):
        attend_forward(qkv_out, heads_out, log_out, at)
        own_att[at, :] = dot(
            dot_nt(heads_out[at, :], whole[:, qkv_cols:cut]).astype(BF16), spread[...]
        ).astype(BF16)
        if idx == 0:
            pl.semaphore_wait(barrier, PLANES * PLANE)
        pair_copies.append(half_copy(own_att.at[at, :], low_att.at[at, :], half_sems, idx))
        pair_copies[-1].start()
    route(ids, hot0, hot1, pick0, pick1)
    for copy in pair_copies:
        copy.wait_recv()
    after = state[...] + (own_att[...].astype(F32) + low_att[...].astype(F32)) + shift2
    after_out[...] = after
    h_two = norm_rows(after, gain1, shift1).astype(BF16)
    h_out[...] = h_two
    send[...] = dot_tn(pick0[...] + pick1[...], h_two).astype(BF16)
    send_all(send, rows, exp, send_sem, recv_sem)
    logits = dot_nt(h_two, small.astype(BF16))
    chosen = [jnp.sum(logits * hot[...].astype(F32), axis=1, keepdims=True) for hot in (hot0, hot1)]
    top = jnp.maximum(chosen[0], chosen[1])
    raw = [jnp.exp(value - top) for value in chosen]
    gates = [value / (raw[0] + raw[1]) for value in raw]
    gates_out[...] = lanes(gates)
    bias_in = b_in[...].astype(F32)
    for load in loads[1:]:
        load.wait()
    tile = 512

    def work(at):
        for col in range(0, active.shape[1], tile):
            cols = slice(col, col + tile)
            inner = dot(rows[at, :], w_in[:, cols]) + bias_in[:, cols]
            cdf = 0.5 * (1.0 + lax.erf(inner * (0.5**0.5)))
            active[at, cols] = (inner * cdf).astype(BF16)
            slope[at, cols] = (
                cdf + inner * jnp.exp(-0.5 * inner * inner) * 0.3989422804014327
            ).astype(BF16)
        back_src[at, :] = (dot(active[at, :], w_out[...]) + b_out[...]).astype(BF16)

    each_plane(send, back_src, rows, back, exp, sems, work)
    saves = [
        pltpu.make_async_copy(src, dst, out_sems.at[idx])
        for idx, (src, dst) in enumerate(
            ((rows, rows_out), (slope, slope_out), (active, active_out))
        )
    ]
    for save in saves:
        save.start()
    wait_back(back_src, back, exp, sems)
    for idx, at in enumerate(halves):
        picked = [dot(pick[at, :], back[...]) for pick in (pick0, pick1)]
        own_moe[at, :] = (
            gates_out[at, 0:1] * picked[0] + gates_out[at, 1:2] * picked[1]
        ).astype(BF16)
        pair_copies.append(half_copy(own_moe.at[at, :], low_moe.at[at, :], half_sems, 2 + idx))
        pair_copies[-1].start()
        picked0_out[at, :] = picked[0].astype(BF16)
        picked1_out[at, :] = picked[1].astype(BF16)
    wait_sent(send, rows, back_src, back, exp, sems)
    for copy in pair_copies[2:]:
        copy.wait_recv()
    next_out[...] = after_out[...] + (own_moe[...].astype(F32) + low_moe[...].astype(F32))
    for copy in pair_copies:
        copy.wait_send()
    for save in saves:
        save.wait()


def block_forward(near, whole, weights):
    tokens, width = near[0].shape
    slots = BLOCK * PLANES * PLANE
    hidden = weights[0].shape[1]
    cols = whole.shape[1]
    proj = (cols - SMALL) // 4
    shape = jax.ShapeDtypeStruct
    return pl.pallas_call(
        block_forward_kernel,
        out_shape=(
            shape((tokens, width), F32),
            shape((tokens, width), BF16),
            shape((tokens, 128), F32),
            shape((tokens, width), BF16),
            shape((tokens, width), BF16),
            shape((tokens, width), F32),
            shape((tokens, width), BF16),
            shape((tokens, 3 * proj), BF16),
            shape((tokens, 128), F32),
            shape((tokens, proj), BF16),
            shape((slots, width), BF16),
            shape((slots, hidden), BF16),
            shape((slots, hidden), BF16),
        ),
        in_specs=[VMEM_SPEC] * 5 + [ANY_SPEC] * 5,
        out_specs=tuple([VMEM_SPEC] * 10 + [ANY_SPEC] * 3),
        scratch_shapes=[
            pltpu.VMEM((tokens, 128), BF16),
            pltpu.VMEM((tokens, 128), BF16),
            pltpu.VMEM((tokens, slots), BF16),
            pltpu.VMEM((tokens, slots), BF16),
            pltpu.VMEM(whole.shape, BF16),
            pltpu.VMEM((width, hidden), BF16),
            pltpu.VMEM((hidden, width), BF16),
            pltpu.VMEM((slots, width), BF16),
            pltpu.VMEM((slots, width), BF16),
            pltpu.VMEM((slots, hidden), BF16),
            pltpu.VMEM((slots, hidden), BF16),
            pltpu.VMEM((slots, width), BF16),
            pltpu.VMEM((slots, width), BF16),
        ]
        + [pltpu.VMEM((tokens, width), BF16)] * 4
        + [
            pltpu.SemaphoreType.DMA((5,)),
            pltpu.SemaphoreType.DMA((3,)),
            pltpu.SemaphoreType.DMA((4, 2)),
        ]
        + row_sems(),
        compiler_params=pltpu.CompilerParams(
            collective_id=2, has_side_effects=True, vmem_limit_bytes=56 << 20
        ),
        name="block_forward",
    )(*near, whole, *weights)


def norm_parts(values):
    row_mean = jnp.mean(values, axis=-1, keepdims=True)
    centred = values - row_mean
    row_var = jnp.mean(centred * centred, axis=-1, keepdims=True)
    scale = lax.rsqrt(row_var + EPSILON)
    return centred * scale, scale


def norm_grad(grad, unit, scale, gain):
    scaled = grad * gain
    return scale * (
        scaled
        - jnp.mean(scaled, axis=-1, keepdims=True)
        - unit * jnp.mean(scaled * unit, axis=-1, keepdims=True)
    )


def block_backward_kernel(
    grad_state,
    spread,
    ids,
    gates,
    picked0,
    picked1,
    after,
    state_in,
    qkv,
    log_total,
    heads,
    whole_in,
    own_in,
    other_in,
    own_out,
    other_out,
    slope_in,
    active_in,
    rows_in,
    grad_out,
    grad_att_out,
    grad_logits_out,
    sums_out,
    grad_qkv_out,
    grad_in_out,
    grad_exp_out,
    grad_b_in_out,
    grad_b_out_out,
    hot0,
    hot1,
    pick0,
    pick1,
    whole,
    w_in,
    w_out,
    slope,
    active,
    kept_rows,
    send,
    rows,
    inner,
    back_src,
    back,
    own_gate,
    low_gate,
    own_h,
    low_h,
    own_one,
    low_one,
    product,
    in_away,
    in_got,
    exp_away,
    exp_got,
    bias_own,
    bias_got,
    grad_heads,
    load_sems,
    half_sems,
    core_sems,
    send_sem,
    recv_sem,
    back_send,
    back_recv,
):
    exp = lax.axis_index("exp")
    rep = lax.axis_index("rep")
    sems = (send_sem, recv_sem, back_send, back_recv)
    loads = [
        pltpu.make_async_copy(src, dst, load_sems.at[idx])
        for idx, (src, dst) in enumerate(
            weight_loads(own_in, other_in, own_out, other_out, w_in, w_out)
            + [
                (slope_in, slope),
                (whole_in, whole),
                (active_in, active),
                (rows_in, kept_rows),
            ]
        )
    ]
    for load in loads:
        load.start()
    barrier = greet_all(exp)
    pl.semaphore_signal(barrier, inc=1, device_id={"rep": 1 - rep}, device_id_type=MESH)
    grad = grad_state[...]
    gate0, gate1 = gates[:, 0:1], gates[:, 1:2]
    route(ids, hot0, hot1, pick0, pick1)
    send[...] = (
        dot_tn(pick0[...], (gate0 * grad).astype(BF16))
        + dot_tn(pick1[...], (gate1 * grad).astype(BF16))
    ).astype(BF16)
    pl.semaphore_wait(barrier, PLANES * PLANE + 1)
    send_all(send, rows, exp, send_sem, recv_sem)
    own_gate[...] = lanes(
        [
            jnp.sum(grad * picked[...].astype(F32), axis=1, keepdims=True)
            for picked in (picked0, picked1)
        ]
    )
    first = half_copy(own_gate, low_gate, half_sems, 0)
    first.start()
    for load in loads:
        load.wait()
    qkv_cols = qkv.shape[1]
    cut = qkv_cols + heads.shape[1]
    small = dot_tn(whole[:, cut:], spread[...])
    first_row = PLANES * PLANE
    gain0, gain1 = [small[first_row + idx : first_row + idx + 1, :] for idx in range(2)]

    def work(at):
        grad_active = dot_nt(rows[at, :], w_out[...])
        inner[at, :] = (grad_active * slope[at, :].astype(F32)).astype(BF16)
        back_src[at, :] = dot_nt(inner[at, :], w_in[...]).astype(BF16)

    each_plane(send, back_src, rows, back, exp, sems, work)

    half = grad_in_out.shape[0]
    hidden = inner.shape[1]
    own_at = pl.ds(pl.multiple_of(rep * half, 128), half)
    other_at = pl.ds(pl.multiple_of((1 - rep) * half, 128), half)
    in_away[...] = dot_tn(kept_rows[:, other_at], inner[...]).astype(BF16)
    in_copy = core_send_copy(in_away, in_got, core_sems, 0)
    in_copy.start()
    tall = product.shape[0]
    for start in range(0, hidden, tall):
        part = slice(start, start + tall)
        product[...] = dot_tn(active[:, part], rows[...])
        grad_exp_out[part, :] = product[:, own_at]
        exp_away[part, :] = product[:, other_at].astype(BF16)
    exp_copy = core_send_copy(exp_away, exp_got, core_sems, 1)
    exp_copy.start()
    bias_own[...] = jnp.zeros_like(bias_own)
    bias_own[0:1, :hidden] = jnp.sum(inner[...].astype(F32), axis=0, keepdims=True)
    bias_own[0:1, hidden:] = jnp.sum(rows[...].astype(F32), axis=0, keepdims=True)
    bias_copy = core_send_copy(bias_own, bias_got, core_sems, 2)
    bias_copy.start()
    grad_in_out[...] = dot_tn(kept_rows[:, own_at], inner[...])

    first.wait_recv()
    total = own_gate[...] + low_gate[...]
    grad0, grad1 = total[:, 0:1], total[:, 1:2]
    mean = gate0 * grad0 + gate1 * grad1
    grad_logits = (
        gate0 * (grad0 - mean) * hot0[...].astype(F32)
        + gate1 * (grad1 - mean) * hot1[...].astype(F32)
    ).astype(BF16)
    grad_logits_out[...] = grad_logits
    from_router = dot(grad_logits, small.astype(BF16))
    unit, scale = norm_parts(after[...])
    wait_back(back_src, back, exp, sems)
    own_h[...] = dot(pick0[...] + pick1[...], back[...]).astype(BF16)
    second = half_copy(own_h, low_h, half_sems, 1)
    second.start()
    in_copy.wait_recv()
    grad_in_out[...] += in_got[...].astype(F32)
    exp_copy.wait_recv()
    grad_exp_out[...] += exp_got[...].astype(F32)
    bias_copy.wait()
    bias_own[...] += bias_got[...]
    grad_b_in_out[...] = bias_own[0:1, :hidden]
    grad_b_out_out[...] = bias_own[
        0:1, pl.ds(pl.multiple_of(hidden + rep * half, 128), half)
    ]
    wait_sent(send, rows, back_src, back, exp, sems)
    second.wait_recv()
    grad_h = own_h[...].astype(F32) + low_h[...].astype(F32) + from_router
    grad_after = norm_grad(grad_h, unit, scale, gain1) + grad_state[...]
    grad_att = grad_after.astype(BF16)
    grad_att_out[...] = grad_att
    sums_out[...] = jnp.zeros_like(sums_out)
    put = lambda idx, value: sums_out.__setitem__(
        (slice(first_row + idx, first_row + idx + 1), slice(None)),
        jnp.sum(value, axis=0, keepdims=True),
    )
    put(1, grad_h * unit)
    put(3, grad_h)
    put(4, grad_after)
    wide = dot_nt(grad_att, spread[...]).astype(BF16)
    grad_heads[...] = dot(wide, whole[:, qkv_cols:cut]).astype(BF16)
    attend_backward(grad_heads, qkv, log_total, grad_qkv_out)
    own_one[...] = dot(
        dot_nt(grad_qkv_out[...], whole[:, :qkv_cols]).astype(BF16), spread[...]
    ).astype(BF16)
    third = half_copy(own_one, low_one, half_sems, 2)
    third.start()
    unit, scale = norm_parts(state_in[...])
    third.wait_recv()
    grad_one = own_one[...].astype(F32) + low_one[...].astype(F32)
    grad_out[...] = grad_after + norm_grad(grad_one, unit, scale, gain0)
    put(0, grad_one * unit)
    put(2, grad_one)
    for copy in (first, second, third, in_copy, exp_copy):
        copy.wait_send()


def block_backward(near, whole, weights, kept):
    tokens, width = near[0].shape
    slots = BLOCK * PLANES * PLANE
    hidden = weights[0].shape[1]
    cols = whole.shape[1]
    proj = (cols - SMALL) // 4
    half = width // 2
    shape = jax.ShapeDtypeStruct
    return pl.pallas_call(
        block_backward_kernel,
        out_shape=(
            shape((tokens, width), F32),
            shape((tokens, width), BF16),
            shape((tokens, 128), BF16),
            shape((128, width), F32),
            shape((tokens, 3 * proj), BF16),
            shape((half, hidden), F32),
            shape((hidden, half), F32),
            shape((1, hidden), F32),
            shape((1, half), F32),
        ),
        in_specs=[VMEM_SPEC] * 11 + [ANY_SPEC] * 8,
        out_specs=tuple([VMEM_SPEC] * 9),
        scratch_shapes=[
            pltpu.VMEM((tokens, 128), BF16),
            pltpu.VMEM((tokens, 128), BF16),
            pltpu.VMEM((tokens, slots), BF16),
            pltpu.VMEM((tokens, slots), BF16),
            pltpu.VMEM(whole.shape, BF16),
            pltpu.VMEM((width, hidden), BF16),
            pltpu.VMEM((hidden, width), BF16),
            pltpu.VMEM((slots, hidden), BF16),
            pltpu.VMEM((slots, hidden), BF16),
            pltpu.VMEM((slots, width), BF16),
            pltpu.VMEM((slots, width), BF16),
            pltpu.VMEM((slots, width), BF16),
            pltpu.VMEM((slots, hidden), BF16),
            pltpu.VMEM((slots, width), BF16),
            pltpu.VMEM((slots, width), BF16),
            pltpu.VMEM((tokens, 128), F32),
            pltpu.VMEM((tokens, 128), F32),
        ]
        + [pltpu.VMEM((tokens, width), BF16)] * 4
        + [
            pltpu.VMEM((512, width), F32),
            pltpu.VMEM((half, hidden), BF16),
            pltpu.VMEM((half, hidden), BF16),
            pltpu.VMEM((hidden, half), BF16),
            pltpu.VMEM((hidden, half), BF16),
            pltpu.VMEM((8, hidden + width), F32),
            pltpu.VMEM((8, hidden + width), F32),
            pltpu.VMEM((tokens, proj), BF16),
            pltpu.SemaphoreType.DMA((8,)),
            pltpu.SemaphoreType.DMA((3, 2)),
            pltpu.SemaphoreType.DMA((3, 2)),
        ]
        + row_sems(),
        compiler_params=pltpu.CompilerParams(
            collective_id=3, has_side_effects=True, vmem_limit_bytes=56 << 20
        ),
        name="block_backward",
    )(*near, whole, *weights, *kept)


def on_device(
    tokens_in,
    expert_ids,
    w_qkv,
    w_out,
    router,
    gains,
    shifts,
    w_in,
    b_in,
    w_exp_out,
    b_out,
    cotangent,
):
    tok_rows, width = tokens_in.shape
    layers = w_qkv.shape[0]
    own_rows = w_qkv.shape[1]
    out_cols = w_out.shape[1]
    experts = w_in.shape[1] * lax.axis_size("exp")
    wholes, spread = gather_weights(w_qkv, w_out, router, gains, shifts)
    expert_w = []
    for layer_idx in range(layers):
        own_in, own_out = w_in[layer_idx, 0], w_exp_out[layer_idx, 0]
        expert_w.append((own_in, other_core(own_in), own_out, other_core(own_out)))
    out_bias = 0.5 * in_order(b_out, other_core(b_out), 2).astype(F32)

    spare = -tok_rows % BLOCK
    ids = jnp.pad(expert_ids, ((0, 0), (0, spare), (0, 0)), constant_values=-1)
    state = jnp.pad(tokens_in.astype(F32), ((0, spare), (0, 0)))
    saved = []
    for layer_idx in range(layers):
        got = block_forward(
            (
                state,
                spread,
                ids[layer_idx],
                b_in[layer_idx],
                out_bias[layer_idx],
            ),
            wholes[layer_idx],
            expert_w[layer_idx],
        )
        saved.append((state,) + tuple(got))
        state = got[5]
    mixed = state[:tok_rows].astype(BF16)
    grad_state = jnp.pad(cotangent.astype(F32), ((0, spare), (0, 0)))
    attn_grads = [None] * layers
    expert_grads = [None] * layers
    for layer_idx in reversed(range(layers)):
        (
            state_in,
            after,
            h_two,
            gates,
            picked0,
            picked1,
            _,
            h_one,
            qkv,
            log_total,
            heads,
            rows_in,
            slope,
            active,
        ) = saved[layer_idx]
        grad_state, grad_att, grad_logits, sums, grad_qkv, *expert_grads[layer_idx] = (
            block_backward(
                (
                    grad_state,
                    spread,
                    ids[layer_idx],
                    gates,
                    picked0,
                    picked1,
                    after,
                    state_in,
                    qkv,
                    log_total,
                    heads,
                ),
                wholes[layer_idx],
                expert_w[layer_idx],
                (slope, active, rows_in),
            )
        )
        attn_grads[layer_idx] = (h_one, grad_att, h_two, grad_qkv, heads, grad_logits, sums)
    grads = scatter_grads(attn_grads, spread, expert_grads, own_rows)
    grad_w_qkv, grad_w_out, grad_router, grad_gains, grad_shifts = grads[:5]
    grad_b_in, grad_b_out, grad_w_in, grad_w_exp_out = grads[5:]
    return (
        mixed,
        grad_state[:tok_rows],
        grad_w_qkv,
        grad_w_out,
        grad_router,
        grad_gains,
        grad_shifts,
        grad_w_in,
        grad_b_in,
        grad_w_exp_out,
        grad_b_out,
    )


def solution(mesh):
    tokens = P(("rep", "exp"), None)
    placed = (
        tokens,
        P(None, ("rep", "exp"), None),
        P(None, ("rep", "exp"), None, "mdl"),
        P(None, "mdl", ("rep", "exp")),
        P(None, ("rep", "exp"), None),
        P(None, None, ("rep", "exp")),
        P(None, None, ("rep", "exp")),
        P(None, "exp", "rep", "mdl"),
        P(None, "exp", "mdl"),
        P(None, "exp", "mdl", "rep"),
        P(None, "exp", "rep"),
    )
    return jax.shard_map(
        on_device,
        mesh=mesh,
        in_specs=placed + (tokens,),
        out_specs=(tokens, tokens) + placed[2:],
        check_vma=False,
    )
```

```python
import jax
import jax.numpy as jnp
from jax import lax
from jax.experimental import pallas as pl
from jax.experimental.pallas import tpu as pltpu
from jax.sharding import PartitionSpec as P

HD = 64
SEQ = 197
EPSILON = 1e-06
F32 = jnp.float32
BF16 = jnp.bfloat16


def norm_rows(values, gain, shift):
    row_mean = jnp.mean(values, axis=-1, keepdims=True)
    centred = values - row_mean
    row_var = jnp.mean(centred * centred, axis=-1, keepdims=True)
    return centred * lax.rsqrt(row_var + EPSILON) * gain + shift


def dot(a, b):
    return jnp.dot(a, b, preferred_element_type=F32)


def dot_tn(a, b):
    return lax.dot_general(a, b, (((0,), (0,)), ((), ())), preferred_element_type=F32)


def dot_nt(a, b):
    return lax.dot_general(a, b, (((1,), (1,)), ((), ())), preferred_element_type=F32)


def other_core(values):
    return lax.ppermute(values, "rep", [(0, 1), (1, 0)])


def in_order(own, other, axis):
    first = lax.axis_index("rep") == 0
    return jnp.concatenate(
        [jnp.where(first, own, other), jnp.where(first, other, own)], axis=axis
    )


MESH = pl.DeviceIdType.MESH
BLOCK = 16
VMEM_SPEC = pl.BlockSpec(memory_space=pltpu.VMEM)
ANY_SPEC = pl.BlockSpec(memory_space=pl.ANY)
SMALL = 128
NEAR = 8
FAR = 4


def chip_place():
    rep = lax.axis_index("rep")
    exp = lax.axis_index("exp")
    near = (1 - rep) * (exp // 8 * 2 + exp // 4 % 2) + rep * (exp % 8)
    far = (1 - rep) * (exp % 4) + rep * (exp // 8)

    def chip_of(near_idx, far_idx):
        return (1 - rep) * (near_idx // 2 * 8 + near_idx % 2 * 4 + far_idx) + rep * (
            far_idx * 8 + near_idx
        )

    return rep, exp, near, far, chip_of


def greet(near, far, chip_of, rep):
    barrier = pltpu.get_barrier_semaphore()
    for step in range(1, NEAR):
        peer = chip_of((near + step) % NEAR, far)
        pl.semaphore_signal(barrier, inc=1, device_id={"exp": peer}, device_id_type=MESH)
    for step in range(1, FAR):
        peer = chip_of(near, (far + step) % FAR)
        pl.semaphore_signal(barrier, inc=1, device_id={"exp": peer}, device_id_type=MESH)
    pl.semaphore_signal(barrier, inc=1, device_id={"rep": 1 - rep}, device_id_type=MESH)
    return barrier


GREETED = NEAR + FAR - 1


def gather_kernel(
    w_qkv,
    w_out,
    router,
    gains,
    shifts,
    whole0,
    whole1,
    spread,
    mine,
    filled,
    vectors,
    own_sem,
    near_send,
    near_recv,
    far_send,
    far_recv,
    core_send,
    core_recv,
):
    rep, exp, near, far, chip_of = chip_place()
    wholes = (whole0, whole1)

    def near_copy(layer, step, slot):
        return pltpu.make_async_remote_copy(
            src_ref=mine.at[layer],
            dst_ref=wholes[layer].at[rep, exp],
            send_sem=near_send.at[layer, step],
            recv_sem=near_recv.at[layer, slot],
            device_id={"exp": chip_of((near + step) % NEAR, far)},
            device_id_type=MESH,
        )

    def far_copy(layer, step, source, slot_near, slot_far):
        return pltpu.make_async_remote_copy(
            src_ref=wholes[layer].at[rep, source],
            dst_ref=wholes[layer].at[rep, source],
            send_sem=far_send.at[layer, step, slot_near],
            recv_sem=far_recv.at[layer, slot_far, slot_near],
            device_id={"exp": chip_of(near, (far + step) % FAR)},
            device_id_type=MESH,
        )

    def core_copy(layer, source, part):
        return pltpu.make_async_remote_copy(
            src_ref=wholes[layer].at[part, source],
            dst_ref=wholes[layer].at[part, source],
            send_sem=core_send.at[layer, source],
            recv_sem=core_recv.at[layer, source],
            device_id={"rep": 1 - rep},
            device_id_type=MESH,
        )

    keeps = [
        pltpu.make_async_copy(mine.at[layer], wholes[layer].at[rep, exp], own_sem.at[layer])
        for layer in range(2)
    ]
    barrier = greet(near, far, chip_of, rep)
    layers, own_rows, parts, part_cols = w_qkv.shape
    qkv_cols = parts * part_cols
    cut = qkv_cols + w_out.shape[1]
    experts = router.shape[2]
    turn = (
        lax.broadcasted_iota(jnp.int32, (BLOCK, own_rows), 0)
        == lax.broadcasted_iota(jnp.int32, (BLOCK, own_rows), 1)
    )
    turn = jnp.where(turn, 1.0, 0.0).astype(BF16)
    filled[...] = jnp.zeros_like(filled)
    vectors[...] = jnp.zeros_like(vectors)
    for layer in range(layers):
        for part in range(parts):
            filled[:own_rows, part * part_cols : (part + 1) * part_cols] = w_qkv[
                layer, :, part, :
            ].astype(F32)
        filled[:, qkv_cols:cut] = dot_nt(turn, w_out[layer])
        vectors[experts : experts + 2, :] = gains[layer].astype(F32)
        vectors[experts + 2 : experts + 5, :] = shifts[layer].astype(F32)
        filled[:, cut:] = dot_nt(turn, vectors[...].astype(BF16))
        filled[:own_rows, cut : cut + experts] = router[layer].astype(F32)
        mine[layer] = filled[...].astype(BF16)
    for keep in keeps:
        keep.start()
    pl.semaphore_wait(barrier, GREETED)
    for layer in range(2):

        @pl.loop(1, NEAR)
        def _(step):
            near_copy(layer, step, near).start()

    row = lax.broadcasted_iota(jnp.int32, spread.shape, 0)
    col = lax.broadcasted_iota(jnp.int32, spread.shape, 1)
    inside = row & (BLOCK - 1)
    true_row = (row >> 4) * own_rows + inside
    spread[...] = jnp.where((inside < own_rows) & (true_row == col), 1.0, 0.0).astype(BF16)
    for keep in keeps:
        keep.wait()
    for layer in range(2):

        @pl.loop(0, NEAR)
        def _(back):
            slot = (near - back + NEAR) % NEAR
            source = chip_of(slot, far)

            @pl.when(back > 0)
            def _():
                near_copy(layer, back, slot).wait_recv()

            @pl.loop(1, FAR)
            def _(step):
                far_copy(layer, step, source, slot, far).start()

            core_copy(layer, source, rep).start()

    for layer in range(2):

        @pl.loop(0, NEAR)
        def _(back):
            slot = (near - back + NEAR) % NEAR

            @pl.loop(1, FAR)
            def _(step):
                slot_far = (far - step + FAR) % FAR
                source = chip_of(slot, slot_far)
                far_copy(layer, step, source, slot, slot_far).wait_recv()
                core_copy(layer, source, rep).start()

    for layer in range(2):

        @pl.loop(0, NEAR * FAR)
        def _(source):
            core_copy(layer, source, 1 - rep).wait_recv()
            core_copy(layer, source, rep).wait_send()

        @pl.loop(1, NEAR)
        def _(step):
            near_copy(layer, step, near).wait_send()

        @pl.loop(1, FAR)
        def _(step):
            @pl.loop(0, NEAR)
            def _(slot):
                far_copy(layer, step, chip_of(slot, far), slot, far).wait_send()


def gather_weights(w_qkv, w_out, router, gains, shifts):
    layers, own_rows, parts, part_cols = w_qkv.shape
    cols = parts * part_cols + w_out.shape[1] + SMALL
    devices = 2 * NEAR * FAR
    whole = jax.ShapeDtypeStruct((2, NEAR * FAR, BLOCK, cols), BF16)
    got = pl.pallas_call(
        gather_kernel,
        out_shape=(
            whole,
            whole,
            jax.ShapeDtypeStruct((devices * BLOCK, devices * own_rows), BF16),
        ),
        in_specs=[VMEM_SPEC] * 5,
        out_specs=(ANY_SPEC, ANY_SPEC, VMEM_SPEC),
        scratch_shapes=[
            pltpu.VMEM((layers, BLOCK, cols), BF16),
            pltpu.VMEM((BLOCK, cols), F32),
            pltpu.VMEM((SMALL, own_rows), F32),
            pltpu.SemaphoreType.DMA((2,)),
            pltpu.SemaphoreType.DMA((2, NEAR)),
            pltpu.SemaphoreType.DMA((2, NEAR)),
            pltpu.SemaphoreType.DMA((2, FAR, NEAR)),
            pltpu.SemaphoreType.DMA((2, FAR, NEAR)),
            pltpu.SemaphoreType.DMA((2, NEAR * FAR)),
            pltpu.SemaphoreType.DMA((2, NEAR * FAR)),
        ],
        compiler_params=pltpu.CompilerParams(
            collective_id=0, has_side_effects=True, vmem_limit_bytes=32 << 20
        ),
        name="gather_weights",
    )(w_qkv, w_out, router, gains, shifts)
    return [value.reshape(devices * BLOCK, cols) for value in got[:2]], got[2]


def scatter_kernel(*refs):
    per_layer = [refs[7 * layer : 7 * layer + 7] for layer in range(2)]
    spread = refs[14]
    biases = refs[15:19]
    experts = refs[19:23]
    out_qkv, out_rest, out_b_in, out_b_out, out_in, out_exp = refs[23:29]
    (
        lhs_qkv,
        lhs_proj,
        lhs_small,
        sums,
        part,
        from_core,
        from_far,
        total,
        from_near,
        stage_in,
        stage_exp,
        stage_sems,
        core_send,
        core_recv,
        far_send,
        far_recv,
        near_send,
        near_recv,
    ) = refs[29:]
    rep, exp, near, far, chip_of = chip_place()
    qkv_cols, proj_cols = per_layer[0][3].shape[1], per_layer[0][4].shape[1]
    cut = qkv_cols + proj_cols
    rows = BLOCK * 8
    chunks = NEAR * FAR // 8
    loads, stores = [], []
    for layer in range(2):
        for kind, (stage, out) in enumerate(((stage_in, out_in), (stage_exp, out_exp))):
            idx = 2 * layer + kind
            loads.append(
                pltpu.make_async_copy(experts[idx], stage.at[layer], stage_sems.at[idx])
            )
            stores.append(
                pltpu.make_async_copy(stage.at[layer], out.at[layer, 0], stage_sems.at[idx])
            )
    for load in loads:
        load.start()

    def multiply(layer, core, chunk):
        rhs_qkv, rhs_proj, rhs_small = per_layer[layer][3:6]
        at = pl.ds(pl.multiple_of((core * chunks + chunk) * rows, rows), rows)
        to = pl.ds(pl.multiple_of(chunk * rows, rows), rows)
        part[layer, core, to, :qkv_cols] = dot(lhs_qkv[at, :], rhs_qkv[...]).astype(BF16)
        part[layer, core, to, qkv_cols:cut] = dot(lhs_proj[at, :], rhs_proj[...]).astype(BF16)
        part[layer, core, to, cut:] = (
            dot(lhs_small[at, :], rhs_small[...]) + sums[at, :]
        ).astype(BF16)

    def core_copy(layer, chunk):
        to = pl.ds(pl.multiple_of(chunk * rows, rows), rows)
        return pltpu.make_async_remote_copy(
            src_ref=part.at[layer, 1 - rep, to],
            dst_ref=from_core.at[layer, to],
            send_sem=core_send.at[layer, chunk],
            recv_sem=core_recv.at[layer, chunk],
            device_id={"rep": 1 - rep},
            device_id_type=MESH,
        )

    def far_copy(layer, step, slot):
        return pltpu.make_async_remote_copy(
            src_ref=part.at[layer, rep, block(chip_of(slot, (far + step) % FAR))],
            dst_ref=from_far.at[layer, step, block(slot)],
            send_sem=far_send.at[layer, step, slot],
            recv_sem=far_recv.at[layer, step, slot],
            device_id={"exp": chip_of(near, (far + step) % FAR)},
            device_id_type=MESH,
        )

    def near_copy(layer, step):
        return pltpu.make_async_remote_copy(
            src_ref=total.at[layer, block((near + step) % NEAR)],
            dst_ref=from_near.at[layer, step],
            send_sem=near_send.at[layer, step],
            recv_sem=near_recv.at[layer, step],
            device_id={"exp": chip_of((near + step) % NEAR, far)},
            device_id_type=MESH,
        )

    barrier = greet(near, far, chip_of, rep)
    for layer in range(2):
        h_one, grad_att, h_two = per_layer[layer][:3]
        lhs_qkv[...] = dot_nt(spread[...], h_one[...]).astype(BF16)
        lhs_proj[...] = dot_nt(spread[...], grad_att[...]).astype(BF16)
        lhs_small[...] = dot_nt(spread[...], h_two[...]).astype(BF16)
        sums[...] = dot_nt(spread[...], per_layer[layer][6][...].astype(BF16))
        if layer == 0:
            pl.semaphore_wait(barrier, GREETED)

        @pl.loop(0, chunks)
        def _(chunk):
            multiply(layer, 1 - rep, chunk)
            core_copy(layer, chunk).start()

        @pl.loop(0, chunks)
        def _(chunk):
            multiply(layer, rep, chunk)

    for layer in range(2):

        @pl.loop(0, chunks)
        def _(chunk):
            to = pl.ds(pl.multiple_of(chunk * rows, rows), rows)
            core_copy(layer, chunk).wait_recv()
            part[layer, rep, to, :] = (
                part[layer, rep, to, :].astype(F32) + from_core[layer, to, :].astype(F32)
            ).astype(BF16)

        @pl.loop(1, NEAR + 1)
        def _(ahead):
            @pl.loop(1, FAR)
            def _(step):
                far_copy(layer, step, (near + ahead) % NEAR).start()

    for load in loads:
        load.wait()
    for store in stores:
        store.start()
    for layer in range(2):
        out_b_in[layer] = biases[2 * layer][...]
        out_b_out[layer] = biases[2 * layer + 1][...]

    def add_far(layer, slot):
        for step in range(1, FAR):
            far_copy(layer, step, slot).wait_recv()
        value = part[layer, rep, block(chip_of(slot, far)), :].astype(F32)
        for step in range(1, FAR):
            value = value + from_far[layer, step, block(slot), :].astype(F32)
        return value

    for layer in range(2):

        @pl.loop(1, NEAR)
        def _(step):
            slot = (near + step) % NEAR
            total[layer, block(slot), :] = add_far(layer, slot).astype(BF16)
            near_copy(layer, step).start()

    own_rows = out_qkv.shape[1]
    part_cols = qkv_cols // 3
    for layer in range(2):
        value = add_far(layer, near)
        for step in range(1, NEAR):
            near_copy(layer, step).wait_recv()
            value = value + from_near[layer, step].astype(F32)
        for idx in range(3):
            out_qkv[layer, :, idx, :] = value[:own_rows, idx * part_cols : (idx + 1) * part_cols]
        out_rest[layer] = value[:, qkv_cols:]

    for layer in range(2):

        @pl.loop(1, NEAR)
        def _(step):
            near_copy(layer, step).wait_send()

        @pl.loop(1, FAR)
        def _(step):
            @pl.loop(0, NEAR)
            def _(slot):
                far_copy(layer, step, slot).wait_send()

        @pl.loop(0, chunks)
        def _(chunk):
            core_copy(layer, chunk).wait_send()

    for store in stores:
        store.wait()


def scatter_grads(attn, spread, experts, own_rows):
    tokens = attn[0][0].shape[0]
    qkv_cols, proj_cols = attn[0][3].shape[1], attn[0][4].shape[1]
    cols = qkv_cols + proj_cols + SMALL
    half = NEAR * FAR * BLOCK
    grad_in, grad_exp, grad_b_in, grad_b_out = experts[0]
    shape = jax.ShapeDtypeStruct
    chunks = NEAR * FAR // 8
    return pl.pallas_call(
        scatter_kernel,
        out_shape=(
            shape((2, own_rows, 3, qkv_cols // 3), F32),
            shape((2, BLOCK, proj_cols + SMALL), F32),
            shape((2,) + grad_b_in.shape, F32),
            shape((2,) + grad_b_out.shape, F32),
            shape((2, 1) + grad_in.shape, F32),
            shape((2, 1) + grad_exp.shape, F32),
        ),
        in_specs=[VMEM_SPEC] * 19 + [ANY_SPEC] * 4,
        out_specs=tuple([VMEM_SPEC] * 4 + [ANY_SPEC] * 2),
        scratch_shapes=[
            pltpu.VMEM((2 * half, tokens), BF16),
            pltpu.VMEM((2 * half, tokens), BF16),
            pltpu.VMEM((2 * half, tokens), BF16),
            pltpu.VMEM((2 * half, SMALL), F32),
            pltpu.VMEM((2, 2, half, cols), BF16),
            pltpu.VMEM((2, half, cols), BF16),
            pltpu.VMEM((2, FAR, NEAR * BLOCK, cols), BF16),
            pltpu.VMEM((2, NEAR * BLOCK, cols), BF16),
            pltpu.VMEM((2, NEAR, BLOCK, cols), BF16),
            pltpu.VMEM((2,) + grad_in.shape, F32),
            pltpu.VMEM((2,) + grad_exp.shape, F32),
            pltpu.SemaphoreType.DMA((4,)),
            pltpu.SemaphoreType.DMA((2, chunks)),
            pltpu.SemaphoreType.DMA((2, chunks)),
            pltpu.SemaphoreType.DMA((2, FAR, NEAR)),
            pltpu.SemaphoreType.DMA((2, FAR, NEAR)),
            pltpu.SemaphoreType.DMA((2, NEAR)),
            pltpu.SemaphoreType.DMA((2, NEAR)),
        ],
        compiler_params=pltpu.CompilerParams(
            collective_id=1, has_side_effects=True, vmem_limit_bytes=56 << 20
        ),
        name="scatter_grads",
    )(
        *attn[0],
        *attn[1],
        spread,
        *(value for parts in experts for value in parts[2:]),
        *(value for parts in experts for value in parts[:2]),
    )


PLANES = 4
PLANE = 8


def block(source):
    return pl.ds(pl.multiple_of(source * BLOCK, BLOCK), BLOCK)


def plane_rows(plane):
    return pl.ds(pl.multiple_of(plane * (PLANE * BLOCK), PLANE * BLOCK), PLANE * BLOCK)


def plane_step(turn):
    return turn + turn // 2 - 2 * (turn // 3)


def greet_all(exp):
    barrier = pltpu.get_barrier_semaphore()

    @pl.loop(1, PLANES * PLANE)
    def _(step):
        peer = (exp + step) % (PLANES * PLANE)
        pl.semaphore_signal(barrier, inc=1, device_id={"exp": peer}, device_id_type=MESH)

    mdl = lax.axis_index("mdl")
    pl.semaphore_signal(barrier, inc=1, device_id={"mdl": 1 - mdl}, device_id_type=MESH)
    return barrier


def core_send_copy(src, dst, sems, idx):
    return pltpu.make_async_remote_copy(
        src_ref=src,
        dst_ref=dst,
        send_sem=sems.at[idx, 0],
        recv_sem=sems.at[idx, 1],
        device_id={"rep": 1 - lax.axis_index("rep")},
        device_id_type=MESH,
    )


def half_copy(src, dst, sems, idx):
    return pltpu.make_async_remote_copy(
        src_ref=src,
        dst_ref=dst,
        send_sem=sems.at[idx, 0],
        recv_sem=sems.at[idx, 1],
        device_id={"mdl": 1 - lax.axis_index("mdl")},
        device_id_type=MESH,
    )


def row_copy(src, dst, exp, send_sem, recv_sem, peer, source):
    return pltpu.make_async_remote_copy(
        src_ref=src.at[block(peer)],
        dst_ref=dst.at[block(exp)],
        send_sem=send_sem.at[peer],
        recv_sem=recv_sem.at[source],
        device_id={"exp": peer},
        device_id_type=MESH,
    )


def send_all(src, dst, exp, send_sem, recv_sem):
    @pl.loop(0, PLANES)
    def _(turn):
        plane = (exp // PLANE + plane_step(turn)) % PLANES

        @pl.loop(0, PLANE)
        def _(step):
            peer = plane * PLANE + (exp + step) % PLANE

            @pl.when(turn + step > 0)
            def _():
                row_copy(src, dst, exp, send_sem, recv_sem, peer, exp).start()

    dst[block(exp), :] = src[block(exp), :]


def each_plane(src, back_src, dst, back_dst, exp, sems, work):
    send_sem, recv_sem, back_send, back_recv = sems

    @pl.loop(0, PLANES)
    def _(turn):
        plane = (exp // PLANE - plane_step(turn) + PLANES) % PLANES

        @pl.loop(0, PLANE)
        def _(step):
            source = plane * PLANE + (exp - step + PLANE) % PLANE

            @pl.when(turn + step > 0)
            def _():
                row_copy(src, dst, exp, send_sem, recv_sem, source, source).wait_recv()

        work(plane_rows(plane))

        @pl.loop(0, PLANE)
        def _(step):
            source = plane * PLANE + (exp - step + PLANE) % PLANE

            @pl.when(turn + step > 0)
            def _():
                row_copy(back_src, back_dst, exp, back_send, back_recv, source, exp).start()

    back_dst[block(exp), :] = back_src[block(exp), :]


def wait_back(back_src, back_dst, exp, sems):
    @pl.loop(1, PLANES * PLANE)
    def _(step):
        source = (exp + step) % (PLANES * PLANE)
        row_copy(back_src, back_dst, exp, sems[2], sems[3], source, source).wait_recv()


def wait_sent(src, dst, back_src, back_dst, exp, sems):
    @pl.loop(1, PLANES * PLANE)
    def _(step):
        peer = (exp + step) % (PLANES * PLANE)
        row_copy(src, dst, exp, sems[0], sems[1], peer, peer).wait_send()
        row_copy(back_src, back_dst, exp, sems[2], sems[3], peer, peer).wait_send()


def weight_loads(own_in, other_in, own_out, other_out, w_in, w_out):
    rep = lax.axis_index("rep")
    depth = own_in.shape[0]
    pairs = []
    for src_in, src_out, core in ((own_in, own_out, rep), (other_in, other_out, 1 - rep)):
        place = pl.ds(pl.multiple_of(core * depth, 128), depth)
        pairs.append((src_in, w_in.at[place, :]))
        pairs.append((src_out, w_out.at[:, place]))
    return pairs


def lanes(values):
    rows = values[0].shape[0]
    lane = lax.broadcasted_iota(jnp.int32, (rows, 128), 1)
    total = jnp.zeros((rows, 128), F32)
    for idx, value in enumerate(values):
        total = jnp.where(lane == idx, value, total)
    return total


def row_sems():
    return [pltpu.SemaphoreType.DMA((PLANES * PLANE,))] * 4


def head_slices(head, width):
    start = head * HD
    return [slice(part * width + start, part * width + start + HD) for part in range(3)]


def masked_scores(query_rows, key_rows):
    scores = dot_nt(query_rows, key_rows) * HD ** (-0.5)
    col = lax.broadcasted_iota(jnp.int32, scores.shape, 1)
    return jnp.where(col < SEQ, scores, -1e30)


def route(ids, hot0, hot1, pick0, pick1):
    tokens, slots = pick0.shape
    lane = lax.broadcasted_iota(jnp.int32, (tokens, 128), 1)
    hots = [jnp.where(ids[:, k : k + 1] == lane, 1.0, 0.0) for k in range(2)]
    hot0[...], hot1[...] = hots[0].astype(BF16), hots[1].astype(BF16)
    row = lax.broadcasted_iota(jnp.int32, (tokens, tokens), 0)
    col = lax.broadcasted_iota(jnp.int32, (tokens, tokens), 1)
    before = jnp.where(row > col, 1.0, 0.0).astype(BF16)
    earlier = dot(before, (hots[0] + hots[1]).astype(BF16))
    place = lax.broadcasted_iota(jnp.int32, (tokens, slots), 1).astype(F32)
    for k, pick in enumerate((pick0, pick1)):
        within = jnp.sum(earlier * hots[k], axis=1, keepdims=True)
        slot = ids[:, k : k + 1].astype(F32) * BLOCK + within
        pick[...] = jnp.where(slot == place, 1.0, 0.0).astype(BF16)


def attend_forward(qkv, heads, log_total):
    width = heads.shape[1]
    totals = []
    for head in range(width // HD):
        q_at, k_at, v_at = head_slices(head, width)
        scores = masked_scores(qkv[:, q_at], qkv[:, k_at])
        top_score = jnp.max(scores, axis=-1, keepdims=True)
        raw_weight = jnp.exp(scores - top_score)
        row_total = jnp.sum(raw_weight, axis=-1, keepdims=True)
        probs_low = (raw_weight / row_total).astype(BF16)
        totals.append(top_score + jnp.log(row_total))
        heads[:, q_at] = dot(probs_low, qkv[:, v_at]).astype(BF16)
    log_total[...] = lanes(totals)


def attend_backward(grad_heads, qkv, log_total, grad_qkv):
    width = grad_heads.shape[1]
    for head in range(width // HD):
        q_at, k_at, v_at = head_slices(head, width)
        query_rows, key_rows, value_rows = qkv[:, q_at], qkv[:, k_at], qkv[:, v_at]
        grad_out = grad_heads[:, q_at]
        probs = jnp.exp(masked_scores(query_rows, key_rows) - log_total[:, head : head + 1])
        grad_probs = dot_nt(grad_out, value_rows)
        grad_scores = probs * (grad_probs - jnp.sum(grad_probs * probs, axis=-1, keepdims=True))
        grad_scores = grad_scores.astype(BF16)
        grad_qkv[:, q_at] = (dot(grad_scores, key_rows) * HD ** (-0.5)).astype(BF16)
        grad_qkv[:, k_at] = (dot_tn(grad_scores, query_rows) * HD ** (-0.5)).astype(BF16)
        grad_qkv[:, v_at] = dot_tn(probs.astype(BF16), grad_out).astype(BF16)


def block_forward_kernel(
    state,
    spread,
    ids,
    b_in,
    b_out,
    whole_in,
    own_in,
    other_in,
    own_out,
    other_out,
    after_out,
    h_out,
    gates_out,
    picked0_out,
    picked1_out,
    next_out,
    h_one_out,
    qkv_out,
    log_out,
    heads_out,
    rows_out,
    slope_out,
    active_out,
    hot0,
    hot1,
    pick0,
    pick1,
    whole,
    w_in,
    w_out,
    send,
    rows,
    slope,
    active,
    back_src,
    back,
    own_att,
    low_att,
    own_moe,
    low_moe,
    load_sems,
    out_sems,
    half_sems,
    send_sem,
    recv_sem,
    back_send,
    back_recv,
):
    exp = lax.axis_index("exp")
    sems = (send_sem, recv_sem, back_send, back_recv)
    loads = [
        pltpu.make_async_copy(src, dst, load_sems.at[idx])
        for idx, (src, dst) in enumerate(
            [(whole_in, whole)]
            + weight_loads(own_in, other_in, own_out, other_out, w_in, w_out)
        )
    ]
    for load in loads:
        load.start()
    barrier = greet_all(exp)
    qkv_cols = qkv_out.shape[1]
    cut = qkv_cols + heads_out.shape[1]
    loads[0].wait()
    small = dot_tn(whole[:, cut:], spread[...])
    first_row = PLANES * PLANE
    gain0, gain1, shift0, shift1, shift2 = [
        small[first_row + idx : first_row + idx + 1, :] for idx in range(5)
    ]
    h_one = norm_rows(state[...], gain0, shift0).astype(BF16)
    h_one_out[...] = h_one
    wide = dot_nt(h_one, spread[...]).astype(BF16)
    qkv_out[...] = dot(wide, whole[:, :qkv_cols]).astype(BF16)
    attend_forward(qkv_out, heads_out, log_out)
    route(ids, hot0, hot1, pick0, pick1)
    own_att[...] = dot(
        dot_nt(heads_out[...], whole[:, qkv_cols:cut]).astype(BF16), spread[...]
    ).astype(BF16)
    pl.semaphore_wait(barrier, PLANES * PLANE)
    first = half_copy(own_att, low_att, half_sems, 0)
    first.start()
    first.wait_recv()
    after = state[...] + (own_att[...].astype(F32) + low_att[...].astype(F32)) + shift2
    after_out[...] = after
    h_two = norm_rows(after, gain1, shift1).astype(BF16)
    h_out[...] = h_two
    send[...] = dot_tn(pick0[...] + pick1[...], h_two).astype(BF16)
    send_all(send, rows, exp, send_sem, recv_sem)
    logits = dot_nt(h_two, small.astype(BF16))
    chosen = [jnp.sum(logits * hot[...].astype(F32), axis=1, keepdims=True) for hot in (hot0, hot1)]
    top = jnp.maximum(chosen[0], chosen[1])
    raw = [jnp.exp(value - top) for value in chosen]
    gates = [value / (raw[0] + raw[1]) for value in raw]
    gates_out[...] = lanes(gates)
    bias_in = b_in[...].astype(F32)
    for load in loads[1:]:
        load.wait()
    tile = 512

    def work(at):
        for col in range(0, active.shape[1], tile):
            cols = slice(col, col + tile)
            inner = dot(rows[at, :], w_in[:, cols]) + bias_in[:, cols]
            cdf = 0.5 * (1.0 + lax.erf(inner * (0.5**0.5)))
            active[at, cols] = (inner * cdf).astype(BF16)
            slope[at, cols] = (
                cdf + inner * jnp.exp(-0.5 * inner * inner) * 0.3989422804014327
            ).astype(BF16)
        back_src[at, :] = (dot(active[at, :], w_out[...]) + b_out[...]).astype(BF16)

    each_plane(send, back_src, rows, back, exp, sems, work)
    saves = [
        pltpu.make_async_copy(src, dst, out_sems.at[idx])
        for idx, (src, dst) in enumerate(
            ((rows, rows_out), (slope, slope_out), (active, active_out))
        )
    ]
    for save in saves:
        save.start()
    wait_back(back_src, back, exp, sems)
    picked = [dot(pick[...], back[...]) for pick in (pick0, pick1)]
    own_moe[...] = (gates[0] * picked[0] + gates[1] * picked[1]).astype(BF16)
    second = half_copy(own_moe, low_moe, half_sems, 1)
    second.start()
    picked0_out[...] = picked[0].astype(BF16)
    picked1_out[...] = picked[1].astype(BF16)
    wait_sent(send, rows, back_src, back, exp, sems)
    second.wait_recv()
    next_out[...] = after_out[...] + (own_moe[...].astype(F32) + low_moe[...].astype(F32))
    first.wait_send()
    second.wait_send()
    for save in saves:
        save.wait()


def block_forward(near, whole, weights):
    tokens, width = near[0].shape
    slots = BLOCK * PLANES * PLANE
    hidden = weights[0].shape[1]
    cols = whole.shape[1]
    proj = (cols - SMALL) // 4
    shape = jax.ShapeDtypeStruct
    return pl.pallas_call(
        block_forward_kernel,
        out_shape=(
            shape((tokens, width), F32),
            shape((tokens, width), BF16),
            shape((tokens, 128), F32),
            shape((tokens, width), BF16),
            shape((tokens, width), BF16),
            shape((tokens, width), F32),
            shape((tokens, width), BF16),
            shape((tokens, 3 * proj), BF16),
            shape((tokens, 128), F32),
            shape((tokens, proj), BF16),
            shape((slots, width), BF16),
            shape((slots, hidden), BF16),
            shape((slots, hidden), BF16),
        ),
        in_specs=[VMEM_SPEC] * 5 + [ANY_SPEC] * 5,
        out_specs=tuple([VMEM_SPEC] * 10 + [ANY_SPEC] * 3),
        scratch_shapes=[
            pltpu.VMEM((tokens, 128), BF16),
            pltpu.VMEM((tokens, 128), BF16),
            pltpu.VMEM((tokens, slots), BF16),
            pltpu.VMEM((tokens, slots), BF16),
            pltpu.VMEM(whole.shape, BF16),
            pltpu.VMEM((width, hidden), BF16),
            pltpu.VMEM((hidden, width), BF16),
            pltpu.VMEM((slots, width), BF16),
            pltpu.VMEM((slots, width), BF16),
            pltpu.VMEM((slots, hidden), BF16),
            pltpu.VMEM((slots, hidden), BF16),
            pltpu.VMEM((slots, width), BF16),
            pltpu.VMEM((slots, width), BF16),
        ]
        + [pltpu.VMEM((tokens, width), BF16)] * 4
        + [
            pltpu.SemaphoreType.DMA((5,)),
            pltpu.SemaphoreType.DMA((3,)),
            pltpu.SemaphoreType.DMA((2, 2)),
        ]
        + row_sems(),
        compiler_params=pltpu.CompilerParams(
            collective_id=2, has_side_effects=True, vmem_limit_bytes=56 << 20
        ),
        name="block_forward",
    )(*near, whole, *weights)


def norm_parts(values):
    row_mean = jnp.mean(values, axis=-1, keepdims=True)
    centred = values - row_mean
    row_var = jnp.mean(centred * centred, axis=-1, keepdims=True)
    scale = lax.rsqrt(row_var + EPSILON)
    return centred * scale, scale


def norm_grad(grad, unit, scale, gain):
    scaled = grad * gain
    return scale * (
        scaled
        - jnp.mean(scaled, axis=-1, keepdims=True)
        - unit * jnp.mean(scaled * unit, axis=-1, keepdims=True)
    )


def block_backward_kernel(
    grad_state,
    spread,
    ids,
    gates,
    picked0,
    picked1,
    after,
    state_in,
    qkv,
    log_total,
    heads,
    whole_in,
    own_in,
    other_in,
    own_out,
    other_out,
    slope_in,
    active_in,
    rows_in,
    grad_out,
    grad_att_out,
    grad_logits_out,
    sums_out,
    grad_qkv_out,
    grad_in_out,
    grad_exp_out,
    grad_b_in_out,
    grad_b_out_out,
    hot0,
    hot1,
    pick0,
    pick1,
    whole,
    w_in,
    w_out,
    slope,
    active,
    kept_rows,
    send,
    rows,
    inner,
    back_src,
    back,
    own_gate,
    low_gate,
    own_h,
    low_h,
    own_one,
    low_one,
    product,
    in_away,
    in_got,
    exp_away,
    exp_got,
    bias_own,
    bias_got,
    grad_heads,
    load_sems,
    half_sems,
    core_sems,
    send_sem,
    recv_sem,
    back_send,
    back_recv,
):
    exp = lax.axis_index("exp")
    rep = lax.axis_index("rep")
    sems = (send_sem, recv_sem, back_send, back_recv)
    loads = [
        pltpu.make_async_copy(src, dst, load_sems.at[idx])
        for idx, (src, dst) in enumerate(
            weight_loads(own_in, other_in, own_out, other_out, w_in, w_out)
            + [
                (slope_in, slope),
                (whole_in, whole),
                (active_in, active),
                (rows_in, kept_rows),
            ]
        )
    ]
    for load in loads:
        load.start()
    barrier = greet_all(exp)
    pl.semaphore_signal(barrier, inc=1, device_id={"rep": 1 - rep}, device_id_type=MESH)
    grad = grad_state[...]
    gate0, gate1 = gates[:, 0:1], gates[:, 1:2]
    route(ids, hot0, hot1, pick0, pick1)
    send[...] = (
        dot_tn(pick0[...], (gate0 * grad).astype(BF16))
        + dot_tn(pick1[...], (gate1 * grad).astype(BF16))
    ).astype(BF16)
    pl.semaphore_wait(barrier, PLANES * PLANE + 1)
    send_all(send, rows, exp, send_sem, recv_sem)
    own_gate[...] = lanes(
        [
            jnp.sum(grad * picked[...].astype(F32), axis=1, keepdims=True)
            for picked in (picked0, picked1)
        ]
    )
    first = half_copy(own_gate, low_gate, half_sems, 0)
    first.start()
    for load in loads:
        load.wait()
    qkv_cols = qkv.shape[1]
    cut = qkv_cols + heads.shape[1]
    small = dot_tn(whole[:, cut:], spread[...])
    first_row = PLANES * PLANE
    gain0, gain1 = [small[first_row + idx : first_row + idx + 1, :] for idx in range(2)]

    def work(at):
        grad_active = dot_nt(rows[at, :], w_out[...])
        inner[at, :] = (grad_active * slope[at, :].astype(F32)).astype(BF16)
        back_src[at, :] = dot_nt(inner[at, :], w_in[...]).astype(BF16)

    each_plane(send, back_src, rows, back, exp, sems, work)

    half = grad_in_out.shape[0]
    hidden = inner.shape[1]
    own_at = pl.ds(pl.multiple_of(rep * half, 128), half)
    other_at = pl.ds(pl.multiple_of((1 - rep) * half, 128), half)
    in_away[...] = dot_tn(kept_rows[:, other_at], inner[...]).astype(BF16)
    in_copy = core_send_copy(in_away, in_got, core_sems, 0)
    in_copy.start()
    grad_in_out[...] = dot_tn(kept_rows[:, own_at], inner[...])

    first.wait_recv()
    total = own_gate[...] + low_gate[...]
    grad0, grad1 = total[:, 0:1], total[:, 1:2]
    mean = gate0 * grad0 + gate1 * grad1
    grad_logits = (
        gate0 * (grad0 - mean) * hot0[...].astype(F32)
        + gate1 * (grad1 - mean) * hot1[...].astype(F32)
    ).astype(BF16)
    grad_logits_out[...] = grad_logits
    from_router = dot(grad_logits, small.astype(BF16))
    unit, scale = norm_parts(after[...])
    wait_back(back_src, back, exp, sems)
    own_h[...] = dot(pick0[...] + pick1[...], back[...]).astype(BF16)
    second = half_copy(own_h, low_h, half_sems, 1)
    second.start()
    tall = product.shape[0]
    for start in range(0, hidden, tall):
        part = slice(start, start + tall)
        product[...] = dot_tn(active[:, part], rows[...])
        grad_exp_out[part, :] = product[:, own_at]
        exp_away[part, :] = product[:, other_at].astype(BF16)
    exp_copy = core_send_copy(exp_away, exp_got, core_sems, 1)
    exp_copy.start()
    bias_own[...] = jnp.zeros_like(bias_own)
    bias_own[0:1, :hidden] = jnp.sum(inner[...].astype(F32), axis=0, keepdims=True)
    bias_own[0:1, hidden:] = jnp.sum(rows[...].astype(F32), axis=0, keepdims=True)
    bias_copy = core_send_copy(bias_own, bias_got, core_sems, 2)
    bias_copy.start()
    wait_sent(send, rows, back_src, back, exp, sems)
    second.wait_recv()
    grad_h = own_h[...].astype(F32) + low_h[...].astype(F32) + from_router
    grad_after = norm_grad(grad_h, unit, scale, gain1) + grad_state[...]
    grad_att = grad_after.astype(BF16)
    grad_att_out[...] = grad_att
    sums_out[...] = jnp.zeros_like(sums_out)
    put = lambda idx, value: sums_out.__setitem__(
        (slice(first_row + idx, first_row + idx + 1), slice(None)),
        jnp.sum(value, axis=0, keepdims=True),
    )
    put(1, grad_h * unit)
    put(3, grad_h)
    put(4, grad_after)
    wide = dot_nt(grad_att, spread[...]).astype(BF16)
    grad_heads[...] = dot(wide, whole[:, qkv_cols:cut]).astype(BF16)
    attend_backward(grad_heads, qkv, log_total, grad_qkv_out)
    own_one[...] = dot(
        dot_nt(grad_qkv_out[...], whole[:, :qkv_cols]).astype(BF16), spread[...]
    ).astype(BF16)
    third = half_copy(own_one, low_one, half_sems, 2)
    third.start()
    in_copy.wait_recv()
    grad_in_out[...] += in_got[...].astype(F32)
    exp_copy.wait_recv()
    grad_exp_out[...] += exp_got[...].astype(F32)
    bias_copy.wait()
    bias_own[...] += bias_got[...]
    grad_b_in_out[...] = bias_own[0:1, :hidden]
    grad_b_out_out[...] = bias_own[
        0:1, pl.ds(pl.multiple_of(hidden + rep * half, 128), half)
    ]
    unit, scale = norm_parts(state_in[...])
    third.wait_recv()
    grad_one = own_one[...].astype(F32) + low_one[...].astype(F32)
    grad_out[...] = grad_after + norm_grad(grad_one, unit, scale, gain0)
    put(0, grad_one * unit)
    put(2, grad_one)
    for copy in (first, second, third, in_copy, exp_copy):
        copy.wait_send()


def block_backward(near, whole, weights, kept):
    tokens, width = near[0].shape
    slots = BLOCK * PLANES * PLANE
    hidden = weights[0].shape[1]
    cols = whole.shape[1]
    proj = (cols - SMALL) // 4
    half = width // 2
    shape = jax.ShapeDtypeStruct
    return pl.pallas_call(
        block_backward_kernel,
        out_shape=(
            shape((tokens, width), F32),
            shape((tokens, width), BF16),
            shape((tokens, 128), BF16),
            shape((128, width), F32),
            shape((tokens, 3 * proj), BF16),
            shape((half, hidden), F32),
            shape((hidden, half), F32),
            shape((1, hidden), F32),
            shape((1, half), F32),
        ),
        in_specs=[VMEM_SPEC] * 11 + [ANY_SPEC] * 8,
        out_specs=tuple([VMEM_SPEC] * 9),
        scratch_shapes=[
            pltpu.VMEM((tokens, 128), BF16),
            pltpu.VMEM((tokens, 128), BF16),
            pltpu.VMEM((tokens, slots), BF16),
            pltpu.VMEM((tokens, slots), BF16),
            pltpu.VMEM(whole.shape, BF16),
            pltpu.VMEM((width, hidden), BF16),
            pltpu.VMEM((hidden, width), BF16),
            pltpu.VMEM((slots, hidden), BF16),
            pltpu.VMEM((slots, hidden), BF16),
            pltpu.VMEM((slots, width), BF16),
            pltpu.VMEM((slots, width), BF16),
            pltpu.VMEM((slots, width), BF16),
            pltpu.VMEM((slots, hidden), BF16),
            pltpu.VMEM((slots, width), BF16),
            pltpu.VMEM((slots, width), BF16),
            pltpu.VMEM((tokens, 128), F32),
            pltpu.VMEM((tokens, 128), F32),
        ]
        + [pltpu.VMEM((tokens, width), BF16)] * 4
        + [
            pltpu.VMEM((512, width), F32),
            pltpu.VMEM((half, hidden), BF16),
            pltpu.VMEM((half, hidden), BF16),
            pltpu.VMEM((hidden, half), BF16),
            pltpu.VMEM((hidden, half), BF16),
            pltpu.VMEM((8, hidden + width), F32),
            pltpu.VMEM((8, hidden + width), F32),
            pltpu.VMEM((tokens, proj), BF16),
            pltpu.SemaphoreType.DMA((8,)),
            pltpu.SemaphoreType.DMA((3, 2)),
            pltpu.SemaphoreType.DMA((3, 2)),
        ]
        + row_sems(),
        compiler_params=pltpu.CompilerParams(
            collective_id=3, has_side_effects=True, vmem_limit_bytes=56 << 20
        ),
        name="block_backward",
    )(*near, whole, *weights, *kept)


def on_device(
    tokens_in,
    expert_ids,
    w_qkv,
    w_out,
    router,
    gains,
    shifts,
    w_in,
    b_in,
    w_exp_out,
    b_out,
    cotangent,
):
    tok_rows, width = tokens_in.shape
    layers = w_qkv.shape[0]
    own_rows = w_qkv.shape[1]
    out_cols = w_out.shape[1]
    experts = w_in.shape[1] * lax.axis_size("exp")
    wholes, spread = gather_weights(w_qkv, w_out, router, gains, shifts)
    expert_w = []
    for layer_idx in range(layers):
        own_in, own_out = w_in[layer_idx, 0], w_exp_out[layer_idx, 0]
        expert_w.append((own_in, other_core(own_in), own_out, other_core(own_out)))
    out_bias = 0.5 * in_order(b_out, other_core(b_out), 2).astype(F32)

    spare = -tok_rows % BLOCK
    ids = jnp.pad(expert_ids, ((0, 0), (0, spare), (0, 0)), constant_values=-1)
    state = jnp.pad(tokens_in.astype(F32), ((0, spare), (0, 0)))
    saved = []
    for layer_idx in range(layers):
        got = block_forward(
            (
                state,
                spread,
                ids[layer_idx],
                b_in[layer_idx],
                out_bias[layer_idx],
            ),
            wholes[layer_idx],
            expert_w[layer_idx],
        )
        saved.append((state,) + tuple(got))
        state = got[5]
    mixed = state[:tok_rows].astype(BF16)
    grad_state = jnp.pad(cotangent.astype(F32), ((0, spare), (0, 0)))
    attn_grads = [None] * layers
    expert_grads = [None] * layers
    for layer_idx in reversed(range(layers)):
        (
            state_in,
            after,
            h_two,
            gates,
            picked0,
            picked1,
            _,
            h_one,
            qkv,
            log_total,
            heads,
            rows_in,
            slope,
            active,
        ) = saved[layer_idx]
        grad_state, grad_att, grad_logits, sums, grad_qkv, *expert_grads[layer_idx] = (
            block_backward(
                (
                    grad_state,
                    spread,
                    ids[layer_idx],
                    gates,
                    picked0,
                    picked1,
                    after,
                    state_in,
                    qkv,
                    log_total,
                    heads,
                ),
                wholes[layer_idx],
                expert_w[layer_idx],
                (slope, active, rows_in),
            )
        )
        attn_grads[layer_idx] = (h_one, grad_att, h_two, grad_qkv, heads, grad_logits, sums)
    grad_w_qkv, rest, grad_b_in, grad_b_out, grad_w_in, grad_w_exp_out = scatter_grads(
        attn_grads, spread, expert_grads, own_rows
    )
    rest = rest[:, :own_rows]
    small = rest[:, :, out_cols:]
    return (
        mixed,
        grad_state[:tok_rows],
        grad_w_qkv,
        jnp.swapaxes(rest[:, :, :out_cols], 1, 2),
        small[:, :, :experts],
        jnp.swapaxes(small[:, :, experts : experts + 2], 1, 2),
        jnp.swapaxes(small[:, :, experts + 2 : experts + 5], 1, 2),
        grad_w_in,
        grad_b_in,
        grad_w_exp_out,
        grad_b_out,
    )


def solution(mesh):
    tokens = P(("rep", "exp"), None)
    placed = (
        tokens,
        P(None, ("rep", "exp"), None),
        P(None, ("rep", "exp"), None, "mdl"),
        P(None, "mdl", ("rep", "exp")),
        P(None, ("rep", "exp"), None),
        P(None, None, ("rep", "exp")),
        P(None, None, ("rep", "exp")),
        P(None, "exp", "rep", "mdl"),
        P(None, "exp", "mdl"),
        P(None, "exp", "mdl", "rep"),
        P(None, "exp", "rep"),
    )
    return jax.shard_map(
        on_device,
        mesh=mesh,
        in_specs=placed + (tokens,),
        out_specs=(tokens, tokens) + placed[2:],
        check_vma=False,
    )
```
